32 devices in a mesh: pipe: 2 (over core), dp: 16 (over z, y, x).
Axes of the slice: x: 2, y: 2, z: 4, core: 2. Of those that a mesh axis runs over, the one named last changes fastest.
Arguments:
- hidden_in: bfloat16 [2, 16, 256, 1024], P(None, 'dp'), may hold values from -6 to 6
- lengths: int32 [2, 16], P(None, 'dp'), may hold values from 200 to 256, as said below
- out_grad: bfloat16 [2, 16, 256, 1024], P(None, 'dp'), may hold values from -6 to 6
- w_qkv: bfloat16 [2, 1024, 3072], P('pipe', 'dp'), may hold values from -0.1875 to 0.1875
- w_out: bfloat16 [2, 1024, 1024], P('pipe', 'dp'), may hold values from -1.5 to 1.5
- w_up: bfloat16 [2, 1024, 4096], P('pipe', 'dp'), may hold values from -0.1875 to 0.1875
- w_down: bfloat16 [2, 4096, 1024], P('pipe', 'dp'), may hold values from -0.09375 to 0.09375
- vectors: bfloat16 [2, 10, 1024], P('pipe', None, 'dp'), may hold values from -0.41 to 1.41
- up_bias: bfloat16 [2, 4096], P('pipe', 'dp'), may hold values from -3 to 3
Outputs:
- edges: float32 [2, 2, 16, 256, 1024], P('pipe', None, 'dp')
- grad_qkv: float32 [2, 1024, 3072], P('pipe', 'dp')
- grad_out: float32 [2, 1024, 1024], P('pipe', 'dp')
- grad_up: float32 [2, 1024, 4096], P('pipe', 'dp')
- grad_down: float32 [2, 4096, 1024], P('pipe', 'dp')
- grad_vectors: float32 [2, 10, 1024], P('pipe', None, 'dp')
- grad_up_bias: float32 [2, 4096], P('pipe', 'dp')
The draws below stay inside these ranges and needn't reach their ends.
Inputs may be any that keep to these rules, and one draw needn't show every extreme that they name: `lengths`: in each micro-batch one utterance has exactly 256 units.
All inputs are finite; a program needn't handle non-finite values.
Results may differ from the reference program's by a relative error of at most 0.011.
Values may be sent and summed in bfloat16 or wider, within the bound.
A program may use at most 448 MiB of HBM per device.

```python
import jax
import jax.numpy as jnp
from jax import lax

D = 1024
HEADS = 16
HEAD_DIM = 64
FF = 4096
SEQ = 256
MIN_LEN = 200
MICRO = 2
SEQS = 16


def draw_lengths(key, part):
    key = jax.random.fold_in(key, 11)
    first_key, second_key = jax.random.split(key)
    drawn = jax.random.randint(first_key, (MICRO, SEQS), MIN_LEN, SEQ + 1)
    full_at = jax.random.randint(second_key, (MICRO, 1), 0, SEQS)
    columns = jnp.arange(SEQS)[None, :]
    return jnp.where(columns == full_at, SEQ, drawn).astype(jnp.int32)


def draw_vectors(key, part):
    key = jax.random.fold_in(key, 23)
    spread = jax.random.uniform(key, (2, 10, D), jnp.float32, -1.0, 1.0)
    row_ids = jnp.arange(10)[None, :, None]
    gain_rows = (row_ids == 0) | (row_ids == 5) | (row_ids == 8)
    return jnp.where(gain_rows, 1.0 + 0.4 * spread, 0.4 * spread).astype(jnp.bfloat16)


def levels(rng, extent, pieces, least, largest):
    level = 1.0
    for dim, blocks in pieces:
        draws = jax.random.uniform(jax.random.fold_in(jax.random.fold_in(rng, 6), dim), (blocks,), jnp.float32, least / len(pieces), largest / len(pieces))
        level = level * jnp.repeat(jnp.exp(draws), extent[dim] // blocks).reshape((-1,) + (1,) * (len(extent) - 1 - dim))
    return level


def bell_draw(own_key, dims, scale, limit, shards=(), kind=jnp.bfloat16):
    values = jax.random.normal(own_key, dims, jnp.float32) * scale
    if len(shards) > 0:
        values = levels(own_key, dims, shards, -0.22, 0.18) * values
    return jnp.clip(values, min=-limit, max=limit).astype(kind)


def setup_inputs(seed: int = 0) -> dict:
    key_of = jax.random.split(jax.random.key(seed), 10)
    return {
        "hidden_in": bell_draw(key_of[0], (MICRO, SEQS, SEQ, D), 1.0, 6.0, ((1, 16),)),
        "lengths": draw_lengths(jax.random.fold_in(key_of[9], 71), 0),
        "out_grad": bell_draw(key_of[2], (MICRO, SEQS, SEQ, D), 1.0, 6.0, ((1, 16),)),
        "w_qkv": bell_draw(key_of[3], (2, D, 3 * D), D ** -0.5, 0.1875, ((0, 2), (1, 16))),
        "w_out": bell_draw(key_of[4], (2, D, D), (max(D // 64, 16)) ** -0.5, 1.5, ((0, 2), (1, 16))),
        "w_up": bell_draw(key_of[5], (2, D, FF), D ** -0.5, 0.1875, ((0, 2), (1, 16))),
        "w_down": bell_draw(key_of[6], (2, FF, D), FF ** -0.5, 0.09375, ((0, 2), (1, 16))),
        "vectors": draw_vectors(jax.random.fold_in(key_of[9], 71), 0),
        "up_bias": bell_draw(key_of[8], (2, FF), 0.5, 3.0, ((0, 2), (1, 16))),
    }


@jax.custom_vjp
def low(v):
    return lax.optimization_barrier(v.astype(jnp.bfloat16)).astype(jnp.float32)

@jax.custom_vjp
def low_back(v):
    return v

def low_keep(v):
    return (low(v), None)

def low_pass(kept, grad):
    return (grad,)

def back_keep(v):
    return (v, None)

def back_low(kept, grad):
    return (low(grad),)
low.defvjp(low_keep, low_pass)
low_back.defvjp(back_keep, back_low)
EPS = 1e-05
HIGH = lax.Precision.HIGHEST

def layer_norm(values, gain, shift):
    center = values - lax.optimization_barrier(jnp.mean(values, -1, keepdims=True))
    factor = lax.rsqrt(lax.optimization_barrier(jnp.mean(center * center, -1, keepdims=True)) + EPS)
    return center * factor * gain + shift

def matmul(left, right):
    return jnp.dot(left, right, precision=HIGH)

def block(inputs, valid_rows, allowed, weights, is_last):
    w_qkv, w_out, w_up, w_down, vec_rows, up_bias = weights
    row_count = inputs.shape[0]
    attn_in = low(layer_norm(inputs, vec_rows[0], vec_rows[1]))
    projected = matmul(attn_in, w_qkv)
    query = low_back(low(projected[:, :D] + vec_rows[2])).reshape(row_count, HEADS, HEAD_DIM)
    key_heads = low_back(low(projected[:, D:2 * D])).reshape(row_count, HEADS, HEAD_DIM)
    value_heads = low_back(low(projected[:, 2 * D:] + vec_rows[3])).reshape(row_count, HEADS, HEAD_DIM)
    scores = low_back(jnp.einsum('qhd,khd->hqk', query, key_heads, precision=HIGH) * HEAD_DIM ** (-0.5))
    scores = jnp.where(allowed[None], scores, -1e+30)
    attn_probs = low(jax.nn.softmax(scores, axis=-1))
    attended = jnp.einsum('hqk,khd->qhd', attn_probs, value_heads, precision=HIGH).reshape(row_count, D)
    attended = low_back(low(attended))
    hidden = inputs + low_back(matmul(attended, w_out) + vec_rows[4])
    ffn_in = low(layer_norm(hidden, vec_rows[5], vec_rows[6]))
    up_value = low_back(matmul(ffn_in, w_up) + up_bias)
    activated = low(jax.nn.gelu(up_value, approximate=False))
    summed = hidden + low_back(matmul(activated, w_down) + vec_rows[7])
    if is_last:
        summed = layer_norm(summed, vec_rows[8], vec_rows[9])
    return summed * valid_rows

def reference(hidden_in, lengths, out_grad, w_qkv, w_out, w_up, w_down, vectors, up_bias):
    weights = tuple((w.astype(jnp.float32) for w in (w_qkv, w_out, w_up, w_down, vectors, up_bias)))
    positions = jnp.arange(SEQ, dtype=jnp.int32)

    def one_utterance(carry, item):
        states, length, cotangent = item
        valid_rows = (positions < length).astype(jnp.float32)[:, None]
        allowed = (positions[None, :] <= positions[:, None]) & (positions[None, :] < length)

        def chain(first_in, params):
            first_layer = tuple((w[0] for w in params))
            second_layer = tuple((w[1] for w in params))
            first_out = block(first_in, valid_rows, allowed, first_layer, False)
            second_in = low_back(low(first_out))
            return block(second_in, valid_rows, allowed, second_layer, True)
        result, pull = jax.vjp(chain, states.astype(jnp.float32), weights)
        grad_in, grad_params = pull(cotangent.astype(jnp.float32))
        carry = tuple((total + term for total, term in zip(carry, grad_params)))
        return (carry, (grad_in, result))
    start = tuple((jnp.zeros(w.shape, jnp.float32) for w in weights))
    items = (hidden_in.reshape(MICRO * SEQS, SEQ, D), lengths.reshape(MICRO * SEQS).astype(jnp.int32), out_grad.reshape(MICRO * SEQS, SEQ, D))
    grads, (grad_in, result) = lax.scan(one_utterance, start, items)
    edges = jnp.stack([grad_in.reshape(MICRO, SEQS, SEQ, D), result.reshape(MICRO, SEQS, SEQ, D)])
    return (edges, grads[0], grads[1], grads[2], grads[3], grads[4], grads[5])
```

```python
import functools

import jax
import jax.numpy as jnp
from jax import lax
from jax.experimental import pallas as pl
from jax.experimental.pallas import tpu as pltpu
from jax.sharding import PartitionSpec as P

D = 1024
HEADS = 16
HEAD_DIM = 64
FF = 4096
SEQ = 256
EPS = 1e-05
MESH = pl.DeviceIdType.MESH
UNIT = 1024
HALF = UNIT // 2
UNITS = [(0, 0), (0, 1), (0, 2), (1, 0), (2, 0), (2, 1), (2, 2), (2, 3), (3, 0), (3, 1), (3, 2), (3, 3)]
BACK = [(3, 0), (2, 0), (3, 1), (2, 1), (3, 2), (2, 2), (3, 3), (2, 3), (1, 0), (0, 0), (0, 1), (0, 2)]
NU = len(UNITS)


def axis_orders(dims):
    if dims == 4:
        first, second = (3, 0, 1, 2), (2, 0, 1, 3)
        return [first, second, (0, 1, 3, 2), first, second, (0, 1, 2, 3)]
    turned = [tuple((i + 2 * turn) % dims for i in range(dims)) for turn in range(3)]
    return turned + turned


def place(dims):
    core, here = lax.axis_index("pipe"), lax.axis_index("dp")
    bits = [lax.rem(lax.div(here, 2 ** (dims - 1 - i)), 2) for i in range(dims)]
    partners = [(core, here + (1 - 2 * bits[i]) * 2 ** (dims - 1 - i)) for i in range(dims)]
    return core, bits, partners


def greet(core, here, partners):
    barrier = pltpu.get_barrier_semaphore()
    everyone = [(1 - core, here)] + partners
    for device in everyone:
        pl.semaphore_signal(barrier, inc=1, device_id=device, device_id_type=MESH)
    pl.semaphore_wait(barrier, len(everyone))


def part(ref, lead, where, matrix, block, column_half):
    if matrix == 3:
        columns = pl.ds(pl.multiple_of(column_half * HALF, HALF), HALF)
        return ref.at[lead + where + (block, slice(None), columns)]
    columns = pl.ds(pl.multiple_of(block * UNIT + column_half * HALF, HALF), HALF)
    return ref.at[lead + where + (slice(None), columns)]


def gather_kernel(dims, *refs):
    shards, small = refs[:4], refs[4]
    whole, small_all = refs[5:9], refs[9]
    local_sem, first_send, first_recv, send_sem, recv_sem, pass_send, pass_recv, small_send, small_recv = refs[10:]
    core, bits, partners = place(dims)
    here = lax.axis_index("dp")
    other = (1 - core, here)
    greet(core, here, partners)
    orders = axis_orders(dims)
    own = tuple(bits)
    total = 2 * NU

    def remote(source, target, send, recv, device):
        return pltpu.make_async_remote_copy(
            src_ref=source, dst_ref=target, send_sem=send, recv_sem=recv, device_id=device, device_id_type=MESH
        )

    def first_local(u, layer):
        matrix, block = UNITS[u]
        return pltpu.make_async_copy(
            part(shards[matrix], (), (), matrix, block, core),
            part(whole[matrix], (layer,), own, matrix, block, core),
            local_sem.at[u],
        )

    def first_remote(u, layer):
        matrix, block = UNITS[u]
        return remote(
            part(shards[matrix], (), (), matrix, block, 1 - core),
            part(whole[matrix], (layer,), own, matrix, block, 1 - core),
            first_send.at[u],
            first_recv.at[u],
            other,
        )

    def step(v, k):
        layer, u = v // NU, v % NU
        matrix, block = UNITS[u]
        order = orders[v % len(orders)]
        where = tuple(slice(None) if i in order[:k] else bits[i] for i in range(dims))
        ref = part(whole[matrix], (layer,), where, matrix, block, core)
        return remote(ref, ref, send_sem.at[v, k], recv_sem.at[v, k], partners[order[k]])

    def passing(v):
        layer, u = v // NU, v % NU
        matrix, block = UNITS[u]
        ref = part(whole[matrix], (layer,), (slice(None),) * dims, matrix, block, core)
        return remote(ref, ref, pass_send.at[v], pass_recv.at[v], other)

    small_own = pltpu.make_async_copy(small, small_all.at[(core,) + own], small_send.at[dims + 1])
    small_own.start()
    for layer in range(2):

        @pl.when(core == layer)
        def _():
            for u in range(NU):
                first_remote(u, layer).start()
                first_local(u, layer).start()

    small_own.wait()
    for k in range(dims):
        where = tuple(slice(None) if i < k else bits[i] for i in range(dims))
        ref = small_all.at[(core,) + where]
        copy = remote(ref, ref, small_send.at[k], small_recv.at[k], partners[k])
        copy.start()
        copy.wait()
    copy = remote(small_all.at[core], small_all.at[core], small_send.at[dims], small_recv.at[dims], other)
    copy.start()
    copy.wait()

    def arrive(v):
        layer, u = v // NU, v % NU

        @pl.when(core == layer)
        def _():
            first_local(u, layer).wait()
            first_remote(u, layer).wait_send()

        @pl.when(core != layer)
        def _():
            first_remote(u, layer).wait_recv()

    for tick in range(total + dims + 2):
        for k in range(dims + 1, -1, -1):
            v = tick - k
            if not 0 <= v < total:
                continue
            if k == 0:
                arrive(v)
            if 0 < k <= dims:
                step(v, k - 1).wait()
            if k < dims:
                step(v, k).start()
            if k == dims:
                passing(v).start()
            if k == dims + 1:
                passing(v).wait()


def gather(shards, small, dims):
    rows = small.shape[0]
    lead = (2,) + (2,) * dims
    shapes = [lead + s.shape for s in shards[:3]]
    shapes.append(lead + (4, shards[3].shape[0] // 4, D))
    shards = list(shards[:3]) + [shards[3].reshape(4, shards[3].shape[0] // 4, D)]
    outs = [jax.ShapeDtypeStruct(s, jnp.bfloat16) for s in shapes]
    outs.append(jax.ShapeDtypeStruct(lead + (rows, 128), small.dtype))
    dma = pltpu.SemaphoreType.DMA
    return pl.pallas_call(
        functools.partial(gather_kernel, dims),
        out_shape=outs,
        in_specs=[pl.BlockSpec(memory_space=pl.ANY)] * 5,
        out_specs=[pl.BlockSpec(memory_space=pl.ANY)] * 5,
        scratch_shapes=[
            dma((NU,)),
            dma((NU,)),
            dma((NU,)),
            dma((2 * NU, dims)),
            dma((2 * NU, dims)),
            dma((2 * NU,)),
            dma((2 * NU,)),
            dma((dims + 2,)),
            dma((dims + 1,)),
        ],
        compiler_params=pltpu.CompilerParams(collective_id=1, has_side_effects=True, vmem_limit_bytes=56 << 20),
        name="gather",
    )(*shards, small)


SLOTS = 6


def scatter_kernel(dims, *refs):
    grads, small = refs[:4], refs[4]
    outs, small_out = refs[5:9], refs[9]
    held, boxes, result, small_held, small_box = refs[10], refs[11 : 12 + dims], refs[12 + dims], refs[13 + dims], refs[14 + dims]
    load_sem, send_sem, recv_sem, credit, out_sem, end_send, end_recv, small_send, small_recv = refs[15 + dims :]
    core, bits, partners = place(dims)
    here = lax.axis_index("dp")
    other = (1 - core, here)
    greet(core, here, partners)
    orders = [tuple(reversed(o)) for o in axis_orders(dims)]
    total = 2 * NU
    rows = held.shape[-2]

    def remote(source, target, send, recv, device):
        return pltpu.make_async_remote_copy(
            src_ref=source, dst_ref=target, send_sem=send, recv_sem=recv, device_id=device, device_id_type=MESH
        )

    def unit(v):
        return 1 - v // NU, BACK[v % NU]

    def device_of(v, k):
        return other if k == 0 else partners[orders[v % SLOTS][k - 1]]

    def kept(v, k, sent):
        order = orders[v % SLOTS]
        where = []
        for i in range(dims):
            if i in order[: max(k - 1, 0)]:
                where.append(bits[i])
            elif k > 0 and i == order[k - 1]:
                where.append(1 - bits[i] if sent else bits[i])
            else:
                where.append(slice(None))
        return tuple(where)

    def load(v):
        layer, (matrix, block) = unit(v)
        source = part(grads[matrix], (layer,), (slice(None),) * dims, matrix, block, core)
        return pltpu.make_async_copy(source, held.at[v % SLOTS], load_sem.at[v % SLOTS])

    def step(v, k):
        slot = v % SLOTS
        if k == 0:
            layer, (matrix, block) = unit(v)
            source = part(grads[matrix], (layer,), (slice(None),) * dims, matrix, block, 1 - core)
        else:
            source = held.at[(slot,) + kept(v, k, True)]
        return remote(source, boxes[k].at[slot], send_sem.at[slot, k], recv_sem.at[slot, k], device_of(v, k))

    def start(v, k):
        if v >= SLOTS:
            pl.semaphore_wait(credit.at[v % SLOTS, k], 1)
        step(v, k).start()

    def add(v, k):
        slot = v % SLOTS
        where = kept(v, k, False)
        box = boxes[k].at[slot]
        view = held.at[(slot,) + where]
        if k < dims:
            view[...] = view[...] + box[...]
        else:
            total_sum = view[...].astype(jnp.float32) + box[...].astype(jnp.float32)
            result[slot] = total_sum
        if v + SLOTS < total:
            pl.semaphore_signal(credit.at[slot, k], inc=1, device_id=device_of(v, k), device_id_type=MESH)

    def final_place(v):
        layer, (matrix, block) = unit(v)
        return part(outs[matrix], (), (), matrix, block, core)

    def final_local(v):
        return pltpu.make_async_copy(result.at[v % SLOTS], final_place(v), out_sem.at[v % SLOTS])

    def final_remote(v):
        return remote(result.at[v % SLOTS], final_place(v), end_send.at[v % SLOTS], end_recv.at[v % NU], other)

    def finish(v, act):
        layer = unit(v)[0]
        if act == "start":

            @pl.when(core == layer)
            def _():
                final_local(v).start()

            @pl.when(core != layer)
            def _():
                final_remote(v).start()

        else:

            @pl.when(core == layer)
            def _():
                final_local(v).wait()

            @pl.when(core != layer)
            def _():
                final_remote(v).wait_send()

    small_first = remote(small.at[1 - core], small_box.at[0], small_send.at[0], small_recv.at[0], other)
    small_first.start()
    small_load = pltpu.make_async_copy(small.at[core], small_held, small_send.at[dims + 1])
    small_load.start()
    small_load.wait()
    small_first.wait()
    small_held[...] = small_held[...] + small_box[0]
    for k in range(1, dims + 1):
        i = k - 1
        lead = tuple(bits[:i])
        source = small_held.at[lead + (1 - bits[i],)]
        target = small_box.at[(k,) + lead + (bits[i],)]
        copy = remote(
            source, small_box.at[(k,) + lead + (1 - bits[i],)], small_send.at[k], small_recv.at[k], partners[i]
        )
        copy.start()
        copy.wait()
        mine = small_held.at[lead + (bits[i],)]
        mine[...] = mine[...] + target[...]
    out_copy = pltpu.make_async_copy(small_held.at[tuple(bits)], small_out, small_send.at[dims + 1])
    out_copy.start()
    out_copy.wait()

    for tick in range(total + dims + 2):
        for k in range(dims + 1, -1, -1):
            v = tick - k
            if not 0 <= v < total:
                continue
            if k == 0:
                if v >= SLOTS:
                    finish(v - SLOTS, "wait")
                load(v).start()
                start(v, 0)
            else:
                step(v, k - 1).wait()
                if k == 1:
                    load(v).wait()
                add(v, k - 1)
                if k <= dims:
                    start(v, k)
                else:
                    finish(v, "start")
    for v in range(total - SLOTS, total):
        finish(v, "wait")
    for layer in range(2):

        @pl.when(core == layer)
        def _():
            for v in range((1 - layer) * NU, (2 - layer) * NU):
                final_remote(v).wait_recv()


def scatter(grads, small, dims):
    rows = grads[1].shape[-2]
    shapes = [(rows, 3 * D), (rows, D), (rows, FF), (4, rows, D)]
    outs = [jax.ShapeDtypeStruct(s, jnp.float32) for s in shapes]
    outs.append(jax.ShapeDtypeStruct(small.shape[-2:], jnp.float32))
    dma = pltpu.SemaphoreType.DMA
    boxes = [pltpu.VMEM((SLOTS,) + (2,) * (dims - k) + (rows, HALF), jnp.bfloat16) for k in range(dims + 1)]
    return pl.pallas_call(
        functools.partial(scatter_kernel, dims),
        out_shape=outs,
        in_specs=[pl.BlockSpec(memory_space=pl.ANY)] * 5,
        out_specs=[pl.BlockSpec(memory_space=pl.ANY)] * 5,
        scratch_shapes=[pltpu.VMEM((SLOTS,) + (2,) * dims + (rows, HALF), jnp.bfloat16)]
        + boxes
        + [
            pltpu.VMEM((SLOTS, rows, HALF), jnp.float32),
            pltpu.VMEM(small.shape[1:], jnp.float32),
            pltpu.VMEM((dims + 1,) + small.shape[1:], jnp.float32),
            dma((SLOTS,)),
            dma((SLOTS, dims + 1)),
            dma((SLOTS, dims + 1)),
            pltpu.SemaphoreType.REGULAR((SLOTS, dims + 1)),
            dma((SLOTS,)),
            dma((SLOTS,)),
            dma((NU,)),
            dma((dims + 2,)),
            dma((dims + 1,)),
        ],
        compiler_params=pltpu.CompilerParams(collective_id=2, has_side_effects=True, vmem_limit_bytes=56 << 20),
        name="scatter",
    )(*grads, small)


def norm_parts(values):
    center = values - jnp.mean(values, -1, keepdims=True)
    factor = lax.rsqrt(jnp.mean(center * center, -1, keepdims=True) + EPS)
    return (center * factor, factor)


def norm_back(grad_normed, normed, factor):
    return factor * (
        grad_normed
        - jnp.mean(grad_normed, -1, keepdims=True)
        - normed * jnp.mean(grad_normed * normed, -1, keepdims=True)
    )


def gelu_exact(values):
    return jax.nn.gelu(values, approximate=False)


def forward(inputs, length, weights, is_last):
    w_qkv, w_out, w_up, w_down, vec_rows, up_bias = weights
    row_count = inputs.shape[0]
    positions = jnp.arange(row_count, dtype=jnp.int32)
    valid_rows = (positions < length).astype(jnp.float32)[:, None]
    allowed = (positions[None, :] <= positions[:, None]) & (positions[None, :] < length)
    normed_one, factor_one = norm_parts(inputs)
    attn_in = (normed_one * vec_rows[0] + vec_rows[1]).astype(jnp.bfloat16)
    projected = jnp.dot(attn_in, w_qkv, preferred_element_type=jnp.float32)
    query_heads = (projected[:, :D] + vec_rows[2]).astype(jnp.bfloat16).reshape(row_count, HEADS, HEAD_DIM)
    key_heads = projected[:, D : 2 * D].astype(jnp.bfloat16).reshape(row_count, HEADS, HEAD_DIM)
    value_heads = (projected[:, 2 * D :] + vec_rows[3]).astype(jnp.bfloat16).reshape(row_count, HEADS, HEAD_DIM)
    scores = jnp.einsum("qhd,khd->hqk", query_heads, key_heads, preferred_element_type=jnp.float32) * HEAD_DIM**-0.5
    scores = jnp.where(allowed[None], scores, -1e30)
    attn_probs = jax.nn.softmax(scores, axis=-1)
    probs_low = attn_probs.astype(jnp.bfloat16)
    attended = jnp.einsum("hqk,khd->qhd", probs_low, value_heads, preferred_element_type=jnp.float32)
    attended = attended.reshape(row_count, D).astype(jnp.bfloat16)
    hidden = inputs + jnp.dot(attended, w_out, preferred_element_type=jnp.float32) + vec_rows[4]
    normed_two, factor_two = norm_parts(hidden)
    ffn_in = (normed_two * vec_rows[5] + vec_rows[6]).astype(jnp.bfloat16)
    up_value = jnp.dot(ffn_in, w_up, preferred_element_type=jnp.float32) + up_bias
    activated = gelu_exact(up_value).astype(jnp.bfloat16)
    result = hidden + jnp.dot(activated, w_down, preferred_element_type=jnp.float32) + vec_rows[7]
    normed_three, factor_three = norm_parts(result)
    if is_last:
        result = normed_three * vec_rows[8] + vec_rows[9]
    result = result * valid_rows
    return result, (
        valid_rows,
        normed_one,
        factor_one,
        attn_in,
        query_heads,
        key_heads,
        value_heads,
        attn_probs,
        probs_low,
        attended,
        normed_two,
        factor_two,
        ffn_in,
        up_value,
        activated,
        normed_three,
        factor_three,
    )


def backward(saved, weights, is_last, cotangent):
    w_qkv, w_out, w_up, w_down, vec_rows, up_bias = weights
    (
        valid_rows,
        normed_one,
        factor_one,
        attn_in,
        query_heads,
        key_heads,
        value_heads,
        attn_probs,
        probs_low,
        attended,
        normed_two,
        factor_two,
        ffn_in,
        up_value,
        activated,
        normed_three,
        factor_three,
    ) = saved
    row_count = cotangent.shape[0]
    low = jnp.bfloat16
    grad_z = cotangent * valid_rows
    if is_last:
        grad_final_gain = jnp.sum(grad_z * normed_three, 0)
        grad_final_bias = jnp.sum(grad_z, 0)
        grad_y = norm_back(grad_z * vec_rows[8], normed_three, factor_three)
    else:
        grad_final_gain = jnp.zeros((D,), jnp.float32)
        grad_final_bias = jnp.zeros((D,), jnp.float32)
        grad_y = grad_z
    grad_branch = grad_y.astype(low)
    grad_down_bias = jnp.sum(grad_branch.astype(jnp.float32), 0)
    grad_down = jnp.einsum("sf,sd->fd", activated, grad_branch, preferred_element_type=jnp.float32).astype(low)
    grad_act = jnp.einsum("sd,fd->sf", grad_branch, w_down, preferred_element_type=jnp.float32)
    unused, gelu_pull = jax.vjp(gelu_exact, up_value)
    grad_upper = gelu_pull(grad_act)[0].astype(low)
    grad_upper_bias = jnp.sum(grad_upper.astype(jnp.float32), 0)
    grad_up = jnp.einsum("sd,sf->df", ffn_in, grad_upper, preferred_element_type=jnp.float32).astype(low)
    grad_ffn_in = jnp.einsum("sf,df->sd", grad_upper, w_up, preferred_element_type=jnp.float32)
    grad_gain_two = jnp.sum(grad_ffn_in * normed_two, 0)
    grad_bias_two = jnp.sum(grad_ffn_in, 0)
    grad_hidden = grad_y + norm_back(grad_ffn_in * vec_rows[5], normed_two, factor_two)
    grad_attn = grad_hidden.astype(low)
    grad_out_bias = jnp.sum(grad_attn.astype(jnp.float32), 0)
    grad_out = jnp.einsum("sa,sd->ad", attended, grad_attn, preferred_element_type=jnp.float32).astype(low)
    grad_mixed = jnp.einsum("sd,ad->sa", grad_attn, w_out, preferred_element_type=jnp.float32)
    grad_mixed = grad_mixed.astype(low).reshape(row_count, HEADS, HEAD_DIM)
    grad_probs = jnp.einsum("qhd,khd->hqk", grad_mixed, value_heads, preferred_element_type=jnp.float32)
    grad_value = jnp.einsum("hqk,qhd->khd", probs_low, grad_mixed, preferred_element_type=jnp.float32)
    grad_scores = attn_probs * (grad_probs - jnp.sum(grad_probs * attn_probs, -1, keepdims=True))
    grad_scores = grad_scores.astype(low)
    grad_query = jnp.einsum("hqk,khd->qhd", grad_scores, key_heads, preferred_element_type=jnp.float32) * HEAD_DIM**-0.5
    grad_key = jnp.einsum("hqk,qhd->khd", grad_scores, query_heads, preferred_element_type=jnp.float32) * HEAD_DIM**-0.5
    grad_proj = jnp.concatenate(
        [grad_query.reshape(row_count, D), grad_key.reshape(row_count, D), grad_value.reshape(row_count, D)], axis=1
    ).astype(low)
    grad_proj_wide = grad_proj.astype(jnp.float32)
    grad_query_bias = jnp.sum(grad_proj_wide[:, :D], 0)
    grad_value_bias = jnp.sum(grad_proj_wide[:, 2 * D :], 0)
    grad_qkv = jnp.einsum("sd,se->de", attn_in, grad_proj, preferred_element_type=jnp.float32).astype(low)
    grad_attn_in = jnp.einsum("se,de->sd", grad_proj, w_qkv, preferred_element_type=jnp.float32)
    grad_gain_one = jnp.sum(grad_attn_in * normed_one, 0)
    grad_bias_one = jnp.sum(grad_attn_in, 0)
    grad_inputs = grad_hidden + norm_back(grad_attn_in * vec_rows[0], normed_one, factor_one)
    grad_vec = jnp.stack(
        [
            grad_gain_one,
            grad_bias_one,
            grad_query_bias,
            grad_value_bias,
            grad_out_bias,
            grad_gain_two,
            grad_bias_two,
            grad_down_bias,
            grad_final_gain,
            grad_final_bias,
        ]
    )
    return (grad_inputs, (grad_qkv, grad_out, grad_up, grad_down, grad_vec, grad_upper_bias))


def small_layout(count):
    vec_lanes, bias_lanes = D // count, FF // count
    return vec_lanes, 128 // vec_lanes, bias_lanes, max(1, 128 // bias_lanes), max(1, bias_lanes // 128)


def pack_small(vectors, up_bias, count, here):
    vec_lanes, vec_group, bias_lanes, bias_group, bias_rows = small_layout(count)
    packed = jnp.zeros((16, 128), vectors.dtype)
    packed = lax.dynamic_update_slice(packed, vectors, (0, lax.rem(here, vec_group) * vec_lanes))
    wide = up_bias.reshape(bias_rows, bias_lanes // bias_rows)
    return lax.dynamic_update_slice(packed, wide, (10, lax.rem(here, bias_group) * bias_lanes if bias_group > 1 else 0))


def unpack_all(small, count):
    vec_lanes, vec_group, bias_lanes, bias_group, bias_rows = small_layout(count)
    small = small.reshape(2, count, 16, 128).astype(jnp.float32)
    vectors = small[:, :, :10].reshape(2, count // vec_group, vec_group, 10, 128).sum(2)
    vectors = vectors.transpose(0, 2, 1, 3).reshape(2, 10, D)
    bias = small[:, :, 10 : 10 + bias_rows].reshape(2, count // bias_group, bias_group, bias_rows * 128).sum(2)
    return vectors, bias.reshape(2, FF)


def pack_all(vectors, bias, count):
    vec_lanes, vec_group, bias_lanes, bias_group, bias_rows = small_layout(count)
    tiles = vectors.reshape(2, 10, D // 128, 128).transpose(0, 2, 1, 3)
    tiles = jnp.repeat(tiles, vec_group, axis=1)
    wide = jnp.repeat(bias.reshape(2, count // bias_group, bias_rows, 128), bias_group, axis=1)
    blank = jnp.zeros((2, count, 16 - 10 - bias_rows, 128), jnp.float32)
    return jnp.concatenate([tiles, wide, blank], axis=2)


def unpack_share(small, count, here):
    vec_lanes, vec_group, bias_lanes, bias_group, bias_rows = small_layout(count)
    vectors = lax.dynamic_slice(small, (0, lax.rem(here, vec_group) * vec_lanes), (10, vec_lanes))
    start = lax.rem(here, bias_group) * bias_lanes if bias_group > 1 else 0
    bias = lax.dynamic_slice(small, (10, start), (bias_rows, bias_lanes // bias_rows))
    return vectors, bias.reshape(bias_lanes)


def per_device(dims, hidden_in, lengths, out_grad, w_qkv, w_out, w_up, w_down, vectors, up_bias):
    core, here = lax.axis_index("pipe"), lax.axis_index("dp")
    count = 2**dims
    small = pack_small(vectors[0], up_bias[0], count, here)
    gathered = gather((w_qkv[0], w_out[0], w_up[0], w_down[0]), small, dims)
    qkv, out, up, down = (g.reshape(2, -1, g.shape[-1]) for g in gathered[:4])
    vec_rows, bias = unpack_all(gathered[4], count)
    weights = [(qkv[l], out[l], up[l], down[l], vec_rows[l], bias[l]) for l in range(2)]
    length = lax.dynamic_index_in_dim(lengths, core, 0, False)[0]
    states = lax.dynamic_index_in_dim(hidden_in, core, 0, False)[0].astype(jnp.float32)
    cotangent = lax.dynamic_index_in_dim(out_grad, core, 0, False)[0].astype(jnp.float32)
    first, saved_first = forward(states, length, weights[0], False)
    second_in = first.astype(jnp.bfloat16).astype(jnp.float32)
    result, saved_second = forward(second_in, length, weights[1], True)
    grad_second, grads_second = backward(saved_second, weights[1], True, cotangent)
    grad_first, grads_first = backward(
        saved_first, weights[0], False, grad_second.astype(jnp.bfloat16).astype(jnp.float32)
    )
    both = [jnp.stack([a, b]) for a, b in zip(grads_first, grads_second)]
    rows = D // count
    shards = [both[0], both[1], both[2], both[3]]
    shards = [s.reshape((2,) + (2,) * dims + (-1, s.shape[-1])) for s in shards[:3]] + [
        both[3].reshape((2,) + (2,) * dims + (4, rows, D))
    ]
    sums = scatter(shards, pack_all(both[4], both[5], count).reshape((2,) + (2,) * dims + (16, 128)), dims)
    grad_vec, grad_bias = unpack_share(sums[4], count, here)
    mine = jnp.where(core == 0, grad_first, result)
    theirs = lax.ppermute(jnp.where(core == 0, result, grad_first), "pipe", [(0, 1), (1, 0)])
    edges = jnp.where(core == 0, jnp.stack([mine, theirs]), jnp.stack([theirs, mine]))
    return (
        edges[None, :, None],
        sums[0][None],
        sums[1][None],
        sums[2][None],
        sums[3].reshape(1, -1, D),
        grad_vec[None],
        grad_bias[None],
    )


def solution(mesh):
    dims = (mesh.shape["dp"] - 1).bit_length()
    placed = (
        P(None, "dp", None, None),
        P(None, "dp"),
        P(None, "dp", None, None),
        P("pipe", "dp", None),
        P("pipe", "dp", None),
        P("pipe", "dp", None),
        P("pipe", "dp", None),
        P("pipe", None, "dp"),
        P("pipe", "dp"),
    )
    return jax.shard_map(
        functools.partial(per_device, dims),
        mesh=mesh,
        in_specs=placed,
        out_specs=(
            P("pipe", None, "dp", None, None),
            P("pipe", "dp", None),
            P("pipe", "dp", None),
            P("pipe", "dp", None),
            P("pipe", "dp", None),
            P("pipe", None, "dp"),
            P("pipe", "dp"),
        ),
        check_vma=False,
    )
```

```python
import functools
from types import SimpleNamespace

import jax
import jax.numpy as jnp
from jax import lax
from jax.experimental import pallas as pl
from jax.experimental.pallas import tpu as pltpu
from jax.sharding import PartitionSpec as P

D = 1024
HEADS = 16
HEAD_DIM = 64
FF = 4096
SEQ = 256
EPS = 1e-05
SCALE = HEAD_DIM**-0.5
MESH = pl.DeviceIdType.MESH
LOW = jnp.bfloat16
WIDE = jnp.float32
QKV, OUT, UP, DOWN = "qkv", "out", "up", "down"
FLAT = "_flat"
PIPE, DP = "pipe", "dp"
KINDS = [(QKV, 0), (QKV, 1), (QKV, 2), (OUT, 0), (UP, 0), (UP, 1), (DOWN, 0), (DOWN, 1)]
NU = len(KINDS)
GATHER_FIRST = -12
GATHER_LAGS = [2, 0, -3, -5]
GATHER_READY = 3
SMALL_AT = [0, 6, 12, 18, 24, 30]


def axis_order(dims, u):
    kind, block = KINDS[u]
    if kind in (UP, DOWN):
        return tuple(range(dims - 1))
    if dims == 4:
        return [(0, 1, 2, 3), (2, 0, 1, 3), (2, 0, 1, 3), (3, 0, 1, 2)][u]
    return tuple((i + 2 * u) % dims for i in range(dims))


def place(dims):
    core, here = lax.axis_index(PIPE), lax.axis_index(DP)
    bits = [lax.rem(lax.div(here, 2 ** (dims - 1 - i)), 2) for i in range(dims)]
    partners = [(core, here + (1 - 2 * bits[i]) * 2 ** (dims - 1 - i)) for i in range(dims)]
    return core, bits, partners, (1 - core, here)


def greet(everyone):
    barrier = pltpu.get_barrier_semaphore()
    for device in everyone:
        pl.semaphore_signal(barrier, inc=1, device_id=device, device_id_type=MESH)
    pl.semaphore_wait(barrier, len(everyone))


def remote(source, target, send, recv, device):
    return pltpu.make_async_remote_copy(
        src_ref=source, dst_ref=target, send_sem=send, recv_sem=recv, device_id=device, device_id_type=MESH
    )


def span(start, size):
    if isinstance(start, int):
        return pl.ds(start, size)
    return pl.ds(pl.multiple_of(start, size), size)


def for_each(count, body):
    lax.fori_loop(0, count, lambda i, carry: (body(i), carry)[1], 0)


def unit_columns(u, column_half):
    kind, block = KINDS[u]
    if kind == DOWN:
        return span(block * 512 + column_half * 256, 256)
    return span(block * 1024 + column_half * 512, 512)


def norm_parts(values):
    center = values - jnp.mean(values, -1, keepdims=True)
    factor = lax.rsqrt(jnp.mean(center * center, -1, keepdims=True) + EPS)
    return (center * factor, factor)


def norm_back(grad_normed, normed, factor):
    return factor * (
        grad_normed
        - jnp.mean(grad_normed, -1, keepdims=True)
        - normed * jnp.mean(grad_normed * normed, -1, keepdims=True)
    )


def dot(left, right, dims=((1,), (0,))):
    return lax.dot_general(left, right, (dims, ((), ())), preferred_element_type=WIDE)


BY_ROWS = ((0,), (0,))
BY_COLUMNS = ((1,), (1,))


def small_layout(count):
    vec_lanes, bias_lanes = D // count, FF // count
    return vec_lanes, 128 // vec_lanes, bias_lanes, max(1, 128 // bias_lanes), max(1, bias_lanes // 128)


def head_masks():
    lanes = lax.broadcasted_iota(jnp.int32, (1, 128), 1)
    first = (lanes < HEAD_DIM).astype(WIDE)
    return first, 1.0 - first


def valid_rows(length, start, count):
    rows = lax.broadcasted_iota(jnp.int32, (count, 1), 0) + start
    return (rows < length).astype(WIDE)


FORWARD_IN = ["w_qkv", "w_out", "w_up", "w_down", "small", "hidden", "lengths"]
S = "s_"
SAVED = ["x", "a", "q", "k", "v", "o", "p", "h", "c", "g", "gp"]
LOADS = ["vecs", "og", "y", "w_down", "w_up", "w_qkv", "w_out"] + SAVED
N = SimpleNamespace(**{n: n for n in LOADS})


def saved_shapes():
    wide = lambda *s: (s, WIDE)
    low = lambda *s: (s, LOW)
    return dict(
        x=low(SEQ, D),
        a=low(SEQ, D),
        q=low(SEQ, D),
        k=low(SEQ, D),
        v=low(SEQ, D),
        o=low(SEQ, D),
        p=low(HEADS, SEQ, SEQ),
        h=wide(SEQ, D),
        c=low(2, SEQ, D),
        g=low(2, SEQ, FF // 2),
        gp=low(2, SEQ, FF // 2),
    )


def forward_kernel(dims, names, *refs):
    R = SimpleNamespace(**dict(zip(names, refs)))
    core, bits, partners, sibling = place(dims)
    own = tuple(bits)
    half = bits[-1]
    mate = partners[-1]
    greet([sibling] + partners)
    total = 2 * NU
    count = 2**dims
    saved = SimpleNamespace(**{n: [getattr(R, n + str(l)) for l in range(2)] for n in SAVED})

    def first_pairs(u, layer, column_half):
        kind, block = KINDS[u]
        cols = unit_columns(u, column_half)
        if kind == UP:
            return [
                (R.w_up.at[half, :, cols], R.up.at[(layer,) + own + (slice(None), cols)]),
                (R.w_up.at[1 - half, :, cols], R.stage.at[layer, :, cols]),
            ]
        if kind == DOWN:
            return [(R.w_down.at[:, cols], R.down.at[(layer,) + own[:-1] + (slice(None), cols)])]
        return [(getattr(R, "w_" + kind).at[:, cols], getattr(R, kind).at[(layer,) + own + (slice(None), cols)])]

    def first_local(u, layer):
        return [
            pltpu.make_async_copy(s, t, R.local_sem.at[u, i])
            for i, (s, t) in enumerate(first_pairs(u, layer, core))
        ]

    def first_remote(u, layer):
        return [
            remote(s, t, R.first_send.at[u, i], R.first_recv.at[u, i], sibling)
            for i, (s, t) in enumerate(first_pairs(u, layer, 1 - core))
        ]

    def chain(v):
        layer, u = v // NU, v % NU
        kind, block = KINDS[u]
        cols = unit_columns(u, core)
        moves = []
        if kind == UP:
            moves.append((R.stage.at[layer, :, cols], R.up.at[(layer,) + own + (slice(None), cols)], mate))
        order = axis_order(dims, u)
        known = dims - 1 if kind == DOWN else dims
        free = {dims - 1} if kind == UP else set()
        for k in range(len(order) + 1):
            gathered = set(order[:k]) | free
            where = tuple(slice(None) if i in gathered else bits[i] for i in range(known))
            ref = getattr(R, kind).at[(layer,) + where + (slice(None), cols)]
            moves.append((ref, ref, partners[order[k]] if k < len(order) else sibling))
        return [remote(s, t, R.send.at[v, i], R.recv.at[v, i], d) for i, (s, t, d) in enumerate(moves)]

    def small_step(k):
        where = tuple(slice(None) if i < k else bits[i] for i in range(dims))
        ref = R.small_all.at[(core,) + where]
        return remote(ref, ref, R.small_send.at[k], R.small_recv.at[k], partners[k] if k < dims else sibling)

    small_own = pltpu.make_async_copy(R.small, R.small_all.at[(core,) + own], R.io.at[0])
    small_own.start()
    load_x = pltpu.make_async_copy(R.hidden.at[core], saved.x[0], R.io.at[1])
    load_x.start()
    for layer in range(2):

        @pl.when(core == layer)
        def _():
            for u in range(NU):
                for copy in first_remote(u, layer) + first_local(u, layer):
                    copy.start()

    def arrive(v):
        layer, u = v // NU, v % NU

        @pl.when(core == layer)
        def _():
            for copy in first_local(u, layer):
                copy.wait()
            for copy in first_remote(u, layer):
                copy.wait_send()

        @pl.when(core != layer)
        def _():
            for copy in first_remote(u, layer):
                copy.wait_recv()

    length = R.lengths[core]
    vecs, biases = R.vecs, R.biases
    first_head, second_head = head_masks()

    def assemble():
        vec_lanes, vec_group, bias_lanes, bias_group, bias_rows = small_layout(count)
        small = R.small_all

        def shard(layer, d):
            return small[(layer,) + tuple((d >> (dims - 1 - i)) & 1 for i in range(dims))].astype(WIDE)

        def half_shard(layer, b):
            lead = tuple((b >> (dims - 2 - i)) & 1 for i in range(dims - 1))
            return small[(layer,) + lead + (half,)].astype(WIDE)

        for layer in range(2):
            for t in range(D // 128):
                vecs[layer, :, t * 128 : (t + 1) * 128] = sum(
                    shard(layer, d) for d in range(t * vec_group, (t + 1) * vec_group)
                )
            for t in range(count // 2 // bias_group):
                tile = sum(half_shard(layer, b) for b in range(t * bias_group, (t + 1) * bias_group))
                for i in range(bias_rows):
                    at = (t * bias_rows + i) * 128
                    biases[layer, 0:1, at : at + 128] = tile[10 + i : 11 + i, :]

    save_queue = []

    def save(name, layer):
        copy = pltpu.make_async_copy(
            getattr(saved, name)[layer], getattr(R, S + name).at[layer], R.save_sem.at[layer, SAVED.index(name)]
        )
        copy.start()
        save_queue.append(copy)

    def vec(layer, i, cols=slice(None)):
        return vecs[layer, i : i + 1, cols]

    def load_weight(v):
        layer, u = v // NU, v % NU
        kind, block = KINDS[u]
        if kind == DOWN:
            flat = R.down_flat.at[layer, :, pl.ds(block * 512, 512)]
            target = R.w_low.at[:, pl.ds(block * 512, 512)]
        else:
            flat = getattr(R, kind + FLAT).at[layer, :, pl.ds(block * 1024, 1024)]
            target = R.w_slots.at[u % 2]
        return pltpu.make_async_copy(flat, target, R.weight_sem.at[u % 4])

    def first_norm(layer):
        def rows(i):
            at = span(i * 32, 32)
            normed, unused = norm_parts(saved.x[layer][at, :].astype(WIDE))
            saved.a[layer][at, :] = (normed * vec(layer, 0) + vec(layer, 1)).astype(LOW)

        for_each(SEQ // 32, rows)
        save(N.x, layer)
        save(N.a, layer)

    def project(layer, block):
        target = (saved.q, saved.k, saved.v)[block][layer]
        weight = R.w_slots.at[block % 2]

        def columns(n):
            at = span(n * 256, 256)
            values = dot(saved.a[layer][...], weight[:, at])
            if block == 0:
                values = (values + vec(layer, 2, at)).astype(LOW) * SCALE
            elif block == 2:
                values = values + vec(layer, 3, at)
            target[:, at] = values.astype(LOW)

        for_each(D // 256, columns)
        save((N.q, N.k, N.v)[block], layer)

    def attention(layer):
        key_ids = lax.broadcasted_iota(jnp.int32, (SEQ, SEQ), 0)
        query_ids = lax.broadcasted_iota(jnp.int32, (SEQ, SEQ), 1)
        blocked = jnp.where((key_ids <= query_ids) & (key_ids < length), 0.0, -1e30)

        def pair(n):
            at = span(n * 128, 128)
            query, key, value = (part[layer][:, at] for part in (saved.q, saved.k, saved.v))
            parts = []
            for i, mask in enumerate((first_head, second_head)):
                scores = dot(key, query * mask.astype(LOW), BY_COLUMNS) + blocked
                weights = jnp.exp(scores - jnp.max(scores, 0, keepdims=True))
                probs = (weights * (1.0 / jnp.sum(weights, 0, keepdims=True))).astype(LOW)
                saved.p[layer][2 * n + i] = probs
                parts.append(dot(probs, value, BY_ROWS) * mask)
            saved.o[layer][:, at] = (parts[0] + parts[1]).astype(LOW)

        for_each(HEADS // 2, pair)
        save(N.p, layer)
        save(N.o, layer)

    def send_c(layer):
        ref = saved.c[layer]
        return remote(ref.at[0], ref.at[1], R.act_send.at[layer, 0], R.act_recv.at[layer, 0], mate)

    def attend_out(layer):
        weight = R.w_slots.at[1]
        hidden = saved.h[layer]

        def columns(n):
            at = span(n * 256, 256)
            values = dot(saved.o[layer][...], weight[:, at])
            hidden[:, at] = saved.x[layer][:, at].astype(WIDE) + values + vec(layer, 4, at)

        def rows(i):
            at = span(i * 32, 32)
            normed, unused = norm_parts(hidden[at, :])
            saved.c[layer][0, at, :] = (normed * vec(layer, 5) + vec(layer, 6)).astype(LOW)

        for_each(D // 256, columns)
        for_each(SEQ // 32, rows)
        send_c(layer).start()
        save(N.h, layer)

    def feed_up(layer, block):
        if block == 0:
            send_c(layer).wait()
            save(N.c, layer)
        weight = R.w_slots.at[block]

        def columns(n):
            at = span(n * 256, 256)
            to = span(block * 1024 + n * 256, 256)
            for who in range(2):
                value = dot(saved.c[layer][who], weight[:, at]) + biases[layer, 0:1, to]
                share = 0.5 + 0.5 * lax.erf(value * 0.7071067811865476)
                slope = share + value * (jnp.exp(value * value * -0.5) * 0.3989422804014327)
                saved.g[layer][who, :, to] = (value * share).astype(LOW)
                saved.gp[layer][who, :, to] = slope.astype(LOW)

        for_each(4, columns)
        if block == 1:
            save(N.g, layer)
            save(N.gp, layer)

    def send_part(layer, block):
        at = pl.ds(block * 512, 512)
        return remote(
            R.part.at[layer, 0, :, at],
            R.part.at[layer, 1, :, at],
            R.act_send.at[layer, 1 + block],
            R.act_recv.at[layer, 1 + block],
            mate,
        )

    def feed_down(layer, block):
        def theirs(n):
            at = span(block * 512 + n * 256, 256)
            R.part[layer, 0, :, at] = dot(saved.g[layer][1], R.w_low[:, at]).astype(LOW)

        def mine(n):
            at = span(block * 512 + n * 256, 256)
            values = dot(saved.g[layer][0], R.w_low[:, at])
            R.y[:, at] = saved.h[layer][:, at] + values + vec(layer, 7, at)

        for_each(2, theirs)
        send_part(layer, block).start()
        for_each(2, mine)

    def end(layer):
        for block in range(2):
            send_part(layer, block).wait()

        def rows(i):
            at = span(i * 32, 32)
            valid = valid_rows(length, i * 32, 32)
            values = R.y[at, :] + R.part[layer, 1, at, :].astype(WIDE)
            if layer == 0:
                saved.x[1][at, :] = (values * valid).astype(LOW)
            else:
                R.y[at, :] = values
                normed, unused = norm_parts(values)
                R.z[at, :] = (normed * vec(1, 8) + vec(1, 9)) * valid

        for_each(SEQ // 32, rows)

    def work(v):
        layer, u = v // NU, v % NU
        kind, block = KINDS[u]
        load_weight(v).start()
        if u == 0:
            first_norm(layer)
        load_weight(v).wait()
        if kind == QKV:
            project(layer, block)
            if block == 2:
                attention(layer)
        elif kind == OUT:
            attend_out(layer)
        elif kind == UP:
            feed_up(layer, block)
        else:
            feed_down(layer, block)
            if block == 1:
                end(layer)

    chains = [chain(v) for v in range(total)]
    events = []
    for v in range(total):
        for i in range(len(chains[v])):
            left = len(chains[v]) - 1 - i
            lag = GATHER_LAGS[left] if left < len(GATHER_LAGS) else GATHER_LAGS[-1] - left + len(GATHER_LAGS) - 1
            events.append((v + (lag if i else min(GATHER_FIRST, lag)), -i, v))
        events.append((v + GATHER_READY, -9, v))
    events = [(v, -i) for unused, i, v in sorted(events)]
    for k in range(dims + 2):
        events.insert(SMALL_AT[min(k, len(SMALL_AT) - 1)] + max(0, k - 5), (-1, k))
    small_own.wait()
    load_x.wait()
    for v, i in events:
        if v < 0:
            if i > 0:
                small_step(i - 1).wait()
            if i <= dims:
                small_step(i).start()
            else:
                assemble()
        elif i == 9:
            chains[v][-1].wait()
            work(v)
        else:
            if i == 0:
                arrive(v)
            else:
                chains[v][i - 1].wait()
            chains[v][i].start()

    last = [(R.y, R.s_y, 0), (R.z, R.s_z, 1), (R.vecs, R.s_vecs, 2)]
    for source, target, i in last:
        pltpu.make_async_copy(source, target, R.last_sem.at[i]).start()
    for copy in save_queue:
        copy.wait()
    for source, target, i in last:
        pltpu.make_async_copy(source, target, R.last_sem.at[i]).wait()


def forward(shards, small, hidden, lengths, dims):
    rows = D // 2**dims
    bits = (2,) * dims
    outs = dict(
        qkv=((2,) + bits + (rows, 3 * D), LOW),
        out=((2,) + bits + (rows, D), LOW),
        up=((2,) + bits + (rows, FF // 2), LOW),
        down=((2,) + bits[:-1] + (4 * rows, D), LOW),
        stage=((2, rows, FF // 2), LOW),
    )
    for name, (shape, dtype) in saved_shapes().items():
        outs[S + name] = ((2,) + shape, dtype)
    outs[S + N.y] = ((SEQ, D), WIDE)
    outs[S + "z"] = ((SEQ, D), WIDE)
    outs[S + N.vecs] = ((2, 16, D), WIDE)
    dma = pltpu.SemaphoreType.DMA
    total = 2 * NU
    scratch = dict(
        small_all=pltpu.VMEM((2,) + bits + (16, 128), LOW),
        vecs=pltpu.VMEM((2, 16, D), WIDE),
        biases=pltpu.VMEM((2, 8, FF // 2), WIDE),
        w_slots=pltpu.VMEM((2, D, D), LOW),
        w_low=pltpu.VMEM((FF // 2, D), LOW),
        part=pltpu.VMEM((2, 2, SEQ, D), LOW),
        y=pltpu.VMEM((SEQ, D), WIDE),
        z=pltpu.VMEM((SEQ, D), WIDE),
        local_sem=dma((NU, 2)),
        first_send=dma((NU, 2)),
        first_recv=dma((NU, 2)),
        send=dma((total, dims + 2)),
        recv=dma((total, dims + 2)),
        small_send=dma((dims + 1,)),
        small_recv=dma((dims + 1,)),
        io=dma((2,)),
        save_sem=dma((2, len(SAVED))),
        weight_sem=dma((4,)),
        act_send=dma((2, 3)),
        act_recv=dma((2, 3)),
        last_sem=dma((3,)),
    )
    for name, (shape, dtype) in saved_shapes().items():
        for layer in range(2):
            scratch[name + str(layer)] = pltpu.VMEM(shape, dtype)
    names = FORWARD_IN + list(outs) + list(scratch)

    def kernel(*refs):
        by_name = dict(zip(names, refs))
        extra = dict(
            qkv_flat=by_name[QKV].reshape(2, D, 3 * D),
            out_flat=by_name[OUT].reshape(2, D, D),
            up_flat=by_name[UP].reshape(2, D, FF // 2),
            down_flat=by_name[DOWN].reshape(2, FF // 2, D),
        )
        forward_kernel(dims, names + list(extra), *refs, *extra.values())

    anywhere = pl.BlockSpec(memory_space=pl.ANY)
    results = pl.pallas_call(
        kernel,
        out_shape=[jax.ShapeDtypeStruct(s, t) for s, t in outs.values()],
        in_specs=[anywhere] * 6 + [pl.BlockSpec(memory_space=pltpu.SMEM)],
        out_specs=[anywhere] * len(outs),
        scratch_shapes=list(scratch.values()),
        compiler_params=pltpu.CompilerParams(collective_id=1, has_side_effects=True, vmem_limit_bytes=60 << 20),
        name="forward",
    )(*shards, small, hidden, lengths)
    return dict(zip(outs, results))


def pack_small(vectors, up_bias, count, here):
    vec_lanes, vec_group, bias_lanes, bias_group, bias_rows = small_layout(count)
    packed = jnp.zeros((16, 128), vectors.dtype)
    packed = lax.dynamic_update_slice(packed, vectors, (0, lax.rem(here, vec_group) * vec_lanes))
    wide = up_bias.reshape(bias_rows, bias_lanes // bias_rows)
    at = lax.rem(lax.div(here, 2), bias_group) * bias_lanes if bias_group > 1 else 0
    return lax.dynamic_update_slice(packed, wide, (10, at))


def forward_call(dims, here, core, hidden_in, lengths, w_qkv, w_out, w_up, w_down, vectors, up_bias):
    count = 2**dims
    rows = D // count
    small = pack_small(vectors[0], up_bias[0], count, here)
    halves = w_up[0].reshape(rows, count // 2, 2, FF // count).transpose(2, 0, 1, 3).reshape(2, rows, FF // 2)
    return forward((w_qkv[0], w_out[0], halves, w_down[0]), small, hidden_in[:, 0], lengths[:, 0], dims)
BACK = [(DOWN, 0), (DOWN, 1), (UP, 0), (UP, 1), (OUT, 0), (QKV, 0), (QKV, 1), (QKV, 2)]
SCATTER_LAGS = [1, 3, 4, 5, 6]
HELD, B = "held", "b_"
BACK_WEIGHTS = [QKV, OUT, UP, DOWN]
BACK_IN = BACK_WEIGHTS + [S + n for n in SAVED + ["y", "z", "vecs"]] + ["out_grad", "lengths"]


def box_name(u, k):
    return "box%d_%d" % (u, k)


def backward_kernel(dims, names, *refs):
    R = SimpleNamespace(**dict(zip(names, refs)))
    core, bits, partners, sibling = place(dims)
    own = tuple(bits)
    half = bits[-1]
    mate = partners[-1]
    greet([sibling] + partners)
    total = 2 * NU
    count = 2**dims
    length = R.lengths[core]
    vecs, grads = R.vecs, R.grads
    first_head, second_head = head_masks()

    def load(name, layer):
        if name == N.y:
            source = R.s_y
        elif name == N.og:
            source = R.out_grad.at[core]
        elif name == N.vecs:
            source = R.s_vecs
        elif name in (N.w_down, N.w_up, N.w_qkv, N.w_out):
            source = getattr(R, name[2:] + FLAT).at[layer]
        else:
            source = getattr(R, S + name).at[layer]
        if name == N.vecs:
            target = vecs
        elif name == N.w_up:
            target = R.b_w_wide.at[:, pl.ds(0, FF // 2)]
        elif name == N.w_qkv:
            target = R.b_w_wide
        else:
            target = getattr(R, B + name)
        return pltpu.make_async_copy(source, target, R.load_sem.at[LOADS.index(name)])

    def need(layer, *which):
        for name in which:
            load(name, layer).wait()

    def again(layer, *which):
        if layer == 1:
            for name in which:
                load(name, 0).start()

    def unit_of(v):
        return 1 - v // NU, BACK[v % NU]

    def columns_of(v, column_half):
        kind, block = BACK[v % NU]
        if kind == DOWN:
            return span(block * 512 + column_half * 256, 256)
        return span(block * 1024 + column_half * 512, 512)

    def order_of(v):
        return tuple(reversed(axis_order(dims, KINDS.index(BACK[v % NU]))))

    def held(v):
        return getattr(R, HELD + str(v % NU))

    def box(v, k):
        if k == 0:
            kind, block = BACK[v % NU]
            return (R.down_box if kind == DOWN else R.wide_box).at[v % 2]
        return getattr(R, box_name(v % NU, k))

    def stage(v):
        kind, block = BACK[v % NU]
        return (R.down_stage if kind == DOWN else R.wide_stage).at[v % 2]

    def is_up(v):
        return BACK[v % NU][0] == UP

    def steps(v):
        return len(order_of(v)) + (1 if is_up(v) else 0)

    def where(v, k, away):
        order = order_of(v)
        place_of = []
        for i in range(dims - 1 if BACK[v % NU][0] == DOWN else dims):
            if i in order[: max(k - 1, 0)]:
                place_of.append(bits[i])
            elif 0 < k <= len(order) and i == order[k - 1]:
                place_of.append(1 - bits[i] if away else bits[i])
            elif k > len(order) and i == dims - 1:
                place_of.append(1 - half if away else half)
            elif k > len(order):
                place_of.append(bits[i])
            else:
                place_of.append(slice(None))
        return tuple(place_of)

    def device_of(v, k):
        if k == 0:
            return sibling
        return partners[order_of(v)[k - 1]] if k <= len(order_of(v)) else mate

    def move(v, k):
        source = stage(v) if k == 0 else held(v).at[where(v, k, True)]
        return remote(source, box(v, k), R.send.at[v, k], R.recv.at[v, k], device_of(v, k))

    def earlier(v, k):
        if k > 0 or BACK[v % NU][0] == DOWN:
            return v - NU if v >= NU else None
        wide = [w for w in range(total) if BACK[w % NU][0] != DOWN and w % 2 == v % 2 and w < v]
        return wide[-1] if wide else None

    def later(v, k):
        return any(earlier(w, k) == v for w in range(v + 1, total))

    def begin(v, k):
        if earlier(v, k) is not None:
            pl.semaphore_wait(R.credit.at[v % NU, k], 1)
        move(v, k).start()

    def consumed(v, k):
        for w in range(v + 1, total):
            if earlier(w, k) == v:
                pl.semaphore_signal(
                    R.credit.at[w % NU, k], inc=1, device_id=device_of(v, k), device_id_type=MESH
                )

    def finals(v):
        kind, block = BACK[v % NU]
        cols = columns_of(v, core)
        if kind == UP:
            return [
                (held(v).at[own], R.g_up.at[half, :, cols]),
                (box(v, dims), R.g_up.at[1 - half, :, cols]),
            ]
        if kind == DOWN:
            return [(held(v).at[own[:-1]], R.g_down.at[:, cols])]
        return [(held(v).at[own], getattr(R, "g_" + kind).at[:, cols])]

    def final_local(v):
        return [
            pltpu.make_async_copy(s, t, R.out_sem.at[v, i]) for i, (s, t) in enumerate(finals(v))
        ]

    def final_remote(v):
        return [
            remote(s, t, R.end_send.at[v, i], R.end_recv.at[v, i], sibling)
            for i, (s, t) in enumerate(finals(v))
        ]

    def finish(v):
        @pl.when(core == unit_of(v)[0])
        def _():
            for copy in final_local(v):
                copy.start()

        @pl.when(core != unit_of(v)[0])
        def _():
            for copy in final_remote(v):
                copy.start()

    def finished(v):
        @pl.when(core == unit_of(v)[0])
        def _():
            for copy in final_local(v):
                copy.wait()

        @pl.when(core != unit_of(v)[0])
        def _():
            for copy in final_remote(v):
                copy.wait_send()
        if is_up(v):
            consumed(v, dims)

    def event(v, k):
        move(v, k).wait()
        if not (is_up(v) and k == steps(v)):
            view = held(v).at[where(v, k, False)]
            view[...] = view[...] + box(v, k)[...]
            consumed(v, k)
        if k < steps(v):
            begin(v, k + 1)
        else:
            finish(v)

    def vec(layer, i):
        return vecs[layer, i : i + 1, :]

    def collect(layer, i, values):
        grads[layer, i : i + 1, :] = grads[layer, i : i + 1, :] + jnp.sum(values, 0, keepdims=True)

    def send_e(layer):
        ref = R.e
        return remote(ref.at[0], ref.at[1], R.act_send.at[layer, 0], R.act_recv.at[layer, 0], mate)

    def send_dc(layer):
        ref = R.dc_part
        return remote(ref.at[0], ref.at[1], R.act_send.at[layer, 1], R.act_recv.at[layer, 1], mate)

    def top(layer):
        if layer == 1:
            need(1, N.vecs, N.og, N.y)

        def rows(i):
            at = span(i * 32, 32)
            valid = valid_rows(length, i * 32, 32)
            if layer == 1:
                grad_z = R.b_og[at, :].astype(WIDE) * valid
                normed, factor = norm_parts(R.b_y[at, :])
                collect(1, 8, grad_z * normed)
                collect(1, 9, grad_z)
                grad_y = norm_back(grad_z * vec(1, 8), normed, factor)
            else:
                grad_y = R.dx[at, :].astype(WIDE) * valid
            R.dy[at, :] = grad_y
            branch = grad_y.astype(LOW)
            R.e[0, at, :] = branch
            collect(layer, 7, branch.astype(WIDE))

        for_each(SEQ // 32, rows)
        send_e(layer).start()

    def produce(v, body, quarter_shape):
        for target, column_half in ((stage(v), 1 - core), (held(v), core)):
            cols = columns_of(v, column_half)

            def quarter(i):
                target[lax.div(i, 2), lax.rem(i, 2)] = body(i, cols).astype(LOW).reshape(quarter_shape)

            for_each(4, quarter)
            if column_half is not core:
                begin(v, 0)

    def pair_rows(ref, cols):
        values = ref[:, :, cols]
        return values.reshape(2 * SEQ, values.shape[-1])

    inner = (2,) * (dims - 2) + (D // count, 512)
    down_inner = (2,) * (dims - 3) + (FF // count, 256)

    def grad_down(layer, v, block):
        if block == 0:
            need(layer, N.g)
            send_e(layer).wait()
        produce(
            v,
            lambda i, cols: dot(pair_rows(R.b_g, span(i * 512, 512)), pair_rows(R.e, cols), BY_ROWS),
            down_inner,
        )
        if block == 1:
            again(layer, N.g)

    def feed_back(layer):
        need(layer, N.w_down, N.gp)

        def hidden(n):
            at = span(n * 256, 256)
            rows = pair_rows(R.e, slice(None))
            grad_act = dot(rows, R.b_w_down[at, :], BY_COLUMNS)
            grad_upper = (grad_act * pair_rows(R.b_gp, at).astype(WIDE)).astype(LOW)
            R.b_gp[:, :, at] = grad_upper.reshape(2, SEQ, 256)
            R.bias_grads[layer, 0:1, at] = jnp.sum(grad_upper.astype(WIDE), 0, keepdims=True)

        for_each(FF // 2 // 256, hidden)
        again(layer, N.w_down)
        need(layer, N.w_up)
        wide = pl.ds(0, FF // 2)

        def theirs(n):
            at = span(n * 256, 256)
            R.dc_part[0, :, at] = dot(R.b_gp[1], R.b_w_wide[at, wide], BY_COLUMNS).astype(LOW)

        def mine(n):
            at = span(n * 256, 256)
            R.dc[:, at] = dot(R.b_gp[0], R.b_w_wide[at, wide], BY_COLUMNS)

        for_each(D // 256, theirs)
        send_dc(layer).start()
        for_each(D // 256, mine)
        load(N.w_qkv, layer).start()

    def grad_up(layer, v, block):
        if block == 0:
            need(layer, N.c)

        def body(i, cols):
            return dot(pair_rows(R.b_c, span(i * 256, 256)), pair_rows(R.b_gp, cols), BY_ROWS)

        produce(v, body, inner)
        if block == 1:
            again(layer, N.c, N.gp)

    def middle(layer):
        need(layer, N.h)
        send_dc(layer).wait()

        def rows(i):
            at = span(i * 32, 32)
            grad_in = R.dc[at, :] + R.dc_part[1, at, :].astype(WIDE)
            normed, factor = norm_parts(R.b_h[at, :])
            collect(layer, 5, grad_in * normed)
            collect(layer, 6, grad_in)
            grad_hidden = R.dy[at, :] + norm_back(grad_in * vec(layer, 5), normed, factor)
            R.dy[at, :] = grad_hidden
            branch = grad_hidden.astype(LOW)
            R.f[at, :] = branch
            collect(layer, 4, branch.astype(WIDE))

        for_each(SEQ // 32, rows)
        again(layer, N.h)

    def grad_out(layer, v):
        need(layer, N.o)
        produce(v, lambda i, cols: dot(R.b_o[:, span(i * 256, 256)], R.f[:, cols], BY_ROWS), inner)
        again(layer, N.o)

    def attention_back(layer):
        need(layer, N.w_out)

        def columns(n):
            at = span(n * 256, 256)
            R.do[:, at] = dot(R.f[...], R.b_w_out[at, :], BY_COLUMNS).astype(LOW)

        for_each(D // 256, columns)
        again(layer, N.w_out)
        need(layer, N.q, N.k, N.v, N.p)

        def pair(n):
            at = span(n * 128, 128)
            query, key, value, grad_o = R.b_q[:, at], R.b_k[:, at], R.b_v[:, at], R.do[:, at]
            sums = [0.0, 0.0, 0.0]
            for i, mask in enumerate((first_head.astype(LOW), second_head.astype(LOW))):
                probs = R.b_p[2 * n + i]
                grad_head = grad_o * mask
                wide = probs.astype(WIDE)
                grad_probs = dot(value, grad_head, BY_COLUMNS)
                shift = jnp.sum(grad_probs * wide, 0, keepdims=True)
                grad_scores = (wide * (grad_probs - shift)).astype(LOW)
                sums[0] += dot(grad_scores, key * mask, BY_ROWS)
                sums[1] += dot(grad_scores, query * mask)
                sums[2] += dot(probs, grad_head)
            sums[0] = sums[0] * SCALE
            for j in range(3):
                low = sums[j].astype(LOW)
                R.dp[:, pl.ds(pl.multiple_of(n * 128 + j * D, 128), 128)] = low
                if j != 1:
                    row = 2 if j == 0 else 3
                    grads[layer, row : row + 1, at] = jnp.sum(low.astype(WIDE), 0, keepdims=True)

        for_each(HEADS // 2, pair)
        again(layer, N.q, N.k, N.v, N.p)

    def grad_qkv(layer, v, block):
        if block == 0:
            need(layer, N.a)
        produce(v, lambda i, cols: dot(R.b_a[:, span(i * 256, 256)], R.dp[:, cols], BY_ROWS), inner)
        if block == 2:
            again(layer, N.a)

    def bottom(layer):
        need(layer, N.w_qkv)

        def columns(n):
            at = span(n * 256, 256)
            R.dc[:, at] = dot(R.dp[...], R.b_w_wide[at, :], BY_COLUMNS)

        for_each(D // 256, columns)
        again(layer, N.w_up)
        need(layer, N.x)

        def rows(i):
            at = span(i * 32, 32)
            grad_in = R.dc[at, :]
            normed, factor = norm_parts(R.b_x[at, :].astype(WIDE))
            collect(layer, 0, grad_in * normed)
            collect(layer, 1, grad_in)
            grad_x = R.dy[at, :] + norm_back(grad_in * vec(layer, 0), normed, factor)
            if layer == 1:
                R.dx[at, :] = grad_x.astype(LOW)
            else:
                R.b_y[at, :] = grad_x

        for_each(SEQ // 32, rows)
        again(layer, N.x)

    def spread():
        vec_lanes, vec_group, bias_lanes, bias_group, bias_rows = small_layout(count)
        tiles = R.tiles
        tiles[...] = jnp.zeros_like(tiles)
        for layer in range(2):
            for d in range(count):
                lead = tuple((d >> (dims - 1 - i)) & 1 for i in range(dims))
                t = d // vec_group
                tiles[(layer,) + lead + (slice(0, 10),)] = grads[layer, 0:10, t * 128 : (t + 1) * 128]
            for b in range(count // 2):
                lead = tuple((b >> (dims - 2 - i)) & 1 for i in range(dims - 1))
                for i in range(bias_rows):
                    at = (b // bias_group * bias_rows + i) * 128
                    tiles[(layer,) + lead + (half, slice(10 + i, 11 + i))] = R.bias_grads[layer, 0:1, at : at + 128]

    def small_move(k):
        if k == 0:
            return remote(
                R.tiles.at[1 - core], R.tile_box.at[0], R.small_send.at[0], R.small_recv.at[0], sibling
            )
        lead = own[: k - 1] + (1 - bits[k - 1],)
        return remote(
            R.tiles.at[(core,) + lead],
            R.tile_box.at[(k,) + lead],
            R.small_send.at[k],
            R.small_recv.at[k],
            partners[k - 1],
        )

    def small_event(k):
        small_move(k).wait()
        lead = own[:k]
        view = R.tiles.at[(core,) + lead]
        view[...] = view[...] + R.tile_box[(k,) + lead]
        if k < dims:
            small_move(k + 1).start()
        else:
            pltpu.make_async_copy(view, R.g_small, R.edge_sem.at[2]).start()

    for name in (N.vecs, N.og, N.y, N.g, N.w_down, N.gp, N.w_up, N.c, N.h, N.o, N.w_out, N.q, N.k, N.v, N.p, N.x, N.a):
        load(name, 1).start()
    grads[...] = jnp.zeros_like(grads)
    edge1_local = pltpu.make_async_copy(R.s_z, R.edge1.at[1], R.edge_sem.at[0])
    edge1_remote = remote(R.s_z, R.edge1.at[0], R.edge_send.at[0], R.edge_recv.at[0], sibling)
    edge0_local = pltpu.make_async_copy(R.b_y, R.edge0.at[0], R.edge_sem.at[1])
    edge0_remote = remote(R.b_y, R.edge0.at[1], R.edge_send.at[1], R.edge_recv.at[1], sibling)

    @pl.when(core == 0)
    def _():
        edge1_remote.start()

    @pl.when(core == 1)
    def _():
        edge1_local.start()

    def compute(v):
        layer, (kind, block) = unit_of(v)
        if v >= NU:
            finished(v - NU)
        if kind == DOWN:
            if block == 0:
                top(layer)
            grad_down(layer, v, block)
            if block == 1:
                feed_back(layer)
        elif kind == UP:
            grad_up(layer, v, block)
        elif kind == OUT:
            middle(layer)
            grad_out(layer, v)
            attention_back(layer)
        else:
            grad_qkv(layer, v, block)
            if block == 2:
                bottom(layer)

    events = [(v, 1, 0, v) for v in range(total)]
    for v in range(total):
        for k in range(steps(v) + 1):
            lag = SCATTER_LAGS[k] if k < len(SCATTER_LAGS) else SCATTER_LAGS[-1] + (k - len(SCATTER_LAGS) + 1) / 8
            events.append((v + lag, 0, -k, v))
    events = sorted(events)
    tail = 0
    for key, is_compute, k, v in events:
        if is_compute:
            compute(v)
            if v == total - 1:

                @pl.when(core == 0)
                def _():
                    edge0_local.start()

                @pl.when(core == 1)
                def _():
                    edge0_remote.start()

                spread()
                small_move(0).start()
                tail = 1
        else:
            event(v, -k)
            if tail and tail <= dims + 1:
                if tail > 1:
                    small_event(tail - 2)
                tail += 1
    for k in range(max(tail - 2, 0), dims + 1):
        small_event(k)
    for v in range(NU, total):
        finished(v)

    @pl.when(core == 0)
    def _():
        edge1_remote.wait_send()
        edge0_local.wait()
        edge0_remote.wait_recv()

    @pl.when(core == 1)
    def _():
        edge1_local.wait()
        edge1_remote.wait_recv()
        edge0_remote.wait_send()

    pltpu.make_async_copy(R.tiles.at[(core,) + own], R.g_small, R.edge_sem.at[2]).wait()
    for layer in range(2):

        @pl.when(core == layer)
        def _():
            for v in range((1 - layer) * NU, (2 - layer) * NU):
                for copy in final_remote(v):
                    copy.wait_recv()


def backward(left, out_grad, lengths, dims):
    rows = D // 2**dims
    bits = (2,) * dims
    outs = dict(
        g_qkv=((rows, 3 * D), LOW),
        g_out=((rows, D), LOW),
        g_up=((2, rows, FF // 2), LOW),
        g_down=((4 * rows, D), LOW),
        g_small=((16, 128), WIDE),
        edge0=((2, SEQ, D), WIDE),
        edge1=((2, SEQ, D), WIDE),
    )
    dma = pltpu.SemaphoreType.DMA
    total = 2 * NU
    vmem = lambda shape, dtype=LOW: pltpu.VMEM(shape, dtype)
    scratch = dict(
        vecs=vmem((2, 16, D), WIDE),
        grads=vmem((2, 16, D), WIDE),
        bias_grads=vmem((2, 8, FF // 2), WIDE),
        b_og=vmem((SEQ, D)),
        b_y=vmem((SEQ, D), WIDE),
        b_w_down=vmem((FF // 2, D)),
        b_w_wide=vmem((D, 3 * D)),
        b_w_out=vmem((D, D)),
        e=vmem((2, SEQ, D)),
        dc_part=vmem((2, SEQ, D)),
        dc=vmem((SEQ, D), WIDE),
        dy=vmem((SEQ, D), WIDE),
        dx=vmem((SEQ, D)),
        f=vmem((SEQ, D)),
        do=vmem((SEQ, D)),
        dp=vmem((SEQ, 3 * D)),
        tiles=vmem((2,) + bits + (16, 128), WIDE),
        tile_box=vmem((dims + 1,) + bits + (16, 128), WIDE),
        wide_stage=vmem((2,) + bits + (rows, 512)),
        wide_box=vmem((2,) + bits + (rows, 512)),
        down_stage=vmem((2,) + bits[:-1] + (4 * rows, 256)),
        down_box=vmem((2,) + bits[:-1] + (4 * rows, 256)),
        send=dma((total, dims + 1)),
        recv=dma((total, dims + 1)),
        credit=pltpu.SemaphoreType.REGULAR((NU, dims + 1)),
        out_sem=dma((total, 2)),
        end_send=dma((total, 2)),
        end_recv=dma((total, 2)),
        load_sem=dma((len(LOADS),)),
        act_send=dma((2, 2)),
        act_recv=dma((2, 2)),
        small_send=dma((dims + 1,)),
        small_recv=dma((dims + 1,)),
        edge_sem=dma((3,)),
        edge_send=dma((2,)),
        edge_recv=dma((2,)),
    )
    for name, (shape, dtype) in saved_shapes().items():
        scratch[B + name] = vmem(shape, dtype)
    for u, (kind, block) in enumerate(BACK):
        piece = (4 * rows, 256) if kind == DOWN else (rows, 512)
        lead = bits[:-1] if kind == DOWN else bits
        scratch[HELD + str(u)] = vmem(lead + piece)
        count = dims if kind in (QKV, OUT) else dims - 1
        for k in range(1, count + 1):
            scratch[box_name(u, k)] = vmem(lead[k:] + piece)
        if kind == UP:
            scratch[box_name(u, dims)] = vmem(piece)
    names = BACK_IN + list(outs) + list(scratch)

    def kernel(*refs):
        by_name = dict(zip(names, refs))
        extra = dict(
            qkv_flat=by_name[QKV].reshape(2, D, 3 * D),
            out_flat=by_name[OUT].reshape(2, D, D),
            up_flat=by_name[UP].reshape(2, D, FF // 2),
            down_flat=by_name[DOWN].reshape(2, FF // 2, D),
        )
        backward_kernel(dims, names + list(extra), *refs, *extra.values())

    anywhere = pl.BlockSpec(memory_space=pl.ANY)
    arguments = [left[n] for n in BACK_IN[:-2]] + [out_grad, lengths]
    results = pl.pallas_call(
        kernel,
        out_shape=[jax.ShapeDtypeStruct(s, t) for s, t in outs.values()],
        in_specs=[anywhere] * (len(arguments) - 1) + [pl.BlockSpec(memory_space=pltpu.SMEM)],
        out_specs=[anywhere] * len(outs),
        scratch_shapes=list(scratch.values()),
        compiler_params=pltpu.CompilerParams(collective_id=2, has_side_effects=True, vmem_limit_bytes=62 << 20),
        name="backward",
    )(*arguments)
    return SimpleNamespace(**dict(zip(outs, results)))


def unpack_share(small, count, here):
    vec_lanes, vec_group, bias_lanes, bias_group, bias_rows = small_layout(count)
    vectors = lax.dynamic_slice(small, (0, lax.rem(here, vec_group) * vec_lanes), (10, vec_lanes))
    start = lax.rem(lax.div(here, 2), bias_group) * bias_lanes if bias_group > 1 else 0
    bias = lax.dynamic_slice(small, (10, start), (bias_rows, bias_lanes // bias_rows))
    return vectors, bias.reshape(bias_lanes)


def per_device(dims, hidden_in, lengths, out_grad, w_qkv, w_out, w_up, w_down, vectors, up_bias):
    core, here = lax.axis_index(PIPE), lax.axis_index(DP)
    count = 2**dims
    rows = D // count
    left = forward_call(dims, here, core, hidden_in, lengths, w_qkv, w_out, w_up, w_down, vectors, up_bias)
    sums = backward(left, out_grad[:, 0], lengths[:, 0], dims)
    grad_vec, grad_bias = unpack_share(sums.g_small, count, here)
    edges = jnp.where(core == 0, sums.edge0, sums.edge1)
    up = sums.g_up.reshape(2, rows, count // 2, FF // count).transpose(1, 2, 0, 3).reshape(rows, FF)
    return (
        edges[None, :, None],
        sums.g_qkv.astype(WIDE)[None],
        sums.g_out.astype(WIDE)[None],
        up.astype(WIDE)[None],
        sums.g_down.astype(WIDE)[None],
        grad_vec[None],
        grad_bias[None],
    )


def solution(mesh):
    dims = (mesh.shape[DP] - 1).bit_length()
    weights = P(PIPE, DP, None)
    placed = (
        P(None, DP, None, None),
        P(None, DP),
        P(None, DP, None, None),
        weights,
        weights,
        weights,
        weights,
        P(PIPE, None, DP),
        P(PIPE, DP),
    )
    return jax.shard_map(
        functools.partial(per_device, dims),
        mesh=mesh,
        in_specs=placed,
        out_specs=(
            P(PIPE, None, DP, None, None),
            weights,
            weights,
            weights,
            weights,
            P(PIPE, None, DP),
            P(PIPE, DP),
        ),
        check_vma=False,
    )
```

```python
import functools
from types import SimpleNamespace

import jax
import jax.numpy as jnp
from jax import lax
from jax.experimental import pallas as pl
from jax.experimental.pallas import tpu as pltpu
from jax.sharding import PartitionSpec as P

D = 1024
HEADS = 16
HEAD_DIM = 64
FF = 4096
SEQ = 256
EPS = 1e-05
SCALE = HEAD_DIM**-0.5
MESH = pl.DeviceIdType.MESH
LOW = jnp.bfloat16
WIDE = jnp.float32
QKV, OUT, UP, DOWN = "qkv", "out", "up", "down"
FLAT = "_flat"
PIPE, DP = "pipe", "dp"
KINDS = [(QKV, 0), (QKV, 1), (QKV, 2), (OUT, 0), (UP, 0), (UP, 1), (DOWN, 0), (DOWN, 1)]
NU = len(KINDS)
GATHER_ORDERS = [
    (0, 1, 3, 2), (0, 1, 2, 3), (0, 1, 2, 3), (0, 1, 2, 3),
    (0, 1, 2), (2, 0, 1), (0, 1, 2), (0, 1, 2),
    (0, 1, 2, 3), (0, 1, 3, 2), (0, 1, 3, 2), (0, 1, 2, 3),
    (0, 1, 2), (2, 0, 1), (2, 0, 1), (0, 1, 2),
]
SCHEDULE = [
    2000, 2001, 0, 48, 1, 208, 209, 16, 49, 192, 80, 81, 32, 160, 2, 2002, 17, 64, 50, 112,
    2003, 2004, 18, 33, 3, 144, 128, 51, 113, 65, 34, 2005, 161, 176, 145, 19, 114, 4, 129, 15,
    96, 35, 52, 146, 66, 130, 3000, 3001, 20, 97, 82, 31, 177, 36, 67, 193, 3002, 115, 162, 47,
    3003, 63, 131, 3004, 98, 83, 3005, 3006, 3007, 178, 240, 127, 210, 224, 68, 79, 84, 147, 163, 99,
    179, 132, 95, 3008, 3009, 3010, 194, 143, 3011, 111, 225, 3012, 3013, 241, 3014, 3015, 180, 191, 3016, 3017,
    3018, 195, 148, 159, 211, 226, 3019, 164, 3020, 3030, 175, 3031, 3032, 3033, 3034, 3035, 3036, 3037, 196, 242,
    212, 207, 223, 3038, 3039, 227, 3040, 3041, 239, 243, 3042, 3043, 3044, 255, 3045, 3046, 3047, 3048, 3049, 3050,
]
GATHER_FIRST = -10
GATHER_LAGS = [3, 1, -1, -4]
GATHER_READY = 5


def axis_order(dims, u):
    kind, block = KINDS[u]
    if kind in (UP, DOWN):
        return tuple(range(dims - 1))
    return tuple((i + 2 * u) % dims for i in range(dims))


def gather_order(dims, v):
    return GATHER_ORDERS[v] if dims == 4 else axis_order(dims, v % NU)


def place(dims):
    core, here = lax.axis_index(PIPE), lax.axis_index(DP)
    bits = [lax.rem(lax.div(here, 2 ** (dims - 1 - i)), 2) for i in range(dims)]
    partners = [(core, here + (1 - 2 * bits[i]) * 2 ** (dims - 1 - i)) for i in range(dims)]
    return core, bits, partners, (1 - core, here)


def greet(everyone):
    barrier = pltpu.get_barrier_semaphore()
    for device in everyone:
        pl.semaphore_signal(barrier, inc=1, device_id=device, device_id_type=MESH)
    pl.semaphore_wait(barrier, len(everyone))


def remote(source, target, send, recv, device):
    return pltpu.make_async_remote_copy(
        src_ref=source, dst_ref=target, send_sem=send, recv_sem=recv, device_id=device, device_id_type=MESH
    )


def span(start, size):
    if isinstance(start, int):
        return pl.ds(start, size)
    return pl.ds(pl.multiple_of(start, size), size)


def for_each(count, body):
    lax.fori_loop(0, count, lambda i, carry: (body(i), carry)[1], 0, unroll=min(count, 4))


def unit_columns(u, column_half):
    kind, block = KINDS[u]
    if kind == DOWN:
        return span(block * 512 + column_half * 256, 256)
    return span(block * 1024 + column_half * 512, 512)


def norm_parts(values):
    center = values - jnp.mean(values, -1, keepdims=True)
    factor = lax.rsqrt(jnp.mean(center * center, -1, keepdims=True) + EPS)
    return (center * factor, factor)


def norm_back(grad_normed, normed, factor):
    return factor * (
        grad_normed
        - jnp.mean(grad_normed, -1, keepdims=True)
        - normed * jnp.mean(grad_normed * normed, -1, keepdims=True)
    )


def dot(left, right, dims=((1,), (0,))):
    return lax.dot_general(left, right, (dims, ((), ())), preferred_element_type=WIDE)


BY_ROWS = ((0,), (0,))
BY_COLUMNS = ((1,), (1,))


def small_layout(count):
    vec_lanes, bias_lanes = D // count, FF // count
    return vec_lanes, 128 // vec_lanes, bias_lanes, max(1, 128 // bias_lanes), max(1, bias_lanes // 128)


def head_masks():
    lanes = lax.broadcasted_iota(jnp.int32, (1, 128), 1)
    first = (lanes < HEAD_DIM).astype(WIDE)
    return first, 1.0 - first


def valid_rows(length, start, count):
    rows = lax.broadcasted_iota(jnp.int32, (count, 1), 0) + start
    return (rows < length).astype(WIDE)


FORWARD_IN = ["w_qkv", "w_out", "w_up", "w_down", "small", "hidden", "lengths"]
S = "s_"
SAVED = ["x", "a", "q", "k", "v", "o", "p", "h", "c", "g", "gp"]
LOADS = ["vecs", "og", "y", "w_down", "w_up", "w_qkv", "w_out"] + SAVED
N = SimpleNamespace(**{n: n for n in LOADS})


def saved_shapes():
    wide = lambda *s: (s, WIDE)
    low = lambda *s: (s, LOW)
    return dict(
        x=low(SEQ, D),
        a=low(SEQ, D),
        q=low(SEQ, D),
        k=low(SEQ, D),
        v=low(SEQ, D),
        o=low(SEQ, D),
        p=low(HEADS, SEQ, SEQ),
        h=wide(SEQ, D),
        c=low(2, SEQ, D),
        g=low(2, SEQ, FF // 2),
        gp=low(2, SEQ, FF // 2),
    )


def forward_kernel(dims, names, *refs):
    R = SimpleNamespace(**dict(zip(names, refs)))
    core, bits, partners, sibling = place(dims)
    own = tuple(bits)
    half = bits[-1]
    mate = partners[-1]
    greet([sibling] + partners)
    total = 2 * NU
    count = 2**dims
    saved = SimpleNamespace(**{n: [getattr(R, n + str(l)) for l in range(2)] for n in SAVED})

    def first_pairs(u, layer, column_half):
        kind, block = KINDS[u]
        cols = unit_columns(u, column_half)
        if kind == UP:
            return [
                (R.w_up.at[half, :, cols], R.up.at[(layer,) + own + (slice(None), cols)]),
                (R.w_up.at[1 - half, :, cols], R.stage.at[layer, :, cols]),
            ]
        if kind == DOWN:
            return [(R.w_down.at[:, cols], R.down.at[(layer,) + own[:-1] + (slice(None), cols)])]
        return [(getattr(R, "w_" + kind).at[:, cols], getattr(R, kind).at[(layer,) + own + (slice(None), cols)])]

    def first_local(u, layer):
        return [
            pltpu.make_async_copy(s, t, R.local_sem.at[u, i])
            for i, (s, t) in enumerate(first_pairs(u, layer, core))
        ]

    def first_remote(u, layer):
        return [
            remote(s, t, R.first_send.at[u, i], R.first_recv.at[u, i], sibling)
            for i, (s, t) in enumerate(first_pairs(u, layer, 1 - core))
        ]

    def chain(v):
        layer, u = v // NU, v % NU
        kind, block = KINDS[u]
        cols = unit_columns(u, core)
        moves = []
        if kind == UP:
            moves.append((R.stage.at[layer, :, cols], R.up.at[(layer,) + own + (slice(None), cols)], mate))
        order = gather_order(dims, v)
        known = dims - 1 if kind == DOWN else dims
        free = {dims - 1} if kind == UP else set()
        for k in range(len(order) + 1):
            gathered = set(order[:k]) | free
            where = tuple(slice(None) if i in gathered else bits[i] for i in range(known))
            ref = getattr(R, kind).at[(layer,) + where + (slice(None), cols)]
            moves.append((ref, ref, partners[order[k]] if k < len(order) else sibling))
        return [remote(s, t, R.send.at[v, i], R.recv.at[v, i], d) for i, (s, t, d) in enumerate(moves)]

    def small_step(k):
        where = tuple(slice(None) if i < k else bits[i] for i in range(dims))
        ref = R.small_all.at[(core,) + where]
        return remote(ref, ref, R.small_send.at[k], R.small_recv.at[k], partners[k] if k < dims else sibling)

    small_own = pltpu.make_async_copy(R.small, R.small_all.at[(core,) + own], R.io.at[0])
    small_own.start()
    load_x = pltpu.make_async_copy(R.hidden.at[core], saved.x[0], R.io.at[1])
    load_x.start()
    for layer in range(2):

        @pl.when(core == layer)
        def _():
            for u in range(NU):
                for copy in first_remote(u, layer) + first_local(u, layer):
                    copy.start()

    def arrive(v):
        layer, u = v // NU, v % NU

        @pl.when(core == layer)
        def _():
            for copy in first_local(u, layer):
                copy.wait()
            for copy in first_remote(u, layer):
                copy.wait_send()

        @pl.when(core != layer)
        def _():
            for copy in first_remote(u, layer):
                copy.wait_recv()

    length = R.lengths[core]
    vecs, biases = R.vecs, R.biases
    first_head, second_head = head_masks()

    def assemble():
        vec_lanes, vec_group, bias_lanes, bias_group, bias_rows = small_layout(count)
        small = R.small_all

        def shard(layer, d):
            return small[(layer,) + tuple((d >> (dims - 1 - i)) & 1 for i in range(dims))].astype(WIDE)

        def half_shard(layer, b):
            lead = tuple((b >> (dims - 2 - i)) & 1 for i in range(dims - 1))
            return small[(layer,) + lead + (half,)].astype(WIDE)

        for layer in range(2):
            for t in range(D // 128):
                vecs[layer, :, t * 128 : (t + 1) * 128] = sum(
                    shard(layer, d) for d in range(t * vec_group, (t + 1) * vec_group)
                )
            for t in range(count // 2 // bias_group):
                tile = sum(half_shard(layer, b) for b in range(t * bias_group, (t + 1) * bias_group))
                for i in range(bias_rows):
                    at = (t * bias_rows + i) * 128
                    biases[layer, 0:1, at : at + 128] = tile[10 + i : 11 + i, :]

    save_queue = []

    def save(name, layer):
        copy = pltpu.make_async_copy(
            getattr(saved, name)[layer], getattr(R, S + name).at[layer], R.save_sem.at[layer, SAVED.index(name)]
        )
        copy.start()
        save_queue.append(copy)

    def vec(layer, i, cols=slice(None)):
        return vecs[layer, i : i + 1, cols]

    def load_weight(v):
        layer, u = v // NU, v % NU
        kind, block = KINDS[u]
        if kind == DOWN:
            flat = R.down_flat.at[layer, :, pl.ds(block * 512, 512)]
            target = R.w_low.at[:, pl.ds(block * 512, 512)]
        else:
            flat = getattr(R, kind + FLAT).at[layer, :, pl.ds(block * 1024, 1024)]
            target = R.w_slots.at[u]
        return pltpu.make_async_copy(flat, target, R.weight_sem.at[u])

    def first_norm(layer):
        def rows(i):
            at = span(i * 32, 32)
            normed, unused = norm_parts(saved.x[layer][at, :].astype(WIDE))
            saved.a[layer][at, :] = (normed * vec(layer, 0) + vec(layer, 1)).astype(LOW)

        for_each(SEQ // 32, rows)
        save(N.x, layer)
        save(N.a, layer)

    def project(layer, block):
        target = (saved.q, saved.k, saved.v)[block][layer]
        weight = R.w_slots.at[block]

        def columns(n):
            at = span(n * 256, 256)
            values = dot(saved.a[layer][...], weight[:, at])
            if block == 0:
                values = (values + vec(layer, 2, at)).astype(LOW) * SCALE
            elif block == 2:
                values = values + vec(layer, 3, at)
            target[:, at] = values.astype(LOW)

        for_each(D // 256, columns)
        save((N.q, N.k, N.v)[block], layer)

    def attention(layer):
        key_ids = lax.broadcasted_iota(jnp.int32, (SEQ, SEQ), 0)
        query_ids = lax.broadcasted_iota(jnp.int32, (SEQ, SEQ), 1)
        blocked = jnp.where((key_ids <= query_ids) & (key_ids < length), 0.0, -1e30)

        def pair(n):
            at = span(n * 128, 128)
            query, key, value = (part[layer][:, at] for part in (saved.q, saved.k, saved.v))
            parts = []
            for i, mask in enumerate((first_head, second_head)):
                scores = dot(key, query * mask.astype(LOW), BY_COLUMNS) + blocked
                weights = jnp.exp(scores - jnp.max(scores, 0, keepdims=True))
                probs = (weights * (1.0 / jnp.sum(weights, 0, keepdims=True))).astype(LOW)
                saved.p[layer][2 * n + i] = probs
                parts.append(dot(probs, value, BY_ROWS) * mask)
            saved.o[layer][:, at] = (parts[0] + parts[1]).astype(LOW)

        for_each(HEADS // 2, pair)
        save(N.p, layer)
        save(N.o, layer)

    def send_c(layer):
        ref = saved.c[layer]
        return remote(ref.at[0], ref.at[1], R.act_send.at[layer, 0], R.act_recv.at[layer, 0], mate)

    def attend_out(layer):
        weight = R.w_slots.at[3]
        hidden = saved.h[layer]

        def columns(n):
            at = span(n * 256, 256)
            values = dot(saved.o[layer][...], weight[:, at])
            hidden[:, at] = saved.x[layer][:, at].astype(WIDE) + values + vec(layer, 4, at)

        for_each(D // 256, columns)

    def second_norm(layer):
        def rows(i):
            at = span(i * 32, 32)
            normed, unused = norm_parts(saved.h[layer][at, :])
            saved.c[layer][0, at, :] = (normed * vec(layer, 5) + vec(layer, 6)).astype(LOW)

        for_each(SEQ // 32, rows)
        save(N.h, layer)

    def feed_up(layer, block, who):
        weight = R.w_slots.at[4 + block]

        def columns(n):
            at = span(n * 256, 256)
            to = span(block * 1024 + n * 256, 256)
            value = dot(saved.c[layer][who], weight[:, at]) + biases[layer, 0:1, to]
            share = 0.5 + 0.5 * lax.erf(value * 0.7071067811865476)
            slope = share + value * (jnp.exp(value * value * -0.5) * 0.3989422804014327)
            saved.g[layer][who, :, to] = (value * share).astype(LOW)
            saved.gp[layer][who, :, to] = slope.astype(LOW)

        for_each(4, columns)
        if block == 1 and who == 1:
            save(N.g, layer)
            save(N.gp, layer)

    def send_part(layer, block):
        at = pl.ds(block * 512, 512)
        return remote(
            R.part.at[layer, 0, :, at],
            R.part.at[layer, 1, :, at],
            R.act_send.at[layer, 1 + block],
            R.act_recv.at[layer, 1 + block],
            mate,
        )

    def down_theirs(layer, block):
        def columns(n):
            at = span(block * 512 + n * 256, 256)
            R.part[layer, 0, :, at] = dot(saved.g[layer][1], R.w_low[:, at]).astype(LOW)

        for_each(2, columns)

    def down_mine(layer, block):
        def columns(n):
            at = span(block * 512 + n * 256, 256)
            values = dot(saved.g[layer][0], R.w_low[:, at])
            R.y[:, at] = saved.h[layer][:, at] + values + vec(layer, 7, at)

        for_each(2, columns)

    def end(layer):
        def rows(i):
            at = span(i * 32, 32)
            valid = valid_rows(length, i * 32, 32)
            values = R.y[at, :] + R.part[layer, 1, at, :].astype(WIDE)
            if layer == 0:
                saved.x[1][at, :] = (values * valid).astype(LOW)
            else:
                R.y[at, :] = values
                normed, unused = norm_parts(values)
                R.z[at, :] = (normed * vec(1, 8) + vec(1, 9)) * valid

        for_each(SEQ // 32, rows)

    def weight(layer, u):
        load_weight(layer * NU + u).wait()

    def wait_parts(layer):
        for block in range(2):
            send_part(layer, block).wait()

    def wait_c(layer):
        send_c(layer).wait()
        save(N.c, layer)

    pieces = [
        (first_norm, None),
        (lambda layer: project(layer, 0), 0),
        (lambda layer: project(layer, 1), 1),
        (lambda layer: project(layer, 2), 2),
        (attention, None),
        (attend_out, 3),
        (second_norm, None),
        (lambda layer: send_c(layer).start(), None),
        (lambda layer: feed_up(layer, 0, 0), 4),
        (lambda layer: feed_up(layer, 1, 0), 5),
        (wait_c, None),
        (lambda layer: feed_up(layer, 0, 1), None),
        (lambda layer: feed_up(layer, 1, 1), None),
        (lambda layer: down_theirs(layer, 0), 6),
        (lambda layer: send_part(layer, 0).start(), None),
        (lambda layer: down_mine(layer, 0), None),
        (lambda layer: down_theirs(layer, 1), 7),
        (lambda layer: send_part(layer, 1).start(), None),
        (lambda layer: down_mine(layer, 1), None),
        (wait_parts, None),
        (end, None),
    ]

    chains = [chain(v) for v in range(total)]

    def plain_schedule():
        moves = []
        for v in range(total):
            for i in range(len(chains[v])):
                left = len(chains[v]) - 1 - i
                lag = GATHER_LAGS[left] if left < len(GATHER_LAGS) else GATHER_LAGS[-1] - left + len(GATHER_LAGS) - 1
                moves.append((v + (lag if i else min(GATHER_FIRST, lag)), -i, v))
            moves.append((v + GATHER_READY, -99, v))
        codes = [16 * v - i if i > -99 else 16 * v + 15 for unused, i, v in sorted(moves)]
        for k in range(dims + 2):
            codes.insert(6 * k, 2000 + k)
        result, done = [], set()
        jobs = [(layer, w) for layer in range(2) for w in range(len(pieces))]
        for code in codes:
            result.append(code)
            done.add(code)
            while jobs and 2000 + dims + 1 in done:
                layer, w = jobs[0]
                u = pieces[w][1]
                if u is not None and 16 * (layer * NU + u) + 15 not in done:
                    break
                result.append(3000 + 30 * layer + w)
                jobs.pop(0)
        return result

    small_own.wait()
    load_x.wait()
    for code in SCHEDULE if dims == 4 and SCHEDULE else plain_schedule():
        if code >= 3000:
            layer, w = (code - 3000) // 30, (code - 3000) % 30
            if pieces[w][1] is not None:
                weight(layer, pieces[w][1])
            pieces[w][0](layer)
        elif code >= 2000:
            k = code - 2000
            if k > 0:
                small_step(k - 1).wait()
            if k <= dims:
                small_step(k).start()
            else:
                assemble()
        elif code % 16 == 15:
            v = code // 16
            chains[v][-1].wait()
            load_weight(v).start()
        else:
            v, i = code // 16, code % 16
            if i == 0:
                arrive(v)
            else:
                chains[v][i - 1].wait()
            chains[v][i].start()

    last = [(R.y, R.s_y, 0), (R.z, R.s_z, 1), (R.vecs, R.s_vecs, 2)]
    for source, target, i in last:
        pltpu.make_async_copy(source, target, R.last_sem.at[i]).start()
    for copy in save_queue:
        copy.wait()
    for source, target, i in last:
        pltpu.make_async_copy(source, target, R.last_sem.at[i]).wait()


def forward(shards, small, hidden, lengths, dims):
    rows = D // 2**dims
    bits = (2,) * dims
    outs = dict(
        qkv=((2,) + bits + (rows, 3 * D), LOW),
        out=((2,) + bits + (rows, D), LOW),
        up=((2,) + bits + (rows, FF // 2), LOW),
        down=((2,) + bits[:-1] + (4 * rows, D), LOW),
        stage=((2, rows, FF // 2), LOW),
    )
    for name, (shape, dtype) in saved_shapes().items():
        outs[S + name] = ((2,) + shape, dtype)
    outs[S + N.y] = ((SEQ, D), WIDE)
    outs[S + "z"] = ((SEQ, D), WIDE)
    outs[S + N.vecs] = ((2, 16, D), WIDE)
    dma = pltpu.SemaphoreType.DMA
    total = 2 * NU
    scratch = dict(
        small_all=pltpu.VMEM((2,) + bits + (16, 128), LOW),
        vecs=pltpu.VMEM((2, 16, D), WIDE),
        biases=pltpu.VMEM((2, 8, FF // 2), WIDE),
        w_slots=pltpu.VMEM((6, D, D), LOW),
        w_low=pltpu.VMEM((FF // 2, D), LOW),
        part=pltpu.VMEM((2, 2, SEQ, D), LOW),
        y=pltpu.VMEM((SEQ, D), WIDE),
        z=pltpu.VMEM((SEQ, D), WIDE),
        local_sem=dma((NU, 2)),
        first_send=dma((NU, 2)),
        first_recv=dma((NU, 2)),
        send=dma((total, dims + 2)),
        recv=dma((total, dims + 2)),
        small_send=dma((dims + 1,)),
        small_recv=dma((dims + 1,)),
        io=dma((2,)),
        save_sem=dma((2, len(SAVED))),
        weight_sem=dma((NU,)),
        act_send=dma((2, 3)),
        act_recv=dma((2, 3)),
        last_sem=dma((3,)),
    )
    for name, (shape, dtype) in saved_shapes().items():
        for layer in range(2):
            scratch[name + str(layer)] = pltpu.VMEM(shape, dtype)
    names = FORWARD_IN + list(outs) + list(scratch)

    def kernel(*refs):
        by_name = dict(zip(names, refs))
        extra = dict(
            qkv_flat=by_name[QKV].reshape(2, D, 3 * D),
            out_flat=by_name[OUT].reshape(2, D, D),
            up_flat=by_name[UP].reshape(2, D, FF // 2),
            down_flat=by_name[DOWN].reshape(2, FF // 2, D),
        )
        forward_kernel(dims, names + list(extra), *refs, *extra.values())

    anywhere = pl.BlockSpec(memory_space=pl.ANY)
    results = pl.pallas_call(
        kernel,
        out_shape=[jax.ShapeDtypeStruct(s, t) for s, t in outs.values()],
        in_specs=[anywhere] * 6 + [pl.BlockSpec(memory_space=pltpu.SMEM)],
        out_specs=[anywhere] * len(outs),
        scratch_shapes=list(scratch.values()),
        compiler_params=pltpu.CompilerParams(collective_id=1, has_side_effects=True, vmem_limit_bytes=60 << 20),
        name="forward",
    )(*shards, small, hidden, lengths)
    return dict(zip(outs, results))


def pack_small(vectors, up_bias, count, here):
    vec_lanes, vec_group, bias_lanes, bias_group, bias_rows = small_layout(count)
    packed = jnp.zeros((16, 128), vectors.dtype)
    packed = lax.dynamic_update_slice(packed, vectors, (0, lax.rem(here, vec_group) * vec_lanes))
    wide = up_bias.reshape(bias_rows, bias_lanes // bias_rows)
    at = lax.rem(lax.div(here, 2), bias_group) * bias_lanes if bias_group > 1 else 0
    return lax.dynamic_update_slice(packed, wide, (10, at))


def forward_call(dims, here, core, hidden_in, lengths, w_qkv, w_out, w_up, w_down, vectors, up_bias):
    count = 2**dims
    rows = D // count
    small = pack_small(vectors[0], up_bias[0], count, here)
    halves = w_up[0].reshape(rows, count // 2, 2, FF // count).transpose(2, 0, 1, 3).reshape(2, rows, FF // 2)
    return forward((w_qkv[0], w_out[0], halves, w_down[0]), small, hidden_in[:, 0], lengths[:, 0], dims)
BACK = [(DOWN, 0), (DOWN, 1), (UP, 0), (UP, 1), (OUT, 0), (QKV, 0), (QKV, 1), (QKV, 2)]
SCATTER_LAGS = [1, 3, 4, 5, 6]
BACK_ORDERS = [
    (0, 1, 2, 3), (0, 1, 3, 2), (0, 1, 2, 3), (0, 1, 2, 3),
    (0, 1, 2), (0, 1, 2), (0, 1, 2), (2, 0, 1),
]
BACK_SCHEDULE = [
    3000, 3001, 3002, 3003, 3004, 3005, 3006, 3007, 0, 3008, 3009, 3010, 16, 32, 3011, 3012, 3013, 3014, 48, 1,
    3015, 64, 17, 3016, 3017, 3018, 2, 80, 3019, 96, 33, 3020, 3021, 3030, 3031, 49, 65, 34, 81, 97,
    3032, 18, 66, 50, 112, 3, 3033, 3034, 3035, 82, 3036, 128, 35, 19, 98, 51, 3037, 67, 3038, 83,
    144, 99, 3039, 113, 36, 3040, 52, 68, 160, 114, 129, 3041, 3042, 3043, 3044, 176, 3045, 115, 192, 161,
    84, 130, 3046, 3047, 100, 116, 177, 208, 193, 3048, 145, 3049, 224, 3050, 240, 194, 209, 131, 178, 3051,
    4000, 225, 146, 2000, 162, 241, 210, 179, 2001, 195, 163, 226, 164, 211, 2002, 242, 196, 227, 2003, 243,
    147, 180, 2004, 228, 212, 244,
]
HELD, B, TILE = "held", "b_", "tile"
BACK_WEIGHTS = [QKV, OUT, UP, DOWN]
BACK_IN = BACK_WEIGHTS + [S + n for n in SAVED + ["y", "z", "vecs"]] + ["out_grad", "lengths"]


def back_order(dims, u):
    return BACK_ORDERS[u] if dims == 4 else axis_order(dims, u)


def box_name(u, k):
    return "box%d_%d" % (u, k)


def backward_kernel(dims, names, *refs):
    R = SimpleNamespace(**dict(zip(names, refs)))
    core, bits, partners, sibling = place(dims)
    own = tuple(bits)
    half = bits[-1]
    mate = partners[-1]
    greet([sibling] + partners)
    total = 2 * NU
    count = 2**dims
    length = R.lengths[core]
    vecs, grads = R.vecs, R.grads
    first_head, second_head = head_masks()

    def load(name, layer):
        if name == N.y:
            source = R.s_y
        elif name == N.og:
            source = R.out_grad.at[core]
        elif name == N.vecs:
            source = R.s_vecs
        elif name in (N.w_down, N.w_up, N.w_qkv, N.w_out):
            source = getattr(R, name[2:] + FLAT).at[layer]
        else:
            source = getattr(R, S + name).at[layer]
        if name == N.vecs:
            target = vecs
        elif name == N.w_up:
            target = R.b_w_wide.at[:, pl.ds(0, FF // 2)]
        elif name == N.w_qkv:
            target = R.b_w_wide
        else:
            target = getattr(R, B + name)
        return pltpu.make_async_copy(source, target, R.load_sem.at[LOADS.index(name)])

    def need(layer, *which):
        for name in which:
            load(name, layer).wait()

    def again(layer, *which):
        if layer == 1:
            for name in which:
                load(name, 0).start()

    def unit_of(v):
        return 1 - v // NU, BACK[v % NU]

    def columns_of(v, column_half):
        kind, block = BACK[v % NU]
        if kind == DOWN:
            return span(block * 512 + column_half * 256, 256)
        return span(block * 1024 + column_half * 512, 512)

    def order_of(v):
        return tuple(reversed(back_order(dims, KINDS.index(BACK[v % NU]))))

    def held(v):
        return getattr(R, HELD + str(v % NU))

    def box(v, k):
        if k == 0:
            kind, block = BACK[v % NU]
            return (R.down_box if kind == DOWN else R.wide_box).at[v % 2]
        return getattr(R, box_name(v % NU, k))

    def stage(v):
        kind, block = BACK[v % NU]
        return (R.down_stage if kind == DOWN else R.wide_stage).at[v % 2]

    def is_up(v):
        return BACK[v % NU][0] == UP

    def steps(v):
        return len(order_of(v)) + (1 if is_up(v) else 0)

    def where(v, k, away):
        order = order_of(v)
        place_of = []
        for i in range(dims - 1 if BACK[v % NU][0] == DOWN else dims):
            if i in order[: max(k - 1, 0)]:
                place_of.append(bits[i])
            elif 0 < k <= len(order) and i == order[k - 1]:
                place_of.append(1 - bits[i] if away else bits[i])
            elif k > len(order) and i == dims - 1:
                place_of.append(1 - half if away else half)
            elif k > len(order):
                place_of.append(bits[i])
            else:
                place_of.append(slice(None))
        return tuple(place_of)

    def device_of(v, k):
        if k == 0:
            return sibling
        return partners[order_of(v)[k - 1]] if k <= len(order_of(v)) else mate

    def move(v, k):
        source = stage(v) if k == 0 else held(v).at[where(v, k, True)]
        return remote(source, box(v, k), R.send.at[v, k], R.recv.at[v, k], device_of(v, k))

    def earlier(v, k):
        if k > 0 or BACK[v % NU][0] == DOWN:
            return v - NU if v >= NU else None
        wide = [w for w in range(total) if BACK[w % NU][0] != DOWN and w % 2 == v % 2 and w < v]
        return wide[-1] if wide else None

    def later(v, k):
        return any(earlier(w, k) == v for w in range(v + 1, total))

    def begin(v, k):
        if earlier(v, k) is not None:
            pl.semaphore_wait(R.credit.at[v % NU, k], 1)
        move(v, k).start()

    def consumed(v, k):
        for w in range(v + 1, total):
            if earlier(w, k) == v:
                pl.semaphore_signal(
                    R.credit.at[w % NU, k], inc=1, device_id=device_of(v, k), device_id_type=MESH
                )

    def finals(v):
        kind, block = BACK[v % NU]
        cols = columns_of(v, core)
        if kind == UP:
            return [
                (held(v).at[own], R.g_up.at[half, :, cols]),
                (box(v, dims), R.g_up.at[1 - half, :, cols]),
            ]
        if kind == DOWN:
            return [(held(v).at[own[:-1]], R.g_down.at[:, cols])]
        return [(held(v).at[own], getattr(R, "g_" + kind).at[:, cols])]

    def final_local(v):
        return [
            pltpu.make_async_copy(s, t, R.out_sem.at[v, i]) for i, (s, t) in enumerate(finals(v))
        ]

    def final_remote(v):
        return [
            remote(s, t, R.end_send.at[v, i], R.end_recv.at[v, i], sibling)
            for i, (s, t) in enumerate(finals(v))
        ]

    def finish(v):
        @pl.when(core == unit_of(v)[0])
        def _():
            for copy in final_local(v):
                copy.start()

        @pl.when(core != unit_of(v)[0])
        def _():
            for copy in final_remote(v):
                copy.start()

    def finished(v):
        @pl.when(core == unit_of(v)[0])
        def _():
            for copy in final_local(v):
                copy.wait()

        @pl.when(core != unit_of(v)[0])
        def _():
            for copy in final_remote(v):
                copy.wait_send()
        if is_up(v):
            consumed(v, dims)

    def event(v, k):
        move(v, k).wait()
        if not (is_up(v) and k == steps(v)):
            view = held(v).at[where(v, k, False)]
            view[...] = view[...] + box(v, k)[...]
            consumed(v, k)
        if k < steps(v):
            begin(v, k + 1)
        else:
            finish(v)

    def vec(layer, i):
        return vecs[layer, i : i + 1, :]

    def collect(layer, i, values):
        grads[layer, i : i + 1, :] = grads[layer, i : i + 1, :] + jnp.sum(values, 0, keepdims=True)

    def send_e(layer):
        ref = R.e.at[layer]
        return remote(ref.at[0], ref.at[1], R.act_send.at[layer, 0], R.act_recv.at[layer, 0], mate)

    def send_dc(layer):
        ref = R.dc_part
        return remote(ref.at[0], ref.at[1], R.act_send.at[layer, 1], R.act_recv.at[layer, 1], mate)

    def top(layer):
        if layer == 1:
            need(1, N.vecs, N.og, N.y)

        def rows(i):
            at = span(i * 32, 32)
            valid = valid_rows(length, i * 32, 32)
            if layer == 1:
                grad_z = R.b_og[at, :].astype(WIDE) * valid
                normed, factor = norm_parts(R.b_y[at, :])
                collect(1, 8, grad_z * normed)
                collect(1, 9, grad_z)
                grad_y = norm_back(grad_z * vec(1, 8), normed, factor)
            else:
                grad_y = R.dx[at, :].astype(WIDE) * valid
            R.dy[at, :] = grad_y
            branch = grad_y.astype(LOW)
            R.e[layer, 0, at, :] = branch
            collect(layer, 7, branch.astype(WIDE))

        for_each(SEQ // 32, rows)

    def produce(v, body, quarter_shape):
        for target, column_half in ((stage(v), 1 - core), (held(v), core)):
            cols = columns_of(v, column_half)

            def quarter(i):
                target[lax.div(i, 2), lax.rem(i, 2)] = body(i, cols).astype(LOW).reshape(quarter_shape)

            for_each(4, quarter)
            if column_half is not core:
                begin(v, 0)

    def pair_rows(ref, cols):
        values = ref[:, :, cols]
        return values.reshape(2 * SEQ, values.shape[-1])

    inner = (2,) * (dims - 2) + (D // count, 512)
    down_inner = (2,) * (dims - 3) + (FF // count, 256)

    def grad_down(layer, v, block):
        if block == 0:
            need(layer, N.g)
        produce(
            v,
            lambda i, cols: dot(pair_rows(R.b_g, span(i * 512, 512)), pair_rows(R.e.at[layer], cols), BY_ROWS),
            down_inner,
        )
        if block == 1:
            again(layer, N.g)

    def feed_hidden(layer, who):
        if who == 0:
            need(layer, N.w_down, N.gp)

        def hidden(n):
            at = span(n * 256, 256)
            grad_act = dot(R.e[layer, who], R.b_w_down[at, :], BY_COLUMNS)
            grad_upper = (grad_act * R.b_gp[who, :, at].astype(WIDE)).astype(LOW)
            R.b_gp[who, :, at] = grad_upper
            sums = jnp.sum(grad_upper.astype(WIDE), 0, keepdims=True)
            R.bias_grads[layer, 0:1, at] = sums if who == 0 else R.bias_grads[layer, 0:1, at] + sums

        for_each(FF // 2 // 256, hidden)
        if who == 1:
            again(layer, N.w_down)

    def feed_theirs(layer):
        need(layer, N.w_up)

        def theirs(n):
            at = span(n * 256, 256)
            R.dc_part[0, :, at] = dot(R.b_gp[1], R.b_w_wide[at, pl.ds(0, FF // 2)], BY_COLUMNS).astype(LOW)

        for_each(D // 256, theirs)

    def feed_mine(layer):
        def mine(n):
            at = span(n * 256, 256)
            R.dc[:, at] = dot(R.b_gp[0], R.b_w_wide[at, pl.ds(0, FF // 2)], BY_COLUMNS)

        for_each(D // 256, mine)
        load(N.w_qkv, layer).start()

    def grad_up(layer, v, block):
        if block == 0:
            need(layer, N.c)

        def body(i, cols):
            return dot(pair_rows(R.b_c, span(i * 256, 256)), pair_rows(R.b_gp, cols), BY_ROWS)

        produce(v, body, inner)
        if block == 1:
            again(layer, N.c, N.gp)

    def middle(layer):
        need(layer, N.h)

        def rows(i):
            at = span(i * 32, 32)
            grad_in = R.dc[at, :] + R.dc_part[1, at, :].astype(WIDE)
            normed, factor = norm_parts(R.b_h[at, :])
            collect(layer, 5, grad_in * normed)
            collect(layer, 6, grad_in)
            grad_hidden = R.dy[at, :] + norm_back(grad_in * vec(layer, 5), normed, factor)
            R.dy[at, :] = grad_hidden
            branch = grad_hidden.astype(LOW)
            R.f[at, :] = branch
            collect(layer, 4, branch.astype(WIDE))

        for_each(SEQ // 32, rows)
        again(layer, N.h)

    def grad_out(layer, v):
        need(layer, N.o)
        produce(v, lambda i, cols: dot(R.b_o[:, span(i * 256, 256)], R.f[:, cols], BY_ROWS), inner)
        again(layer, N.o)

    def grad_mixed(layer):
        need(layer, N.w_out)

        def columns(n):
            at = span(n * 256, 256)
            R.do[:, at] = dot(R.f[...], R.b_w_out[at, :], BY_COLUMNS).astype(LOW)

        for_each(D // 256, columns)
        again(layer, N.w_out)

    def attention_back(layer):
        need(layer, N.q, N.k, N.v, N.p)

        def pair(n):
            at = span(n * 128, 128)
            query, key, value, grad_o = R.b_q[:, at], R.b_k[:, at], R.b_v[:, at], R.do[:, at]
            sums = [0.0, 0.0, 0.0]
            for i, mask in enumerate((first_head.astype(LOW), second_head.astype(LOW))):
                probs = R.b_p[2 * n + i]
                grad_head = grad_o * mask
                wide = probs.astype(WIDE)
                grad_probs = dot(value, grad_head, BY_COLUMNS)
                shift = jnp.sum(grad_probs * wide, 0, keepdims=True)
                grad_scores = (wide * (grad_probs - shift)).astype(LOW)
                sums[0] += dot(grad_scores, key * mask, BY_ROWS)
                sums[1] += dot(grad_scores, query * mask)
                sums[2] += dot(probs, grad_head)
            sums[0] = sums[0] * SCALE
            for j in range(3):
                low = sums[j].astype(LOW)
                R.dp[:, pl.ds(pl.multiple_of(n * 128 + j * D, 128), 128)] = low
                if j != 1:
                    row = 2 if j == 0 else 3
                    grads[layer, row : row + 1, at] = jnp.sum(low.astype(WIDE), 0, keepdims=True)

        for_each(HEADS // 2, pair)
        again(layer, N.q, N.k, N.v, N.p)

    def grad_qkv(layer, v, block):
        if block == 0:
            need(layer, N.a)
        produce(v, lambda i, cols: dot(R.b_a[:, span(i * 256, 256)], R.dp[:, cols], BY_ROWS), inner)
        if block == 2:
            again(layer, N.a)

    def grad_attn_in(layer):
        need(layer, N.w_qkv)

        def columns(n):
            at = span(n * 256, 256)
            R.dc[:, at] = dot(R.dp[...], R.b_w_wide[at, :], BY_COLUMNS)

        for_each(D // 256, columns)
        again(layer, N.w_up)

    def bottom(layer):
        need(layer, N.x)

        def rows(i):
            at = span(i * 32, 32)
            grad_in = R.dc[at, :]
            normed, factor = norm_parts(R.b_x[at, :].astype(WIDE))
            collect(layer, 0, grad_in * normed)
            collect(layer, 1, grad_in)
            grad_x = R.dy[at, :] + norm_back(grad_in * vec(layer, 0), normed, factor)
            if layer == 1:
                R.dx[at, :] = grad_x.astype(LOW)
            else:
                R.b_y[at, :] = grad_x

        for_each(SEQ // 32, rows)
        again(layer, N.x)

    def spread():
        vec_lanes, vec_group, bias_lanes, bias_group, bias_rows = small_layout(count)
        tiles = R.tiles
        tiles[...] = jnp.zeros_like(tiles)
        for layer in range(2):
            for d in range(count):
                lead = tuple((d >> (dims - 1 - i)) & 1 for i in range(dims))
                t = d // vec_group
                tiles[(layer,) + lead + (slice(0, 10),)] = grads[layer, 0:10, t * 128 : (t + 1) * 128]
            for b in range(count // 2):
                lead = tuple((b >> (dims - 2 - i)) & 1 for i in range(dims - 1))
                for i in range(bias_rows):
                    at = (b // bias_group * bias_rows + i) * 128
                    tiles[(layer,) + lead + (half, slice(10 + i, 11 + i))] = R.bias_grads[layer, 0:1, at : at + 128]

    def tile_box(k):
        return getattr(R, TILE + str(k))

    def small_move(k):
        if k == 0:
            return remote(
                R.tiles.at[1 - core], tile_box(0), R.small_send.at[0], R.small_recv.at[0], sibling
            )
        lead = own[: k - 1] + (1 - bits[k - 1],)
        return remote(
            R.tiles.at[(core,) + lead],
            tile_box(k),
            R.small_send.at[k],
            R.small_recv.at[k],
            partners[k - 1],
        )

    def small_event(k):
        small_move(k).wait()
        lead = own[:k]
        view = R.tiles.at[(core,) + lead]
        view[...] = view[...] + tile_box(k)[...]
        if k < dims:
            small_move(k + 1).start()
        else:
            pltpu.make_async_copy(view, R.g_small, R.edge_sem.at[2]).start()

    for name in (N.vecs, N.og, N.y, N.g, N.w_down, N.gp, N.w_up, N.c, N.h, N.o, N.w_out, N.q, N.k, N.v, N.p, N.x, N.a):
        load(name, 1).start()
    grads[...] = jnp.zeros_like(grads)
    edge_local = [pltpu.make_async_copy(ref, R.edges.at[core], R.edge_sem.at[0]) for ref in (R.b_y, R.s_z)]
    edge_remote = [
        remote(ref, R.edges.at[core], R.edge_send.at[0], R.edge_recv.at[0], sibling) for ref in (R.s_z, R.b_y)
    ]

    @pl.when(core == 0)
    def _():
        edge_remote[0].start()

    @pl.when(core == 1)
    def _():
        edge_local[1].start()

    def last(layer):
        @pl.when(core == 0)
        def _():
            edge_local[0].start()

        @pl.when(core == 1)
        def _():
            edge_remote[1].start()

        spread()
        small_move(0).start()

    def unit(layer, u):
        return (1 - layer) * NU + u

    pieces = [
        (top, None),
        (lambda layer: send_e(layer).start(), None),
        (lambda layer: feed_hidden(layer, 0), None),
        (lambda layer: send_e(layer).wait(), None),
        (lambda layer: grad_down(layer, unit(layer, 0), 0), 0),
        (lambda layer: feed_hidden(layer, 1), None),
        (feed_theirs, None),
        (lambda layer: send_dc(layer).start(), None),
        (lambda layer: grad_down(layer, unit(layer, 1), 1), 1),
        (feed_mine, None),
        (lambda layer: grad_up(layer, unit(layer, 2), 0), 2),
        (lambda layer: grad_up(layer, unit(layer, 3), 1), 3),
        (lambda layer: send_dc(layer).wait(), None),
        (middle, None),
        (lambda layer: grad_out(layer, unit(layer, 4)), 4),
        (grad_mixed, None),
        (attention_back, None),
        (lambda layer: grad_qkv(layer, unit(layer, 5), 0), 5),
        (lambda layer: grad_qkv(layer, unit(layer, 6), 1), 6),
        (lambda layer: grad_qkv(layer, unit(layer, 7), 2), 7),
        (grad_attn_in, None),
        (bottom, None),
    ]

    def plain_schedule():
        timed = []
        for v in range(total):
            for k in range(steps(v) + 1):
                lag = SCATTER_LAGS[k] if k < len(SCATTER_LAGS) else SCATTER_LAGS[-1] + (k - len(SCATTER_LAGS) + 1) / 8
                timed.append((v + lag, 0, -k, v))
            timed.append((v, 1, 0, v))
        result = []
        for turn in range(2):
            at = -1.0
            for w, (unused, u) in enumerate(pieces):
                at = max(at + 0.01, turn * NU + (u or 0))
                timed.append((at, 1, w, (turn, w)))
        codes = []
        for key, is_compute, k, v in sorted(timed, key=lambda item: item[:3]):
            if not is_compute:
                codes.append(16 * v - k)
            elif isinstance(v, tuple):
                codes.append(3000 + 30 * v[0] + v[1])
        codes.append(4000)
        return codes + [2000 + k for k in range(dims + 1)]

    for code in BACK_SCHEDULE if dims == 4 and BACK_SCHEDULE else plain_schedule():
        if code >= 4000:
            last(0)
        elif code >= 3000:
            turn, w = (code - 3000) // 30, (code - 3000) % 30
            u = pieces[w][1]
            if turn == 1 and u is not None:
                finished(u)
            pieces[w][0](1 - turn)
        elif code >= 2000:
            small_event(code - 2000)
        else:
            event(code // 16, code % 16)
    for v in range(NU, total):
        finished(v)

    @pl.when(core == 0)
    def _():
        edge_remote[0].wait_send()
        edge_local[0].wait()

    @pl.when(core == 1)
    def _():
        edge_local[1].wait()
        edge_remote[1].wait_send()

    edge_remote[0].wait_recv()
    pltpu.make_async_copy(R.tiles.at[(core,) + own], R.g_small, R.edge_sem.at[2]).wait()
    for layer in range(2):

        @pl.when(core == layer)
        def _():
            for v in range((1 - layer) * NU, (2 - layer) * NU):
                for copy in final_remote(v):
                    copy.wait_recv()


def backward(left, out_grad, lengths, dims):
    rows = D // 2**dims
    bits = (2,) * dims
    outs = dict(
        g_qkv=((rows, 3 * D), LOW),
        g_out=((rows, D), LOW),
        g_up=((2, rows, FF // 2), LOW),
        g_down=((4 * rows, D), LOW),
        g_small=((16, 128), WIDE),
        edges=((2, SEQ, D), WIDE),
    )
    dma = pltpu.SemaphoreType.DMA
    total = 2 * NU
    vmem = lambda shape, dtype=LOW: pltpu.VMEM(shape, dtype)
    scratch = dict(
        vecs=vmem((2, 16, D), WIDE),
        grads=vmem((2, 16, D), WIDE),
        bias_grads=vmem((2, 8, FF // 2), WIDE),
        b_og=vmem((SEQ, D)),
        b_y=vmem((SEQ, D), WIDE),
        b_w_down=vmem((FF // 2, D)),
        b_w_wide=vmem((D, 3 * D)),
        b_w_out=vmem((D, D)),
        e=vmem((2, 2, SEQ, D)),
        dc_part=vmem((2, SEQ, D)),
        dc=vmem((SEQ, D), WIDE),
        dy=vmem((SEQ, D), WIDE),
        dx=vmem((SEQ, D)),
        f=vmem((SEQ, D)),
        do=vmem((SEQ, D)),
        dp=vmem((SEQ, 3 * D)),
        tiles=vmem((2,) + bits + (16, 128), WIDE),
        wide_stage=vmem((2,) + bits + (rows, 512)),
        wide_box=vmem((2,) + bits + (rows, 512)),
        down_stage=vmem((2,) + bits[:-1] + (4 * rows, 256)),
        down_box=vmem((2,) + bits[:-1] + (4 * rows, 256)),
        send=dma((total, dims + 1)),
        recv=dma((total, dims + 1)),
        credit=pltpu.SemaphoreType.REGULAR((NU, dims + 1)),
        out_sem=dma((total, 2)),
        end_send=dma((total, 2)),
        end_recv=dma((total, 2)),
        load_sem=dma((len(LOADS),)),
        act_send=dma((2, 2)),
        act_recv=dma((2, 2)),
        small_send=dma((dims + 1,)),
        small_recv=dma((dims + 1,)),
        edge_sem=dma((3,)),
        edge_send=dma((1,)),
        edge_recv=dma((1,)),
    )
    for k in range(dims + 1):
        scratch[TILE + str(k)] = vmem(bits[k:] + (16, 128), WIDE)
    for name, (shape, dtype) in saved_shapes().items():
        scratch[B + name] = vmem(shape, dtype)
    for u, (kind, block) in enumerate(BACK):
        piece = (4 * rows, 256) if kind == DOWN else (rows, 512)
        lead = bits[:-1] if kind == DOWN else bits
        scratch[HELD + str(u)] = vmem(lead + piece)
        count = dims if kind in (QKV, OUT) else dims - 1
        for k in range(1, count + 1):
            scratch[box_name(u, k)] = vmem(lead[k:] + piece)
        if kind == UP:
            scratch[box_name(u, dims)] = vmem(piece)
    names = BACK_IN + list(outs) + list(scratch)

    def kernel(*refs):
        by_name = dict(zip(names, refs))
        extra = dict(
            qkv_flat=by_name[QKV].reshape(2, D, 3 * D),
            out_flat=by_name[OUT].reshape(2, D, D),
            up_flat=by_name[UP].reshape(2, D, FF // 2),
            down_flat=by_name[DOWN].reshape(2, FF // 2, D),
        )
        backward_kernel(dims, names + list(extra), *refs, *extra.values())

    anywhere = pl.BlockSpec(memory_space=pl.ANY)
    arguments = [left[n] for n in BACK_IN[:-2]] + [out_grad, lengths]
    results = pl.pallas_call(
        kernel,
        out_shape=[jax.ShapeDtypeStruct(s, t) for s, t in outs.values()],
        in_specs=[anywhere] * (len(arguments) - 1) + [pl.BlockSpec(memory_space=pltpu.SMEM)],
        out_specs=[anywhere] * len(outs),
        scratch_shapes=list(scratch.values()),
        compiler_params=pltpu.CompilerParams(collective_id=2, has_side_effects=True, vmem_limit_bytes=62 << 20),
        name="backward",
    )(*arguments)
    return SimpleNamespace(**dict(zip(outs, results)))


def unpack_share(small, count, here):
    vec_lanes, vec_group, bias_lanes, bias_group, bias_rows = small_layout(count)
    vectors = lax.dynamic_slice(small, (0, lax.rem(here, vec_group) * vec_lanes), (10, vec_lanes))
    start = lax.rem(lax.div(here, 2), bias_group) * bias_lanes if bias_group > 1 else 0
    bias = lax.dynamic_slice(small, (10, start), (bias_rows, bias_lanes // bias_rows))
    return vectors, bias.reshape(bias_lanes)


def per_device(dims, hidden_in, lengths, out_grad, w_qkv, w_out, w_up, w_down, vectors, up_bias):
    core, here = lax.axis_index(PIPE), lax.axis_index(DP)
    count = 2**dims
    rows = D // count
    left = forward_call(dims, here, core, hidden_in, lengths, w_qkv, w_out, w_up, w_down, vectors, up_bias)
    sums = backward(left, out_grad[:, 0], lengths[:, 0], dims)
    grad_vec, grad_bias = unpack_share(sums.g_small, count, here)
    up = sums.g_up.reshape(2, rows, count // 2, FF // count).transpose(1, 2, 0, 3).reshape(rows, FF)
    return (
        sums.edges[None, :, None],
        sums.g_qkv.astype(WIDE)[None],
        sums.g_out.astype(WIDE)[None],
        up.astype(WIDE)[None],
        sums.g_down.astype(WIDE)[None],
        grad_vec[None],
        grad_bias[None],
    )


def solution(mesh):
    dims = (mesh.shape[DP] - 1).bit_length()
    weights = P(PIPE, DP, None)
    placed = (
        P(None, DP, None, None),
        P(None, DP),
        P(None, DP, None, None),
        weights,
        weights,
        weights,
        weights,
        P(PIPE, None, DP),
        P(PIPE, DP),
    )
    return jax.shard_map(
        functools.partial(per_device, dims),
        mesh=mesh,
        in_specs=placed,
        out_specs=(
            P(PIPE, None, DP, None, None),
            weights,
            weights,
            weights,
            weights,
            P(PIPE, None, DP),
            P(PIPE, DP),
        ),
        check_vma=False,
    )
```

```python
import functools
from types import SimpleNamespace

import jax
import jax.numpy as jnp
from jax import lax
from jax.experimental import pallas as pl
from jax.experimental.pallas import tpu as pltpu
from jax.sharding import PartitionSpec as P

D = 1024
HEADS = 16
HEAD_DIM = 64
FF = 4096
SEQ = 256
EPS = 1e-05
SCALE = HEAD_DIM**-0.5
MESH = pl.DeviceIdType.MESH
LOW = jnp.bfloat16
WIDE = jnp.float32
QKV, OUT, UP, DOWN = "qkv", "out", "up", "down"
FLAT = "_flat"
PIPE, DP = "pipe", "dp"
KINDS = [(QKV, 0), (QKV, 1), (QKV, 2), (OUT, 0), (UP, 0), (UP, 1), (DOWN, 0), (DOWN, 1)]
NU = len(KINDS)
GATHER_ORDERS = [
    (0, 1, 3, 2), (0, 1, 2, 3), (0, 1, 2, 3), (0, 1, 2, 3),
    (0, 1, 2), (0, 1, 2), (2, 0, 1), (0, 1, 2),
    (0, 1, 3, 2), (0, 1, 3, 2), (0, 1, 2, 3), (2, 0, 1, 3),
    (0, 1, 2), (0, 1, 2), (2, 0, 1), (2, 0, 1),
]
SCHEDULE = [
    2000, 16, 2001, 192, 224, 64, 176, 0, 80, 17, 96, 2002, 48, 1, 240, 208, 18, 128, 49, 2003,
    2004, 32, 160, 2, 19, 129, 50, 81, 3, 33, 65, 161, 51, 112, 66, 34, 4, 2005, 162, 144,
    35, 82, 3000, 52, 177, 130, 20, 145, 67, 31, 15, 178, 97, 83, 63, 36, 163, 47, 3002, 146,
    113, 3003, 68, 193, 3001, 3004, 79, 131, 3005, 3006, 3007, 84, 98, 95, 209, 114, 3009, 132, 194, 3008,
    179, 164, 175, 3010, 3011, 147, 3012, 225, 99, 115, 111, 210, 143, 3013, 3014, 127, 3016, 180, 3018, 3015,
    195, 3017, 241, 226, 148, 159, 191, 3019, 3020, 3030, 3033, 211, 3031, 3032, 3034, 3035, 3036, 3037, 196, 242,
    207, 212, 227, 223, 3038, 239, 3039, 3040, 3041, 3042, 3043, 243, 3044, 3045, 255, 3046, 3047, 3048, 3049, 3050,
]
GATHER_FIRST = -10
GATHER_LAGS = [3, 1, -1, -4]
GATHER_READY = 5


def axis_order(dims, u):
    kind, block = KINDS[u]
    if kind in (UP, DOWN):
        return tuple(range(dims - 1))
    return tuple((i + 2 * u) % dims for i in range(dims))


def gather_order(dims, v):
    return GATHER_ORDERS[v] if dims == 4 else axis_order(dims, v % NU)


def place(dims):
    core, here = lax.axis_index(PIPE), lax.axis_index(DP)
    bits = [lax.rem(lax.div(here, 2 ** (dims - 1 - i)), 2) for i in range(dims)]
    partners = [(core, here + (1 - 2 * bits[i]) * 2 ** (dims - 1 - i)) for i in range(dims)]
    return core, bits, partners, (1 - core, here)


def greet(everyone):
    barrier = pltpu.get_barrier_semaphore()
    for device in everyone:
        pl.semaphore_signal(barrier, inc=1, device_id=device, device_id_type=MESH)
    pl.semaphore_wait(barrier, len(everyone))


def remote(source, target, send, recv, device):
    return pltpu.make_async_remote_copy(
        src_ref=source, dst_ref=target, send_sem=send, recv_sem=recv, device_id=device, device_id_type=MESH
    )


def span(start, size):
    if isinstance(start, int):
        return pl.ds(start, size)
    return pl.ds(pl.multiple_of(start, size), size)


def for_each(count, body):
    lax.fori_loop(0, count, lambda i, carry: (body(i), carry)[1], 0, unroll=min(count, 4))


def unit_columns(u, column_half):
    kind, block = KINDS[u]
    if kind == DOWN:
        return span(block * 512 + column_half * 256, 256)
    return span(block * 1024 + column_half * 512, 512)


def norm_parts(values):
    center = values - jnp.mean(values, -1, keepdims=True)
    factor = lax.rsqrt(jnp.mean(center * center, -1, keepdims=True) + EPS)
    return (center * factor, factor)


def norm_back(grad_normed, normed, factor):
    return factor * (
        grad_normed
        - jnp.mean(grad_normed, -1, keepdims=True)
        - normed * jnp.mean(grad_normed * normed, -1, keepdims=True)
    )


def dot(left, right, dims=((1,), (0,))):
    return lax.dot_general(left, right, (dims, ((), ())), preferred_element_type=WIDE)


BY_ROWS = ((0,), (0,))
BY_COLUMNS = ((1,), (1,))


def small_layout(count):
    vec_lanes, bias_lanes = D // count, FF // count
    return vec_lanes, 128 // vec_lanes, bias_lanes, max(1, 128 // bias_lanes), max(1, bias_lanes // 128)


def head_masks():
    lanes = lax.broadcasted_iota(jnp.int32, (1, 128), 1)
    first = (lanes < HEAD_DIM).astype(WIDE)
    return first, 1.0 - first


def valid_rows(length, start, count):
    rows = lax.broadcasted_iota(jnp.int32, (count, 1), 0) + start
    return (rows < length).astype(WIDE)


FORWARD_IN = ["w_qkv", "w_out", "w_up", "w_down", "hidden", "vectors", "up_bias", "lengths"]
S = "s_"
SAVED = ["x", "a", "q", "k", "v", "o", "p", "h", "c", "g", "gp"]
LOADS = ["vecs", "og", "y", "w_down", "w_up", "w_qkv", "w_out"] + SAVED
N = SimpleNamespace(**{n: n for n in LOADS})


def saved_shapes():
    wide = lambda *s: (s, WIDE)
    low = lambda *s: (s, LOW)
    return dict(
        x=low(SEQ, D),
        a=low(SEQ, D),
        q=low(SEQ, D),
        k=low(SEQ, D),
        v=low(SEQ, D),
        o=low(SEQ, D),
        p=low(HEADS, SEQ, SEQ),
        h=wide(SEQ, D),
        c=low(2, SEQ, D),
        g=low(2, SEQ, FF // 2),
        gp=low(2, SEQ, FF // 2),
    )


def forward_kernel(dims, names, *refs):
    R = SimpleNamespace(**dict(zip(names, refs)))
    core, bits, partners, sibling = place(dims)
    own = tuple(bits)
    half = bits[-1]
    mate = partners[-1]
    greet([sibling] + partners)
    total = 2 * NU
    count = 2**dims
    saved = SimpleNamespace(**{n: [getattr(R, n + str(l)) for l in range(2)] for n in SAVED})

    def first_pairs(u, layer, column_half):
        kind, block = KINDS[u]
        cols = unit_columns(u, column_half)
        if kind == UP:
            pairs = []
            for i in range(2):
                block_id = block * 4 + column_half * 2 + i
                to = span(block_id * 256, 256)
                for which, target in ((half, R.up.at[(layer,) + own]), (1 - half, R.stage.at[layer])):
                    pairs.append((R.w_up.at[0, :, span((2 * block_id + which) * 256, 256)], target.at[:, to]))
            return pairs
        if kind == DOWN:
            return [(R.w_down.at[0, :, cols], R.down.at[(layer,) + own[:-1] + (slice(None), cols)])]
        return [(getattr(R, "w_" + kind).at[0, :, cols], getattr(R, kind).at[(layer,) + own + (slice(None), cols)])]

    def first_local(u, layer):
        return [
            pltpu.make_async_copy(s, t, R.local_sem.at[u, i])
            for i, (s, t) in enumerate(first_pairs(u, layer, core))
        ]

    def first_remote(u, layer):
        return [
            remote(s, t, R.first_send.at[u, i], R.first_recv.at[u, i], sibling)
            for i, (s, t) in enumerate(first_pairs(u, layer, 1 - core))
        ]

    def chain(v):
        layer, u = v // NU, v % NU
        kind, block = KINDS[u]
        cols = unit_columns(u, core)
        moves = []
        if kind == UP:
            moves.append((R.stage.at[layer, :, cols], R.up.at[(layer,) + own + (slice(None), cols)], mate))
        order = gather_order(dims, v)
        known = dims - 1 if kind == DOWN else dims
        free = {dims - 1} if kind == UP else set()
        for k in range(len(order) + 1):
            gathered = set(order[:k]) | free
            where = tuple(slice(None) if i in gathered else bits[i] for i in range(known))
            ref = getattr(R, kind).at[(layer,) + where + (slice(None), cols)]
            moves.append((ref, ref, partners[order[k]] if k < len(order) else sibling))
        return [remote(s, t, R.send.at[v, i], R.recv.at[v, i], d) for i, (s, t, d) in enumerate(moves)]

    def small_step(k):
        where = tuple(slice(None) if i < k else bits[i] for i in range(dims))
        ref = R.small_all.at[(core,) + where]
        return remote(ref, ref, R.small_send.at[k], R.small_recv.at[k], partners[k] if k < dims else sibling)

    def pack_small():
        vec_lanes, vec_group, bias_lanes, bias_group, bias_rows = small_layout(count)
        here = lax.axis_index(DP)

        def put(values, at, group):
            if group == 1:
                return values
            return jnp.concatenate([jnp.where(at == i, values, 0.0) for i in range(group)], axis=1)

        tile = R.tile
        tile[...] = jnp.zeros_like(tile)
        tile[0:10, :] = put(R.vectors[0].astype(WIDE), lax.rem(here, vec_group), vec_group)
        bias = put(R.up_bias[...].astype(WIDE), lax.rem(lax.div(here, 2), bias_group), bias_group)
        for i in range(bias_rows):
            tile[10 + i : 11 + i, :] = bias[:, i * 128 : (i + 1) * 128]
        R.small_all[(core,) + own] = tile[...].astype(LOW)

    load_x = pltpu.make_async_copy(R.hidden.at[core, 0], saved.x[0], R.io.at[1])
    load_x.start()
    for layer in range(2):

        @pl.when(core == layer)
        def _():
            for u in range(NU):
                for copy in first_remote(u, layer) + first_local(u, layer):
                    copy.start()

    pack_small()

    def arrive(v):
        layer, u = v // NU, v % NU

        @pl.when(core == layer)
        def _():
            for copy in first_local(u, layer):
                copy.wait()
            for copy in first_remote(u, layer):
                copy.wait_send()

        @pl.when(core != layer)
        def _():
            for copy in first_remote(u, layer):
                copy.wait_recv()

    length = R.lengths[core, 0]
    vecs, biases = R.vecs, R.biases
    first_head, second_head = head_masks()

    def assemble():
        vec_lanes, vec_group, bias_lanes, bias_group, bias_rows = small_layout(count)
        small = R.small_all

        def shard(layer, d):
            return small[(layer,) + tuple((d >> (dims - 1 - i)) & 1 for i in range(dims))].astype(WIDE)

        def half_shard(layer, b):
            lead = tuple((b >> (dims - 2 - i)) & 1 for i in range(dims - 1))
            return small[(layer,) + lead + (half,)].astype(WIDE)

        for layer in range(2):
            for t in range(D // 128):
                vecs[layer, :, t * 128 : (t + 1) * 128] = sum(
                    shard(layer, d) for d in range(t * vec_group, (t + 1) * vec_group)
                )
            for t in range(count // 2 // bias_group):
                tile = sum(half_shard(layer, b) for b in range(t * bias_group, (t + 1) * bias_group))
                for i in range(bias_rows):
                    at = (t * bias_rows + i) * 128
                    biases[layer, 0:1, at : at + 128] = tile[10 + i : 11 + i, :]

    save_queue = []

    def save(name, layer):
        copy = pltpu.make_async_copy(
            getattr(saved, name)[layer], getattr(R, S + name).at[layer], R.save_sem.at[layer, SAVED.index(name)]
        )
        copy.start()
        save_queue.append(copy)

    def vec(layer, i, cols=slice(None)):
        return vecs[layer, i : i + 1, cols]

    def load_weight(v):
        layer, u = v // NU, v % NU
        kind, block = KINDS[u]
        if kind == DOWN:
            flat = R.down_flat.at[layer, :, pl.ds(block * 512, 512)]
            target = R.w_low.at[:, pl.ds(block * 512, 512)]
        else:
            flat = getattr(R, kind + FLAT).at[layer, :, pl.ds(block * 1024, 1024)]
            target = R.w_slots.at[u]
        return pltpu.make_async_copy(flat, target, R.weight_sem.at[u])

    def first_norm(layer):
        def rows(i):
            at = span(i * 32, 32)
            normed, unused = norm_parts(saved.x[layer][at, :].astype(WIDE))
            saved.a[layer][at, :] = (normed * vec(layer, 0) + vec(layer, 1)).astype(LOW)

        for_each(SEQ // 32, rows)
        save(N.x, layer)
        save(N.a, layer)

    def project(layer, block):
        target = (saved.q, saved.k, saved.v)[block][layer]
        weight = R.w_slots.at[block]

        def columns(n):
            at = span(n * 256, 256)
            values = dot(saved.a[layer][...], weight[:, at])
            if block == 0:
                values = (values + vec(layer, 2, at)).astype(LOW) * SCALE
            elif block == 2:
                values = values + vec(layer, 3, at)
            target[:, at] = values.astype(LOW)

        for_each(D // 256, columns)
        save((N.q, N.k, N.v)[block], layer)

    def attention(layer):
        key_ids = lax.broadcasted_iota(jnp.int32, (SEQ, SEQ), 0)
        query_ids = lax.broadcasted_iota(jnp.int32, (SEQ, SEQ), 1)
        blocked = jnp.where((key_ids <= query_ids) & (key_ids < length), 0.0, -1e30)

        def pair(n):
            at = span(n * 128, 128)
            query, key, value = (part[layer][:, at] for part in (saved.q, saved.k, saved.v))
            parts = []
            for i, mask in enumerate((first_head, second_head)):
                scores = dot(key, query * mask.astype(LOW), BY_COLUMNS) + blocked
                weights = jnp.exp(scores - jnp.max(scores, 0, keepdims=True))
                probs = (weights * (1.0 / jnp.sum(weights, 0, keepdims=True))).astype(LOW)
                saved.p[layer][2 * n + i] = probs
                parts.append(dot(probs, value, BY_ROWS) * mask)
            saved.o[layer][:, at] = (parts[0] + parts[1]).astype(LOW)

        for_each(HEADS // 2, pair)
        save(N.p, layer)
        save(N.o, layer)

    def send_c(layer):
        ref = saved.c[layer]
        return remote(ref.at[0], ref.at[1], R.act_send.at[layer, 0], R.act_recv.at[layer, 0], mate)

    def attend_out(layer):
        weight = R.w_slots.at[3]
        hidden = saved.h[layer]

        def columns(n):
            at = span(n * 256, 256)
            values = dot(saved.o[layer][...], weight[:, at])
            hidden[:, at] = saved.x[layer][:, at].astype(WIDE) + values + vec(layer, 4, at)

        for_each(D // 256, columns)

    def second_norm(layer):
        def rows(i):
            at = span(i * 32, 32)
            normed, unused = norm_parts(saved.h[layer][at, :])
            saved.c[layer][0, at, :] = (normed * vec(layer, 5) + vec(layer, 6)).astype(LOW)

        for_each(SEQ // 32, rows)
        save(N.h, layer)

    def feed_up(layer, block, who):
        weight = R.w_slots.at[4 + block]

        def columns(n):
            at = span(n * 256, 256)
            to = span(block * 1024 + n * 256, 256)
            value = dot(saved.c[layer][who], weight[:, at]) + biases[layer, 0:1, to]
            share = 0.5 + 0.5 * lax.erf(value * 0.7071067811865476)
            slope = share + value * (jnp.exp(value * value * -0.5) * 0.3989422804014327)
            saved.g[layer][who, :, to] = (value * share).astype(LOW)
            saved.gp[layer][who, :, to] = slope.astype(LOW)

        for_each(4, columns)
        if block == 1 and who == 1:
            save(N.g, layer)
            save(N.gp, layer)

    def send_part(layer, block):
        at = pl.ds(block * 512, 512)
        return remote(
            R.part.at[layer, 0, :, at],
            R.part.at[layer, 1, :, at],
            R.act_send.at[layer, 1 + block],
            R.act_recv.at[layer, 1 + block],
            mate,
        )

    def down_theirs(layer, block):
        def columns(n):
            at = span(block * 512 + n * 256, 256)
            R.part[layer, 0, :, at] = dot(saved.g[layer][1], R.w_low[:, at]).astype(LOW)

        for_each(2, columns)

    def down_mine(layer, block):
        def columns(n):
            at = span(block * 512 + n * 256, 256)
            values = dot(saved.g[layer][0], R.w_low[:, at])
            R.y[:, at] = saved.h[layer][:, at] + values + vec(layer, 7, at)

        for_each(2, columns)

    def end(layer):
        def rows(i):
            at = span(i * 32, 32)
            valid = valid_rows(length, i * 32, 32)
            values = R.y[at, :] + R.part[layer, 1, at, :].astype(WIDE)
            if layer == 0:
                saved.x[1][at, :] = (values * valid).astype(LOW)
            else:
                R.y[at, :] = values
                normed, unused = norm_parts(values)
                R.z[at, :] = (normed * vec(1, 8) + vec(1, 9)) * valid

        for_each(SEQ // 32, rows)

    def weight(layer, u):
        load_weight(layer * NU + u).wait()

    def wait_parts(layer):
        for block in range(2):
            send_part(layer, block).wait()

    def wait_c(layer):
        send_c(layer).wait()
        save(N.c, layer)

    pieces = [
        (first_norm, None),
        (lambda layer: project(layer, 0), 0),
        (lambda layer: project(layer, 1), 1),
        (lambda layer: project(layer, 2), 2),
        (attention, None),
        (attend_out, 3),
        (second_norm, None),
        (lambda layer: send_c(layer).start(), None),
        (lambda layer: feed_up(layer, 0, 0), 4),
        (lambda layer: feed_up(layer, 1, 0), 5),
        (wait_c, None),
        (lambda layer: feed_up(layer, 0, 1), None),
        (lambda layer: feed_up(layer, 1, 1), None),
        (lambda layer: down_theirs(layer, 0), 6),
        (lambda layer: send_part(layer, 0).start(), None),
        (lambda layer: down_mine(layer, 0), None),
        (lambda layer: down_theirs(layer, 1), 7),
        (lambda layer: send_part(layer, 1).start(), None),
        (lambda layer: down_mine(layer, 1), None),
        (wait_parts, None),
        (end, None),
    ]

    chains = [chain(v) for v in range(total)]

    def plain_schedule():
        moves = []
        for v in range(total):
            for i in range(len(chains[v])):
                left = len(chains[v]) - 1 - i
                lag = GATHER_LAGS[left] if left < len(GATHER_LAGS) else GATHER_LAGS[-1] - left + len(GATHER_LAGS) - 1
                moves.append((v + (lag if i else min(GATHER_FIRST, lag)), -i, v))
            moves.append((v + GATHER_READY, -99, v))
        codes = [16 * v - i if i > -99 else 16 * v + 15 for unused, i, v in sorted(moves)]
        for k in range(dims + 2):
            codes.insert(6 * k, 2000 + k)
        result, done = [], set()
        jobs = [(layer, w) for layer in range(2) for w in range(len(pieces))]
        for code in codes:
            result.append(code)
            done.add(code)
            while jobs and 2000 + dims + 1 in done:
                layer, w = jobs[0]
                u = pieces[w][1]
                if u is not None and 16 * (layer * NU + u) + 15 not in done:
                    break
                result.append(3000 + 30 * layer + w)
                jobs.pop(0)
        return result

    load_x.wait()
    for code in SCHEDULE if dims == 4 and SCHEDULE else plain_schedule():
        if code >= 3000:
            layer, w = (code - 3000) // 30, (code - 3000) % 30
            if pieces[w][1] is not None:
                weight(layer, pieces[w][1])
            pieces[w][0](layer)
        elif code >= 2000:
            k = code - 2000
            if k > 0:
                small_step(k - 1).wait()
            if k <= dims:
                small_step(k).start()
            else:
                assemble()
        elif code % 16 == 15:
            v = code // 16
            chains[v][-1].wait()
            load_weight(v).start()
        else:
            v, i = code // 16, code % 16
            if i == 0:
                arrive(v)
            else:
                chains[v][i - 1].wait()
            chains[v][i].start()

    last = [(R.y, R.s_y, 0), (R.z, R.s_z, 1), (R.vecs, R.s_vecs, 2)]
    for source, target, i in last:
        pltpu.make_async_copy(source, target, R.last_sem.at[i]).start()
    for copy in save_queue:
        copy.wait()
    for source, target, i in last:
        pltpu.make_async_copy(source, target, R.last_sem.at[i]).wait()


def forward(shards, hidden, vectors, up_bias, lengths, dims):
    rows = D // 2**dims
    bits = (2,) * dims
    outs = dict(
        qkv=((2,) + bits + (rows, 3 * D), LOW),
        out=((2,) + bits + (rows, D), LOW),
        up=((2,) + bits + (rows, FF // 2), LOW),
        down=((2,) + bits[:-1] + (4 * rows, D), LOW),
        stage=((2, rows, FF // 2), LOW),
    )
    for name, (shape, dtype) in saved_shapes().items():
        outs[S + name] = ((2,) + shape, dtype)
    outs[S + N.y] = ((SEQ, D), WIDE)
    outs[S + "z"] = ((SEQ, D), WIDE)
    outs[S + N.vecs] = ((2, 16, D), WIDE)
    dma = pltpu.SemaphoreType.DMA
    total = 2 * NU
    scratch = dict(
        small_all=pltpu.VMEM((2,) + bits + (16, 128), LOW),
        vecs=pltpu.VMEM((2, 16, D), WIDE),
        biases=pltpu.VMEM((2, 8, FF // 2), WIDE),
        w_slots=pltpu.VMEM((6, D, D), LOW),
        w_low=pltpu.VMEM((FF // 2, D), LOW),
        part=pltpu.VMEM((2, 2, SEQ, D), LOW),
        y=pltpu.VMEM((SEQ, D), WIDE),
        z=pltpu.VMEM((SEQ, D), WIDE),
        local_sem=dma((NU, 4)),
        first_send=dma((NU, 4)),
        first_recv=dma((NU, 4)),
        send=dma((total, dims + 2)),
        recv=dma((total, dims + 2)),
        small_send=dma((dims + 1,)),
        small_recv=dma((dims + 1,)),
        io=dma((2,)),
        tile=pltpu.VMEM((16, 128), WIDE),
        save_sem=dma((2, len(SAVED))),
        weight_sem=dma((NU,)),
        act_send=dma((2, 3)),
        act_recv=dma((2, 3)),
        last_sem=dma((3,)),
    )
    for name, (shape, dtype) in saved_shapes().items():
        for layer in range(2):
            scratch[name + str(layer)] = pltpu.VMEM(shape, dtype)
    names = FORWARD_IN + list(outs) + list(scratch)

    def kernel(*refs):
        by_name = dict(zip(names, refs))
        extra = dict(
            qkv_flat=by_name[QKV].reshape(2, D, 3 * D),
            out_flat=by_name[OUT].reshape(2, D, D),
            up_flat=by_name[UP].reshape(2, D, FF // 2),
            down_flat=by_name[DOWN].reshape(2, FF // 2, D),
        )
        forward_kernel(dims, names + list(extra), *refs, *extra.values())

    anywhere = pl.BlockSpec(memory_space=pl.ANY)
    whole = pl.BlockSpec(memory_space=pltpu.VMEM)
    results = pl.pallas_call(
        kernel,
        out_shape=[jax.ShapeDtypeStruct(s, t) for s, t in outs.values()],
        in_specs=[anywhere] * 5 + [whole] * 2 + [pl.BlockSpec(memory_space=pltpu.SMEM)],
        out_specs=[anywhere] * len(outs),
        scratch_shapes=list(scratch.values()),
        compiler_params=pltpu.CompilerParams(collective_id=1, has_side_effects=True, vmem_limit_bytes=60 << 20),
        name="forward",
    )(*shards, hidden, vectors, up_bias, lengths)
    return dict(zip(outs, results))


BACK = [(DOWN, 0), (DOWN, 1), (UP, 0), (UP, 1), (OUT, 0), (QKV, 0), (QKV, 1), (QKV, 2)]
SCATTER_LAGS = [1, 3, 4, 5, 6]
BACK_ORDERS = [
    (0, 1, 2, 3), (0, 1, 3, 2), (0, 1, 2, 3), (0, 1, 2, 3),
    (0, 1, 2), (0, 1, 2), (0, 1, 2), (2, 0, 1),
]
BACK_SCHEDULE = [
    3000, 3001, 3003, 3002, 3004, 3006, 0, 3005, 3007, 3008, 3009, 3010, 3012, 16, 3011, 32, 1, 3013, 3014, 3015,
    3016, 48, 17, 64, 3017, 3018, 33, 3019, 80, 3020, 3022, 3023, 2, 65, 49, 3030, 3033, 3031, 18, 34,
    3021, 3032, 81, 66, 112, 3, 19, 96, 3034, 50, 3036, 35, 82, 67, 3035, 3040, 144, 128, 51, 3037,
    113, 3038, 3039, 68, 97, 52, 36, 83, 3041, 3042, 145, 3043, 176, 160, 3044, 114, 3045, 3046, 98, 84,
    192, 3047, 115, 129, 3048, 3049, 99, 177, 208, 100, 193, 116, 3050, 130, 3051, 161, 224, 178, 240, 3052,
    3053, 194, 4000, 2000, 209, 162, 225, 195, 241, 2001, 210, 163, 226, 146, 2002, 211, 196, 131, 242, 227,
    179, 180, 212, 147, 243, 164, 2003, 2004, 228, 244,
]
HELD, B, TILE = "held", "b_", "tile"
BACK_WEIGHTS = [QKV, OUT, UP, DOWN]
BACK_IN = BACK_WEIGHTS + [S + n for n in SAVED + ["y", "z", "vecs"]] + ["out_grad", "lengths"]


def back_order(dims, u):
    return BACK_ORDERS[u] if dims == 4 else axis_order(dims, u)


def box_name(u, k):
    return "box%d_%d" % (u, k)


def backward_kernel(dims, names, *refs):
    R = SimpleNamespace(**dict(zip(names, refs)))
    core, bits, partners, sibling = place(dims)
    own = tuple(bits)
    half = bits[-1]
    mate = partners[-1]
    greet([sibling] + partners)
    total = 2 * NU
    count = 2**dims
    length = R.lengths[core, 0]
    vecs, grads = R.vecs, R.grads
    first_head, second_head = head_masks()

    def load(name, layer):
        if name == N.y:
            source = R.s_y
        elif name == N.og:
            source = R.out_grad.at[core, 0]
        elif name == N.vecs:
            source = R.s_vecs
        elif name in (N.w_down, N.w_up, N.w_qkv, N.w_out):
            source = getattr(R, name[2:] + FLAT).at[layer]
        else:
            source = getattr(R, S + name).at[layer]
        if name == N.vecs:
            target = vecs
        elif name == N.w_up:
            target = R.b_w_wide.at[:, pl.ds(0, FF // 2)]
        elif name == N.w_qkv:
            target = R.b_w_wide
        else:
            target = getattr(R, B + name)
        return pltpu.make_async_copy(source, target, R.load_sem.at[LOADS.index(name)])

    def need(layer, *which):
        for name in which:
            load(name, layer).wait()

    def again(layer, *which):
        if layer == 1:
            for name in which:
                load(name, 0).start()

    def unit_of(v):
        return 1 - v // NU, BACK[v % NU]

    def columns_of(v, column_half):
        kind, block = BACK[v % NU]
        if kind == DOWN:
            return span(block * 512 + column_half * 256, 256)
        return span(block * 1024 + column_half * 512, 512)

    def order_of(v):
        return tuple(reversed(back_order(dims, KINDS.index(BACK[v % NU]))))

    def held(v):
        return getattr(R, HELD + str(v % NU))

    def box(v, k):
        if k == 0:
            kind, block = BACK[v % NU]
            return (R.down_box if kind == DOWN else R.wide_box).at[v % 2]
        return getattr(R, box_name(v % NU, k))

    def stage(v):
        kind, block = BACK[v % NU]
        return (R.down_stage if kind == DOWN else R.wide_stage).at[v % 2]

    def is_up(v):
        return BACK[v % NU][0] == UP

    def steps(v):
        return len(order_of(v)) + (1 if is_up(v) else 0)

    def where(v, k, away):
        order = order_of(v)
        place_of = []
        for i in range(dims - 1 if BACK[v % NU][0] == DOWN else dims):
            if i in order[: max(k - 1, 0)]:
                place_of.append(bits[i])
            elif 0 < k <= len(order) and i == order[k - 1]:
                place_of.append(1 - bits[i] if away else bits[i])
            elif k > len(order) and i == dims - 1:
                place_of.append(1 - half if away else half)
            elif k > len(order):
                place_of.append(bits[i])
            else:
                place_of.append(slice(None))
        return tuple(place_of)

    def device_of(v, k):
        if k == 0:
            return sibling
        return partners[order_of(v)[k - 1]] if k <= len(order_of(v)) else mate

    def move(v, k):
        source = stage(v) if k == 0 else held(v).at[where(v, k, True)]
        return remote(source, box(v, k), R.send.at[v, k], R.recv.at[v, k], device_of(v, k))

    def earlier(v, k):
        if k > 0 or BACK[v % NU][0] == DOWN:
            return v - NU if v >= NU else None
        wide = [w for w in range(total) if BACK[w % NU][0] != DOWN and w % 2 == v % 2 and w < v]
        return wide[-1] if wide else None

    def later(v, k):
        return any(earlier(w, k) == v for w in range(v + 1, total))

    def begin(v, k):
        if earlier(v, k) is not None:
            pl.semaphore_wait(R.credit.at[v % NU, k], 1)
        move(v, k).start()

    def consumed(v, k):
        for w in range(v + 1, total):
            if earlier(w, k) == v:
                pl.semaphore_signal(
                    R.credit.at[w % NU, k], inc=1, device_id=device_of(v, k), device_id_type=MESH
                )

    def finals(v):
        kind, block = BACK[v % NU]
        cols = columns_of(v, core)
        if kind == UP:
            pairs = []
            for i in range(2):
                block_id = block * 4 + core * 2 + i
                part = (slice(None), pl.ds(i * 256, 256))
                for which, source in ((half, held(v).at[own + part]), (1 - half, box(v, dims).at[part])):
                    pairs.append((source, R.g_up.at[:, span((2 * block_id + which) * 256, 256)]))
            return pairs
        if kind == DOWN:
            return [(held(v).at[own[:-1]], R.g_down.at[:, cols])]
        return [(held(v).at[own], getattr(R, "g_" + kind).at[:, cols])]

    def final_local(v):
        return [
            pltpu.make_async_copy(s, t, R.out_sem.at[v, i]) for i, (s, t) in enumerate(finals(v))
        ]

    def final_remote(v):
        return [
            remote(s, t, R.end_send.at[v, i], R.end_recv.at[v, i], sibling)
            for i, (s, t) in enumerate(finals(v))
        ]

    def finish(v):
        @pl.when(core == unit_of(v)[0])
        def _():
            for copy in final_local(v):
                copy.start()

        @pl.when(core != unit_of(v)[0])
        def _():
            for copy in final_remote(v):
                copy.start()

    def finished(v):
        @pl.when(core == unit_of(v)[0])
        def _():
            for copy in final_local(v):
                copy.wait()

        @pl.when(core != unit_of(v)[0])
        def _():
            for copy in final_remote(v):
                copy.wait_send()
        if is_up(v):
            consumed(v, dims)

    def event(v, k):
        move(v, k).wait()
        if not (is_up(v) and k == steps(v)):
            view = held(v).at[where(v, k, False)]
            view[...] = view[...] + box(v, k)[...]
            consumed(v, k)
        if k < steps(v):
            begin(v, k + 1)
        else:
            finish(v)

    def vec(layer, i):
        return vecs[layer, i : i + 1, :]

    def collect(layer, i, values):
        grads[layer, i : i + 1, :] = grads[layer, i : i + 1, :] + jnp.sum(values, 0, keepdims=True)

    def send_e(layer, block):
        ref = R.e.at[layer]
        at = pl.ds(block * 512, 512)
        send, recv = R.act_send.at[layer, 2 * block], R.act_recv.at[layer, 2 * block]
        return remote(ref.at[0, :, at], ref.at[1, :, at], send, recv, mate)

    def send_dc(layer):
        ref = R.dc_part
        return remote(ref.at[0], ref.at[1], R.act_send.at[layer, 1], R.act_recv.at[layer, 1], mate)

    def top(layer):
        if layer == 1:
            need(1, N.vecs, N.og, N.y)

        def rows(i):
            at = span(i * 32, 32)
            valid = valid_rows(length, i * 32, 32)
            if layer == 1:
                grad_z = R.b_og[at, :].astype(WIDE) * valid
                normed, factor = norm_parts(R.b_y[at, :])
                collect(1, 8, grad_z * normed)
                collect(1, 9, grad_z)
                grad_y = norm_back(grad_z * vec(1, 8), normed, factor)
            else:
                grad_y = R.dx[at, :].astype(WIDE) * valid
            R.dy[at, :] = grad_y
            branch = grad_y.astype(LOW)
            R.e[layer, 0, at, :] = branch
            collect(layer, 7, branch.astype(WIDE))

        for_each(SEQ // 32, rows)

    def produce(v, body, quarter_shape):
        for target, column_half in ((stage(v), 1 - core), (held(v), core)):
            cols = columns_of(v, column_half)

            def quarter(i):
                target[lax.div(i, 2), lax.rem(i, 2)] = body(i, cols).astype(LOW).reshape(quarter_shape)

            for_each(4, quarter)
            if column_half is not core:
                begin(v, 0)

    def pair_rows(ref, cols):
        values = ref[:, :, cols]
        return values.reshape(2 * SEQ, values.shape[-1])

    inner = (2,) * (dims - 2) + (D // count, 512)
    down_inner = (2,) * (dims - 3) + (FF // count, 256)

    def grad_down(layer, v, block):
        if block == 0:
            need(layer, N.g)
        produce(
            v,
            lambda i, cols: dot(pair_rows(R.b_g, span(i * 512, 512)), pair_rows(R.e.at[layer], cols), BY_ROWS),
            down_inner,
        )
        if block == 1:
            again(layer, N.g)

    def feed_hidden(layer, who):
        if who == 0:
            need(layer, N.w_down, N.gp)

        def hidden(n):
            at = span(n * 256, 256)
            grad_act = dot(R.e[layer, who], R.b_w_down[at, :], BY_COLUMNS)
            grad_upper = (grad_act * R.b_gp[who, :, at].astype(WIDE)).astype(LOW)
            R.b_gp[who, :, at] = grad_upper
            sums = jnp.sum(grad_upper.astype(WIDE), 0, keepdims=True)
            R.bias_grads[layer, 0:1, at] = sums if who == 0 else R.bias_grads[layer, 0:1, at] + sums

        for_each(FF // 2 // 256, hidden)
        if who == 1:
            again(layer, N.w_down)

    def feed_theirs(layer):
        need(layer, N.w_up)

        def theirs(n):
            at = span(n * 256, 256)
            R.dc_part[0, :, at] = dot(R.b_gp[1], R.b_w_wide[at, pl.ds(0, FF // 2)], BY_COLUMNS).astype(LOW)

        for_each(D // 256, theirs)

    def feed_mine(layer):
        def mine(n):
            at = span(n * 256, 256)
            R.dc[:, at] = dot(R.b_gp[0], R.b_w_wide[at, pl.ds(0, FF // 2)], BY_COLUMNS)

        for_each(D // 256, mine)
        load(N.w_qkv, layer).start()

    def grad_up(layer, v, block):
        if block == 0:
            need(layer, N.c)

        def body(i, cols):
            return dot(pair_rows(R.b_c, span(i * 256, 256)), pair_rows(R.b_gp, cols), BY_ROWS)

        produce(v, body, inner)
        if block == 1:
            again(layer, N.c, N.gp)

    def middle(layer):
        need(layer, N.h)

        def rows(i):
            at = span(i * 32, 32)
            grad_in = R.dc[at, :] + R.dc_part[1, at, :].astype(WIDE)
            normed, factor = norm_parts(R.b_h[at, :])
            collect(layer, 5, grad_in * normed)
            collect(layer, 6, grad_in)
            grad_hidden = R.dy[at, :] + norm_back(grad_in * vec(layer, 5), normed, factor)
            R.dy[at, :] = grad_hidden
            branch = grad_hidden.astype(LOW)
            R.f[at, :] = branch
            collect(layer, 4, branch.astype(WIDE))

        for_each(SEQ // 32, rows)
        again(layer, N.h)

    def grad_out(layer, v):
        need(layer, N.o)
        produce(v, lambda i, cols: dot(R.b_o[:, span(i * 256, 256)], R.f[:, cols], BY_ROWS), inner)
        again(layer, N.o)

    def grad_mixed(layer):
        need(layer, N.w_out)

        def columns(n):
            at = span(n * 256, 256)
            R.do[:, at] = dot(R.f[...], R.b_w_out[at, :], BY_COLUMNS).astype(LOW)

        for_each(D // 256, columns)
        again(layer, N.w_out)

    def attention_back(layer):
        need(layer, N.q, N.k, N.v, N.p)

        def pair(n):
            at = span(n * 128, 128)
            query, key, value, grad_o = R.b_q[:, at], R.b_k[:, at], R.b_v[:, at], R.do[:, at]
            sums = [0.0, 0.0, 0.0]
            for i, mask in enumerate((first_head.astype(LOW), second_head.astype(LOW))):
                probs = R.b_p[2 * n + i]
                grad_head = grad_o * mask
                wide = probs.astype(WIDE)
                grad_probs = dot(value, grad_head, BY_COLUMNS)
                shift = jnp.sum(grad_probs * wide, 0, keepdims=True)
                grad_scores = (wide * (grad_probs - shift)).astype(LOW)
                sums[0] += dot(grad_scores, key * mask, BY_ROWS)
                sums[1] += dot(grad_scores, query * mask)
                sums[2] += dot(probs, grad_head)
            sums[0] = sums[0] * SCALE
            for j in range(3):
                low = sums[j].astype(LOW)
                R.dp[:, pl.ds(pl.multiple_of(n * 128 + j * D, 128), 128)] = low
                if j != 1:
                    row = 2 if j == 0 else 3
                    grads[layer, row : row + 1, at] = jnp.sum(low.astype(WIDE), 0, keepdims=True)

        for_each(HEADS // 2, pair)
        again(layer, N.q, N.k, N.v, N.p)

    def grad_qkv(layer, v, block):
        if block == 0:
            need(layer, N.a)
        produce(v, lambda i, cols: dot(R.b_a[:, span(i * 256, 256)], R.dp[:, cols], BY_ROWS), inner)
        if block == 2:
            again(layer, N.a)

    def grad_attn_in(layer):
        need(layer, N.w_qkv)

        def columns(n):
            at = span(n * 256, 256)
            R.dc[:, at] = dot(R.dp[...], R.b_w_wide[at, :], BY_COLUMNS)

        for_each(D // 256, columns)
        again(layer, N.w_up)

    def bottom(layer):
        need(layer, N.x)

        def rows(i):
            at = span(i * 32, 32)
            grad_in = R.dc[at, :]
            normed, factor = norm_parts(R.b_x[at, :].astype(WIDE))
            collect(layer, 0, grad_in * normed)
            collect(layer, 1, grad_in)
            grad_x = R.dy[at, :] + norm_back(grad_in * vec(layer, 0), normed, factor)
            if layer == 1:
                R.dx[at, :] = grad_x.astype(LOW)
            else:
                R.b_y[at, :] = grad_x

        for_each(SEQ // 32, rows)
        again(layer, N.x)

    def spread():
        vec_lanes, vec_group, bias_lanes, bias_group, bias_rows = small_layout(count)
        tiles = R.tiles
        tiles[...] = jnp.zeros_like(tiles)
        for layer in range(2):
            for d in range(count):
                lead = tuple((d >> (dims - 1 - i)) & 1 for i in range(dims))
                t = d // vec_group
                tiles[(layer,) + lead + (slice(0, 10),)] = grads[layer, 0:10, t * 128 : (t + 1) * 128]
            for b in range(count // 2):
                lead = tuple((b >> (dims - 2 - i)) & 1 for i in range(dims - 1))
                for i in range(bias_rows):
                    at = (b // bias_group * bias_rows + i) * 128
                    tiles[(layer,) + lead + (half, slice(10 + i, 11 + i))] = R.bias_grads[layer, 0:1, at : at + 128]

    def tile_box(k):
        return getattr(R, TILE + str(k))

    def small_move(k):
        if k == 0:
            return remote(
                R.tiles.at[1 - core], tile_box(0), R.small_send.at[0], R.small_recv.at[0], sibling
            )
        lead = own[: k - 1] + (1 - bits[k - 1],)
        return remote(
            R.tiles.at[(core,) + lead],
            tile_box(k),
            R.small_send.at[k],
            R.small_recv.at[k],
            partners[k - 1],
        )

    def small_event(k):
        small_move(k).wait()
        lead = own[:k]
        view = R.tiles.at[(core,) + lead]
        view[...] = view[...] + tile_box(k)[...]
        if k < dims:
            small_move(k + 1).start()
        else:
            pltpu.make_async_copy(view, R.g_small, R.edge_sem.at[2]).start()

    for name in (N.vecs, N.og, N.y, N.g, N.w_down, N.gp, N.w_up, N.c, N.h, N.o, N.w_out, N.q, N.k, N.v, N.p, N.x, N.a):
        load(name, 1).start()
    grads[...] = jnp.zeros_like(grads)
    edge_local = [pltpu.make_async_copy(ref, R.edges.at[core], R.edge_sem.at[0]) for ref in (R.b_y, R.s_z)]
    edge_remote = [
        remote(ref, R.edges.at[core], R.edge_send.at[0], R.edge_recv.at[0], sibling) for ref in (R.s_z, R.b_y)
    ]

    @pl.when(core == 0)
    def _():
        edge_remote[0].start()

    @pl.when(core == 1)
    def _():
        edge_local[1].start()

    def last(layer):
        @pl.when(core == 0)
        def _():
            edge_local[0].start()

        @pl.when(core == 1)
        def _():
            edge_remote[1].start()

        spread()
        small_move(0).start()

    def unit(layer, u):
        return (1 - layer) * NU + u

    pieces = [
        (top, None),
        (lambda layer: send_e(layer, 0).start(), None),
        (lambda layer: send_e(layer, 1).start(), None),
        (lambda layer: feed_hidden(layer, 0), None),
        (lambda layer: send_e(layer, 0).wait(), None),
        (lambda layer: send_e(layer, 1).wait(), None),
        (lambda layer: grad_down(layer, unit(layer, 0), 0), 0),
        (lambda layer: feed_hidden(layer, 1), None),
        (feed_theirs, None),
        (lambda layer: send_dc(layer).start(), None),
        (lambda layer: grad_down(layer, unit(layer, 1), 1), 1),
        (feed_mine, None),
        (lambda layer: grad_up(layer, unit(layer, 2), 0), 2),
        (lambda layer: grad_up(layer, unit(layer, 3), 1), 3),
        (lambda layer: send_dc(layer).wait(), None),
        (middle, None),
        (lambda layer: grad_out(layer, unit(layer, 4)), 4),
        (grad_mixed, None),
        (attention_back, None),
        (lambda layer: grad_qkv(layer, unit(layer, 5), 0), 5),
        (lambda layer: grad_qkv(layer, unit(layer, 6), 1), 6),
        (lambda layer: grad_qkv(layer, unit(layer, 7), 2), 7),
        (grad_attn_in, None),
        (bottom, None),
    ]

    def plain_schedule():
        timed = []
        for v in range(total):
            for k in range(steps(v) + 1):
                lag = SCATTER_LAGS[k] if k < len(SCATTER_LAGS) else SCATTER_LAGS[-1] + (k - len(SCATTER_LAGS) + 1) / 8
                timed.append((v + lag, 0, -k, v))
            timed.append((v, 1, 0, v))
        result = []
        for turn in range(2):
            at = -1.0
            for w, (unused, u) in enumerate(pieces):
                at = max(at + 0.01, turn * NU + (u or 0))
                timed.append((at, 1, w, (turn, w)))
        codes = []
        for key, is_compute, k, v in sorted(timed, key=lambda item: item[:3]):
            if not is_compute:
                codes.append(16 * v - k)
            elif isinstance(v, tuple):
                codes.append(3000 + 30 * v[0] + v[1])
        codes.append(4000)
        return codes + [2000 + k for k in range(dims + 1)]

    for code in BACK_SCHEDULE if dims == 4 and BACK_SCHEDULE else plain_schedule():
        if code >= 4000:
            last(0)
        elif code >= 3000:
            turn, w = (code - 3000) // 30, (code - 3000) % 30
            u = pieces[w][1]
            if turn == 1 and u is not None:
                finished(u)
            pieces[w][0](1 - turn)
        elif code >= 2000:
            small_event(code - 2000)
        else:
            event(code // 16, code % 16)
    for v in range(NU, total):
        finished(v)

    @pl.when(core == 0)
    def _():
        edge_remote[0].wait_send()
        edge_local[0].wait()

    @pl.when(core == 1)
    def _():
        edge_local[1].wait()
        edge_remote[1].wait_send()

    edge_remote[0].wait_recv()
    pltpu.make_async_copy(R.tiles.at[(core,) + own], R.g_small, R.edge_sem.at[2]).wait()
    for layer in range(2):

        @pl.when(core == layer)
        def _():
            for v in range((1 - layer) * NU, (2 - layer) * NU):
                for copy in final_remote(v):
                    copy.wait_recv()


def backward(left, out_grad, lengths, dims):
    rows = D // 2**dims
    bits = (2,) * dims
    outs = dict(
        g_qkv=((rows, 3 * D), LOW),
        g_out=((rows, D), LOW),
        g_up=((rows, FF), LOW),
        g_down=((4 * rows, D), LOW),
        g_small=((16, 128), WIDE),
        edges=((2, SEQ, D), WIDE),
    )
    dma = pltpu.SemaphoreType.DMA
    total = 2 * NU
    vmem = lambda shape, dtype=LOW: pltpu.VMEM(shape, dtype)
    scratch = dict(
        vecs=vmem((2, 16, D), WIDE),
        grads=vmem((2, 16, D), WIDE),
        bias_grads=vmem((2, 8, FF // 2), WIDE),
        b_og=vmem((SEQ, D)),
        b_y=vmem((SEQ, D), WIDE),
        b_w_down=vmem((FF // 2, D)),
        b_w_wide=vmem((D, 3 * D)),
        b_w_out=vmem((D, D)),
        e=vmem((2, 2, SEQ, D)),
        dc_part=vmem((2, SEQ, D)),
        dc=vmem((SEQ, D), WIDE),
        dy=vmem((SEQ, D), WIDE),
        dx=vmem((SEQ, D)),
        f=vmem((SEQ, D)),
        do=vmem((SEQ, D)),
        dp=vmem((SEQ, 3 * D)),
        tiles=vmem((2,) + bits + (16, 128), WIDE),
        wide_stage=vmem((2,) + bits + (rows, 512)),
        wide_box=vmem((2,) + bits + (rows, 512)),
        down_stage=vmem((2,) + bits[:-1] + (4 * rows, 256)),
        down_box=vmem((2,) + bits[:-1] + (4 * rows, 256)),
        send=dma((total, dims + 1)),
        recv=dma((total, dims + 1)),
        credit=pltpu.SemaphoreType.REGULAR((NU, dims + 1)),
        out_sem=dma((total, 4)),
        end_send=dma((total, 4)),
        end_recv=dma((total, 4)),
        load_sem=dma((len(LOADS),)),
        act_send=dma((2, 3)),
        act_recv=dma((2, 3)),
        small_send=dma((dims + 1,)),
        small_recv=dma((dims + 1,)),
        edge_sem=dma((3,)),
        edge_send=dma((1,)),
        edge_recv=dma((1,)),
    )
    for k in range(dims + 1):
        scratch[TILE + str(k)] = vmem(bits[k:] + (16, 128), WIDE)
    for name, (shape, dtype) in saved_shapes().items():
        scratch[B + name] = vmem(shape, dtype)
    for u, (kind, block) in enumerate(BACK):
        piece = (4 * rows, 256) if kind == DOWN else (rows, 512)
        lead = bits[:-1] if kind == DOWN else bits
        scratch[HELD + str(u)] = vmem(lead + piece)
        count = dims if kind in (QKV, OUT) else dims - 1
        for k in range(1, count + 1):
            scratch[box_name(u, k)] = vmem(lead[k:] + piece)
        if kind == UP:
            scratch[box_name(u, dims)] = vmem(piece)
    names = BACK_IN + list(outs) + list(scratch)

    def kernel(*refs):
        by_name = dict(zip(names, refs))
        extra = dict(
            qkv_flat=by_name[QKV].reshape(2, D, 3 * D),
            out_flat=by_name[OUT].reshape(2, D, D),
            up_flat=by_name[UP].reshape(2, D, FF // 2),
            down_flat=by_name[DOWN].reshape(2, FF // 2, D),
        )
        backward_kernel(dims, names + list(extra), *refs, *extra.values())

    anywhere = pl.BlockSpec(memory_space=pl.ANY)
    arguments = [left[n] for n in BACK_IN[:-2]] + [out_grad, lengths]
    results = pl.pallas_call(
        kernel,
        out_shape=[jax.ShapeDtypeStruct(s, t) for s, t in outs.values()],
        in_specs=[anywhere] * (len(arguments) - 1) + [pl.BlockSpec(memory_space=pltpu.SMEM)],
        out_specs=[anywhere] * len(outs),
        scratch_shapes=list(scratch.values()),
        compiler_params=pltpu.CompilerParams(collective_id=2, has_side_effects=True, vmem_limit_bytes=62 << 20),
        name="backward",
    )(*arguments)
    return SimpleNamespace(**dict(zip(outs, results)))


def finish_kernel(dims, *refs):
    grads, small, edges = refs[:4], refs[4], refs[5]
    outs, out_vec, out_bias, out_edges, sem = refs[6:10], refs[10], refs[11], refs[12], refs[13]
    copy = pltpu.make_async_copy(edges, out_edges.at[0, :, 0], sem)
    copy.start()
    for grad, out in zip(grads, outs):
        out[0] = grad[...].astype(WIDE)
    vec_lanes, vec_group, bias_lanes, bias_group, bias_rows = small_layout(2**dims)
    here = lax.axis_index(DP)

    def pick(values, lanes, at, group):
        result = values[:, 0:lanes]
        for i in range(1, group):
            result = jnp.where(at == i, values[:, i * lanes : (i + 1) * lanes], result)
        return result

    out_vec[0] = pick(small[0:10, :], vec_lanes, lax.rem(here, vec_group), vec_group)
    if bias_group > 1:
        out_bias[...] = pick(small[10:11, :], bias_lanes, lax.rem(lax.div(here, 2), bias_group), bias_group)
    else:
        for i in range(bias_rows):
            out_bias[:, i * 128 : (i + 1) * 128] = small[10 + i : 11 + i, :]
    copy.wait()


def finish(sums, dims):
    count = 2**dims
    rows = D // count
    anywhere = pl.BlockSpec(memory_space=pl.ANY)
    whole = pl.BlockSpec(memory_space=pltpu.VMEM)
    shapes = [
        (1, rows, 3 * D),
        (1, rows, D),
        (1, rows, FF),
        (1, 4 * rows, D),
        (1, 10, D // count),
        (1, FF // count),
        (1, 2, 1, SEQ, D),
    ]
    return pl.pallas_call(
        functools.partial(finish_kernel, dims),
        out_shape=[jax.ShapeDtypeStruct(shape, WIDE) for shape in shapes],
        in_specs=[whole] * 5 + [anywhere],
        out_specs=[whole] * 6 + [anywhere],
        scratch_shapes=[pltpu.SemaphoreType.DMA],
        compiler_params=pltpu.CompilerParams(vmem_limit_bytes=40 << 20),
        name="finish",
    )(sums.g_qkv, sums.g_out, sums.g_up, sums.g_down, sums.g_small, sums.edges)


def regroup(values, outer, inner):
    lead = values.shape[:-1]
    values = values.reshape(lead + (-1, 2, inner))
    values = jnp.moveaxis(values, -2, -3).reshape(lead + (2, -1, outer))
    return jnp.moveaxis(values, -3, -2).reshape(lead + (-1,))


def per_device(dims, hidden_in, lengths, out_grad, w_qkv, w_out, w_up, w_down, vectors, up_bias):
    lanes = FF // 2**dims
    if lanes != 256:
        w_up = regroup(w_up, 256, lanes)
    left = forward((w_qkv, w_out, w_up, w_down), hidden_in, vectors, up_bias, lengths, dims)
    sums = backward(left, out_grad, lengths, dims)
    qkv, out, up, down, grad_vec, grad_bias, edges = finish(sums, dims)
    if lanes != 256:
        up = regroup(up, lanes, 256)
    return (edges, qkv, out, up, down, grad_vec, grad_bias)


def solution(mesh):
    dims = (mesh.shape[DP] - 1).bit_length()
    weights = P(PIPE, DP, None)
    placed = (
        P(None, DP, None, None),
        P(None, DP),
        P(None, DP, None, None),
        weights,
        weights,
        weights,
        weights,
        P(PIPE, None, DP),
        P(PIPE, DP),
    )
    return jax.shard_map(
        functools.partial(per_device, dims),
        mesh=mesh,
        in_specs=placed,
        out_specs=(
            P(PIPE, None, DP, None, None),
            weights,
            weights,
            weights,
            weights,
            P(PIPE, None, DP),
            P(PIPE, DP),
        ),
        check_vma=False,
    )
```

```python
import functools
from types import SimpleNamespace

import jax
import jax.numpy as jnp
from jax import lax
from jax.experimental import pallas as pl
from jax.experimental.pallas import tpu as pltpu
from jax.sharding import PartitionSpec as P

D = 1024
HEADS = 16
HEAD_DIM = 64
FF = 4096
SEQ = 256
EPS = 1e-05
SCALE = HEAD_DIM**-0.5
MESH = pl.DeviceIdType.MESH
LOW = jnp.bfloat16
WIDE = jnp.float32
QKV, OUT, UP, DOWN = "qkv", "out", "up", "down"
FLAT = "_flat"
PIPE, DP = "pipe", "dp"
PARTS = 4
DOWN_WIDE = D // PARTS
KINDS = [(QKV, 0), (QKV, 1), (QKV, 2), (OUT, 0), (UP, 0), (UP, 1)] + [(DOWN, i) for i in range(PARTS)]
NU = len(KINDS)
GATHER_ORDERS = [
    (0, 1, 2, 3), (0, 1, 2, 3), (0, 1, 3, 2), (0, 1, 3, 2),
    (0, 1, 2), (0, 1, 2), (0, 1, 2), (2, 0, 1),
    (2, 0, 1), (0, 1, 2), (0, 1, 3, 2), (2, 0, 1, 3),
    (0, 1, 2, 3), (0, 1, 3, 2), (0, 1, 2), (2, 0, 1),
    (0, 1, 2), (2, 0, 1), (2, 0, 1), (0, 1, 2),
]
SCHEDULE = [
    2000, 2001, 16, 112, 2002, 32, 240, 80, 241, 17, 128, 176, 0, 33, 2003, 224, 2004, 48, 18, 64,
    288, 1, 2005, 34, 192, 49, 272, 81, 19, 2, 193, 96, 160, 35, 82, 50, 177, 161, 194, 3,
    65, 36, 51, 178, 208, 256, 66, 195, 144, 3000, 20, 47, 4, 3003, 97, 113, 83, 15, 209, 225,
    31, 179, 52, 162, 67, 145, 3002, 129, 3001, 63, 84, 98, 114, 3004, 3005, 3006, 3007, 68, 146, 210,
    130, 95, 180, 242, 226, 3009, 79, 99, 111, 163, 115, 147, 127, 3008, 257, 159, 3010, 3011, 3012, 3013,
    3016, 3017, 131, 196, 3015, 211, 3022, 3023, 3018, 304, 3014, 143, 3019, 243, 3020, 207, 164, 3024, 289, 3021,
    227, 175, 191, 305, 273, 3025, 3026, 3030, 212, 3031, 3033, 258, 3032, 223, 3034, 3035, 3036, 3037, 244, 228,
    290, 255, 306, 3039, 239, 259, 274, 3038, 291, 271, 3040, 3041, 3042, 3043, 3044, 307, 303, 275, 3049, 3050,
    319, 3051, 287, 3052, 3053, 3045, 3046, 3047, 3054, 3048, 3055, 3056,
]
GATHER_FIRST = -10
GATHER_LAGS = [3, 1, -1, -4]
GATHER_READY = 5


def axis_order(dims, u):
    kind, block = KINDS[u]
    if kind in (UP, DOWN):
        return tuple(range(dims - 1))
    return tuple((i + 2 * u) % dims for i in range(dims))


def gather_order(dims, v):
    return GATHER_ORDERS[v] if dims == 4 else axis_order(dims, v % NU)


def place(dims):
    core, here = lax.axis_index(PIPE), lax.axis_index(DP)
    bits = [lax.rem(lax.div(here, 2 ** (dims - 1 - i)), 2) for i in range(dims)]
    partners = [(core, here + (1 - 2 * bits[i]) * 2 ** (dims - 1 - i)) for i in range(dims)]
    return core, bits, partners, (1 - core, here)


def greet(everyone):
    barrier = pltpu.get_barrier_semaphore()
    for device in everyone:
        pl.semaphore_signal(barrier, inc=1, device_id=device, device_id_type=MESH)
    pl.semaphore_wait(barrier, len(everyone))


def remote(source, target, send, recv, device):
    return pltpu.make_async_remote_copy(
        src_ref=source, dst_ref=target, send_sem=send, recv_sem=recv, device_id=device, device_id_type=MESH
    )


def span(start, size):
    if isinstance(start, int):
        return pl.ds(start, size)
    return pl.ds(pl.multiple_of(start, size), size)


def for_each(count, body):
    lax.fori_loop(0, count, lambda i, carry: (body(i), carry)[1], 0, unroll=min(count, 4))


def unit_columns(u, column_half):
    kind, block = KINDS[u]
    if kind == DOWN:
        return span(block * DOWN_WIDE + column_half * (DOWN_WIDE // 2), DOWN_WIDE // 2)
    return span(block * 1024 + column_half * 512, 512)


def norm_parts(values):
    center = values - jnp.mean(values, -1, keepdims=True)
    factor = lax.rsqrt(jnp.mean(center * center, -1, keepdims=True) + EPS)
    return (center * factor, factor)


def norm_back(grad_normed, normed, factor):
    return factor * (
        grad_normed
        - jnp.mean(grad_normed, -1, keepdims=True)
        - normed * jnp.mean(grad_normed * normed, -1, keepdims=True)
    )


def dot(left, right, dims=((1,), (0,))):
    return lax.dot_general(left, right, (dims, ((), ())), preferred_element_type=WIDE)


BY_ROWS = ((0,), (0,))
BY_COLUMNS = ((1,), (1,))


def small_layout(count):
    vec_lanes, bias_lanes = D // count, FF // count
    return vec_lanes, 128 // vec_lanes, bias_lanes, max(1, 128 // bias_lanes), max(1, bias_lanes // 128)


def head_masks():
    lanes = lax.broadcasted_iota(jnp.int32, (1, 128), 1)
    first = (lanes < HEAD_DIM).astype(WIDE)
    return first, 1.0 - first


def valid_rows(length, start, count):
    rows = lax.broadcasted_iota(jnp.int32, (count, 1), 0) + start
    return (rows < length).astype(WIDE)


FORWARD_IN = ["w_qkv", "w_out", "w_up", "w_down", "hidden", "vectors", "up_bias", "lengths"]
S = "s_"
SAVED = ["x", "a", "q", "k", "v", "o", "p", "h", "c", "g", "gp"]
LOADS = ["vecs", "og", "y", "w_down", "w_up", "w_qkv", "w_out"] + SAVED
N = SimpleNamespace(**{n: n for n in LOADS})


def saved_shapes():
    wide = lambda *s: (s, WIDE)
    low = lambda *s: (s, LOW)
    return dict(
        x=low(SEQ, D),
        a=low(SEQ, D),
        q=low(SEQ, D),
        k=low(SEQ, D),
        v=low(SEQ, D),
        o=low(SEQ, D),
        p=low(HEADS, SEQ, SEQ),
        h=wide(SEQ, D),
        c=low(2, SEQ, D),
        g=low(2, SEQ, FF // 2),
        gp=low(2, SEQ, FF // 2),
    )


def forward_kernel(dims, names, *refs):
    R = SimpleNamespace(**dict(zip(names, refs)))
    core, bits, partners, sibling = place(dims)
    own = tuple(bits)
    half = bits[-1]
    mate = partners[-1]
    load_x = pltpu.make_async_copy(R.hidden.at[core, 0], R.x0, R.io.at[0])
    load_x.start()
    own_loads = [
        pltpu.make_async_copy(source.at[0], target, R.io.at[1 + i])
        for i, (source, target) in enumerate(
            [(R.w_qkv, R.own_qkv), (R.w_out, R.own_out), (R.w_up, R.own_up), (R.w_down, R.own_down)]
        )
    ]
    for copy in own_loads:
        copy.start()
    greet([sibling] + partners)
    total = 2 * NU
    count = 2**dims
    saved = SimpleNamespace(**{n: [getattr(R, n + str(l)) for l in range(2)] for n in SAVED})

    def first_pairs(u, layer, column_half):
        kind, block = KINDS[u]
        cols = unit_columns(u, column_half)
        if kind == UP:
            pairs = []
            for i in range(2):
                block_id = block * 4 + column_half * 2 + i
                to = span(block_id * 256, 256)
                for which, target in ((half, R.up.at[(layer,) + own]), (1 - half, R.stage.at[layer])):
                    pairs.append((R.own_up.at[:, span((2 * block_id + which) * 256, 256)], target.at[:, to]))
            return pairs
        if kind == DOWN:
            return [(R.own_down.at[:, cols], R.down.at[(layer,) + own[:-1] + (slice(None), cols)])]
        return [(getattr(R, "own_" + kind).at[:, cols], getattr(R, kind).at[(layer,) + own + (slice(None), cols)])]

    def first_local(u, layer):
        return [
            pltpu.make_async_copy(s, t, R.local_sem.at[u, i])
            for i, (s, t) in enumerate(first_pairs(u, layer, core))
        ]

    def first_remote(u, layer):
        return [
            remote(s, t, R.first_send.at[u, i], R.first_recv.at[u, i], sibling)
            for i, (s, t) in enumerate(first_pairs(u, layer, 1 - core))
        ]

    def chain(v):
        layer, u = v // NU, v % NU
        kind, block = KINDS[u]
        cols = unit_columns(u, core)
        moves = []
        if kind == UP:
            moves.append((R.stage.at[layer, :, cols], R.up.at[(layer,) + own + (slice(None), cols)], mate))
        order = gather_order(dims, v)
        known = dims - 1 if kind == DOWN else dims
        free = {dims - 1} if kind == UP else set()
        for k in range(len(order) + 1):
            gathered = set(order[:k]) | free
            where = tuple(slice(None) if i in gathered else bits[i] for i in range(known))
            ref = getattr(R, kind).at[(layer,) + where + (slice(None), cols)]
            moves.append((ref, ref, partners[order[k]] if k < len(order) else sibling))
        return [remote(s, t, R.send.at[v, i], R.recv.at[v, i], d) for i, (s, t, d) in enumerate(moves)]

    def small_step(k):
        where = tuple(slice(None) if i < k else bits[i] for i in range(dims))
        ref = R.small_all.at[(core,) + where]
        return remote(ref, ref, R.small_send.at[k], R.small_recv.at[k], partners[k] if k < dims else sibling)

    def pack_small():
        vec_lanes, vec_group, bias_lanes, bias_group, bias_rows = small_layout(count)
        here = lax.axis_index(DP)

        def put(values, at, group):
            if group == 1:
                return values
            return jnp.concatenate([jnp.where(at == i, values, 0.0) for i in range(group)], axis=1)

        tile = R.tile
        tile[...] = jnp.zeros_like(tile)
        tile[0:10, :] = put(R.vectors[0].astype(WIDE), lax.rem(here, vec_group), vec_group)
        bias = put(R.up_bias[...].astype(WIDE), lax.rem(lax.div(here, 2), bias_group), bias_group)
        for i in range(bias_rows):
            tile[10 + i : 11 + i, :] = bias[:, i * 128 : (i + 1) * 128]
        R.small_all[(core,) + own] = tile[...].astype(LOW)

    for copy in own_loads:
        copy.wait()
    for layer in range(2):

        @pl.when(core == layer)
        def _():
            for u in range(NU):
                for copy in first_remote(u, layer) + first_local(u, layer):
                    copy.start()

    pack_small()

    def arrive(v):
        layer, u = v // NU, v % NU

        @pl.when(core == layer)
        def _():
            for copy in first_local(u, layer):
                copy.wait()
            for copy in first_remote(u, layer):
                copy.wait_send()

        @pl.when(core != layer)
        def _():
            for copy in first_remote(u, layer):
                copy.wait_recv()

    length = R.lengths[core]
    vecs, biases = R.vecs, R.biases
    first_head, second_head = head_masks()

    def assemble():
        vec_lanes, vec_group, bias_lanes, bias_group, bias_rows = small_layout(count)
        small = R.small_all

        def shard(layer, d):
            return small[(layer,) + tuple((d >> (dims - 1 - i)) & 1 for i in range(dims))].astype(WIDE)

        def half_shard(layer, b):
            lead = tuple((b >> (dims - 2 - i)) & 1 for i in range(dims - 1))
            return small[(layer,) + lead + (half,)].astype(WIDE)

        for layer in range(2):
            for t in range(D // 128):
                vecs[layer, :, t * 128 : (t + 1) * 128] = sum(
                    shard(layer, d) for d in range(t * vec_group, (t + 1) * vec_group)
                )
            for t in range(count // 2 // bias_group):
                tile = sum(half_shard(layer, b) for b in range(t * bias_group, (t + 1) * bias_group))
                for i in range(bias_rows):
                    at = (t * bias_rows + i) * 128
                    biases[layer, 0:1, at : at + 128] = tile[10 + i : 11 + i, :]

    save_queue = []

    def save(name, layer):
        copy = pltpu.make_async_copy(
            getattr(saved, name)[layer], getattr(R, S + name).at[layer], R.save_sem.at[layer, SAVED.index(name)]
        )
        copy.start()
        save_queue.append(copy)

    def vec(layer, i, cols=slice(None)):
        return vecs[layer, i : i + 1, cols]

    def load_weight(v):
        layer, u = v // NU, v % NU
        kind, block = KINDS[u]
        if kind == DOWN:
            flat = R.down_flat.at[layer, :, pl.ds(block * DOWN_WIDE, DOWN_WIDE)]
            target = R.w_low.at[:, pl.ds(block * DOWN_WIDE, DOWN_WIDE)]
        else:
            flat = getattr(R, kind + FLAT).at[layer, :, pl.ds(block * 1024, 1024)]
            target = R.w_slots.at[u]
        return pltpu.make_async_copy(flat, target, R.weight_sem.at[u])

    def first_norm(layer):
        def rows(i):
            at = span(i * 32, 32)
            normed, unused = norm_parts(saved.x[layer][at, :].astype(WIDE))
            saved.a[layer][at, :] = (normed * vec(layer, 0) + vec(layer, 1)).astype(LOW)

        for_each(SEQ // 32, rows)
        save(N.x, layer)
        save(N.a, layer)

    def project(layer, block):
        target = (saved.q, saved.k, saved.v)[block][layer]
        weight = R.w_slots.at[block]

        def columns(n):
            at = span(n * 256, 256)
            values = dot(saved.a[layer][...], weight[:, at])
            if block == 0:
                values = (values + vec(layer, 2, at)).astype(LOW) * SCALE
            elif block == 2:
                values = values + vec(layer, 3, at)
            target[:, at] = values.astype(LOW)

        for_each(D // 256, columns)
        save((N.q, N.k, N.v)[block], layer)

    def attention(layer):
        key_ids = lax.broadcasted_iota(jnp.int32, (SEQ, SEQ), 0)
        query_ids = lax.broadcasted_iota(jnp.int32, (SEQ, SEQ), 1)
        blocked = jnp.where((key_ids <= query_ids) & (key_ids < length), 0.0, -1e30)

        def pair(n):
            at = span(n * 128, 128)
            query, key, value = (part[layer][:, at] for part in (saved.q, saved.k, saved.v))
            parts = []
            for i, mask in enumerate((first_head, second_head)):
                scores = dot(key, query * mask.astype(LOW), BY_COLUMNS) + blocked
                weights = jnp.exp(scores - jnp.max(scores, 0, keepdims=True))
                probs = (weights * (1.0 / jnp.sum(weights, 0, keepdims=True))).astype(LOW)
                saved.p[layer][2 * n + i] = probs
                parts.append(dot(probs, value, BY_ROWS) * mask)
            saved.o[layer][:, at] = (parts[0] + parts[1]).astype(LOW)

        for_each(HEADS // 2, pair)
        save(N.p, layer)
        save(N.o, layer)

    def send_c(layer):
        ref = saved.c[layer]
        return remote(ref.at[0], ref.at[1], R.act_send.at[layer, 0], R.act_recv.at[layer, 0], mate)

    def attend_out(layer):
        weight = R.w_slots.at[3]
        hidden = saved.h[layer]

        def columns(n):
            at = span(n * 256, 256)
            values = dot(saved.o[layer][...], weight[:, at])
            hidden[:, at] = saved.x[layer][:, at].astype(WIDE) + values + vec(layer, 4, at)

        for_each(D // 256, columns)

    def second_norm(layer):
        def rows(i):
            at = span(i * 32, 32)
            normed, unused = norm_parts(saved.h[layer][at, :])
            saved.c[layer][0, at, :] = (normed * vec(layer, 5) + vec(layer, 6)).astype(LOW)

        for_each(SEQ // 32, rows)
        save(N.h, layer)

    def feed_up(layer, block, who):
        weight = R.w_slots.at[4 + block]

        def columns(n):
            at = span(n * 256, 256)
            to = span(block * 1024 + n * 256, 256)
            value = dot(saved.c[layer][who], weight[:, at]) + biases[layer, 0:1, to]
            share = 0.5 + 0.5 * lax.erf(value * 0.7071067811865476)
            slope = share + value * (jnp.exp(value * value * -0.5) * 0.3989422804014327)
            saved.g[layer][who, :, to] = (value * share).astype(LOW)
            saved.gp[layer][who, :, to] = slope.astype(LOW)

        for_each(4, columns)
        if block == 1 and who == 1:
            save(N.g, layer)
            save(N.gp, layer)

    def send_part(layer, block):
        at = pl.ds(block * DOWN_WIDE, DOWN_WIDE)
        return remote(
            R.part.at[layer, 0, :, at],
            R.part.at[layer, 1, :, at],
            R.act_send.at[layer, 1 + block],
            R.act_recv.at[layer, 1 + block],
            mate,
        )

    def down_theirs(layer, block):
        at = pl.ds(block * DOWN_WIDE, DOWN_WIDE)
        R.part[layer, 0, :, at] = dot(saved.g[layer][1], R.w_low[:, at]).astype(LOW)

    def down_mine(layer, block):
        at = pl.ds(block * DOWN_WIDE, DOWN_WIDE)
        values = dot(saved.g[layer][0], R.w_low[:, at])
        R.y[:, at] = saved.h[layer][:, at] + values + vec(layer, 7, at)

    def end(layer):
        def rows(i):
            at = span(i * 32, 32)
            valid = valid_rows(length, i * 32, 32)
            values = R.y[at, :] + R.part[layer, 1, at, :].astype(WIDE)
            if layer == 0:
                saved.x[1][at, :] = (values * valid).astype(LOW)
            else:
                R.y[at, :] = values
                normed, unused = norm_parts(values)
                R.z[at, :] = (normed * vec(1, 8) + vec(1, 9)) * valid

        for_each(SEQ // 32, rows)

    def weight(layer, u):
        load_weight(layer * NU + u).wait()

    def wait_parts(layer):
        for block in range(PARTS):
            send_part(layer, block).wait()

    def wait_c(layer):
        send_c(layer).wait()
        save(N.c, layer)

    pieces = [
        (first_norm, None),
        (lambda layer: project(layer, 0), 0),
        (lambda layer: project(layer, 1), 1),
        (lambda layer: project(layer, 2), 2),
        (attention, None),
        (attend_out, 3),
        (second_norm, None),
        (lambda layer: send_c(layer).start(), None),
        (lambda layer: feed_up(layer, 0, 0), 4),
        (lambda layer: feed_up(layer, 1, 0), 5),
        (wait_c, None),
        (lambda layer: feed_up(layer, 0, 1), None),
        (lambda layer: feed_up(layer, 1, 1), None),
    ]
    for block in range(PARTS):
        pieces.append((functools.partial(lambda block, layer: down_theirs(layer, block), block), 6 + block))
        pieces.append((functools.partial(lambda block, layer: send_part(layer, block).start(), block), None))
        pieces.append((functools.partial(lambda block, layer: down_mine(layer, block), block), None))
    pieces += [(wait_parts, None), (end, None)]

    chains = [chain(v) for v in range(total)]

    def plain_schedule():
        moves = []
        for v in range(total):
            for i in range(len(chains[v])):
                left = len(chains[v]) - 1 - i
                lag = GATHER_LAGS[left] if left < len(GATHER_LAGS) else GATHER_LAGS[-1] - left + len(GATHER_LAGS) - 1
                moves.append((v + (lag if i else min(GATHER_FIRST, lag)), -i, v))
            moves.append((v + GATHER_READY, -99, v))
        codes = [16 * v - i if i > -99 else 16 * v + 15 for unused, i, v in sorted(moves)]
        for k in range(dims + 2):
            codes.insert(6 * k, 2000 + k)
        result, done = [], set()
        jobs = [(layer, w) for layer in range(2) for w in range(len(pieces))]
        for code in codes:
            result.append(code)
            done.add(code)
            while jobs and 2000 + dims + 1 in done:
                layer, w = jobs[0]
                u = pieces[w][1]
                if u is not None and 16 * (layer * NU + u) + 15 not in done:
                    break
                result.append(3000 + 30 * layer + w)
                jobs.pop(0)
        return result

    load_x.wait()
    for code in SCHEDULE if dims == 4 and SCHEDULE else plain_schedule():
        if code >= 3000:
            layer, w = (code - 3000) // 30, (code - 3000) % 30
            if pieces[w][1] is not None:
                weight(layer, pieces[w][1])
            pieces[w][0](layer)
        elif code >= 2000:
            k = code - 2000
            if k > 0:
                small_step(k - 1).wait()
            if k <= dims:
                small_step(k).start()
            else:
                assemble()
        elif code % 16 == 15:
            v = code // 16
            chains[v][-1].wait()
            load_weight(v).start()
        else:
            v, i = code // 16, code % 16
            if i == 0:
                arrive(v)
            else:
                chains[v][i - 1].wait()
            chains[v][i].start()

    last = [(R.y, R.s_y, 0), (R.z, R.s_z, 1), (R.vecs, R.s_vecs, 2)]
    for source, target, i in last:
        pltpu.make_async_copy(source, target, R.last_sem.at[i]).start()
    for copy in save_queue:
        copy.wait()
    for source, target, i in last:
        pltpu.make_async_copy(source, target, R.last_sem.at[i]).wait()


def forward(shards, hidden, vectors, up_bias, lengths, dims):
    rows = D // 2**dims
    bits = (2,) * dims
    outs = dict(
        qkv=((2,) + bits + (rows, 3 * D), LOW),
        out=((2,) + bits + (rows, D), LOW),
        up=((2,) + bits + (rows, FF // 2), LOW),
        down=((2,) + bits[:-1] + (4 * rows, D), LOW),
        stage=((2, rows, FF // 2), LOW),
    )
    for name, (shape, dtype) in saved_shapes().items():
        outs[S + name] = ((2,) + shape, dtype)
    outs[S + N.y] = ((SEQ, D), WIDE)
    outs[S + "z"] = ((SEQ, D), WIDE)
    outs[S + N.vecs] = ((2, 16, D), WIDE)
    dma = pltpu.SemaphoreType.DMA
    total = 2 * NU
    scratch = dict(
        small_all=pltpu.VMEM((2,) + bits + (16, 128), LOW),
        vecs=pltpu.VMEM((2, 16, D), WIDE),
        biases=pltpu.VMEM((2, 8, FF // 2), WIDE),
        w_slots=pltpu.VMEM((6, D, D), LOW),
        w_low=pltpu.VMEM((FF // 2, D), LOW),
        part=pltpu.VMEM((2, 2, SEQ, D), LOW),
        y=pltpu.VMEM((SEQ, D), WIDE),
        z=pltpu.VMEM((SEQ, D), WIDE),
        local_sem=dma((NU, 4)),
        first_send=dma((NU, 4)),
        first_recv=dma((NU, 4)),
        send=dma((total, dims + 2)),
        recv=dma((total, dims + 2)),
        small_send=dma((dims + 1,)),
        small_recv=dma((dims + 1,)),
        io=dma((5,)),
        tile=pltpu.VMEM((16, 128), WIDE),
        own_qkv=pltpu.VMEM((rows, 3 * D), LOW),
        own_out=pltpu.VMEM((rows, D), LOW),
        own_up=pltpu.VMEM((rows, FF), LOW),
        own_down=pltpu.VMEM((4 * rows, D), LOW),
        save_sem=dma((2, len(SAVED))),
        weight_sem=dma((NU,)),
        act_send=dma((2, 1 + PARTS)),
        act_recv=dma((2, 1 + PARTS)),
        last_sem=dma((3,)),
    )
    for name, (shape, dtype) in saved_shapes().items():
        for layer in range(2):
            scratch[name + str(layer)] = pltpu.VMEM(shape, dtype)
    names = FORWARD_IN + list(outs) + list(scratch)

    def kernel(*refs):
        by_name = dict(zip(names, refs))
        extra = dict(
            qkv_flat=by_name[QKV].reshape(2, D, 3 * D),
            out_flat=by_name[OUT].reshape(2, D, D),
            up_flat=by_name[UP].reshape(2, D, FF // 2),
            down_flat=by_name[DOWN].reshape(2, FF // 2, D),
        )
        forward_kernel(dims, names + list(extra), *refs, *extra.values())

    anywhere = pl.BlockSpec(memory_space=pl.ANY)
    whole = pl.BlockSpec(memory_space=pltpu.VMEM)
    results = pl.pallas_call(
        kernel,
        out_shape=[jax.ShapeDtypeStruct(s, t) for s, t in outs.values()],
        in_specs=[anywhere] * 5 + [whole] * 2 + [pl.BlockSpec(memory_space=pltpu.SMEM)],
        out_specs=[anywhere] * len(outs),
        scratch_shapes=list(scratch.values()),
        compiler_params=pltpu.CompilerParams(collective_id=1, has_side_effects=True, vmem_limit_bytes=60 << 20),
        name="forward",
    )(*shards, hidden, vectors, up_bias, lengths)
    return dict(zip(outs, results))


BACK_PARTS = 2
BACK_WIDE = D // BACK_PARTS
BACK = [(DOWN, i) for i in range(BACK_PARTS)] + [(UP, 0), (UP, 1), (OUT, 0), (QKV, 0), (QKV, 1), (QKV, 2)]
NB = len(BACK)
SCATTER_LAGS = [1, 3, 4, 5, 6]
BACK_ORDERS = [
    (0, 1, 2), (2, 0, 1), (0, 1, 2), (0, 1, 2),
    (0, 1, 2, 3), (0, 1, 2, 3), (0, 1, 3, 2), (0, 1, 2, 3),
]
BACK_SCHEDULE = [
    3000, 3001, 3003, 3002, 3004, 3005, 0, 3006, 3008, 3009, 3010, 3007, 3012, 16, 3011, 32, 1, 3013, 3014, 3015,
    3016, 48, 17, 64, 3017, 3018, 33, 3019, 80, 3020, 3022, 3023, 2, 65, 49, 3030, 3033, 3031, 18, 34,
    3021, 3032, 81, 66, 112, 3, 19, 96, 3034, 50, 3035, 35, 82, 67, 3036, 3037, 144, 128, 51, 3038,
    113, 3039, 3040, 68, 97, 52, 36, 83, 3041, 3042, 145, 3043, 176, 160, 3044, 114, 3045, 3046, 98, 84,
    192, 3047, 115, 129, 3048, 3049, 99, 177, 208, 100, 193, 116, 3050, 130, 3051, 161, 224, 178, 240, 3052,
    3053, 194, 4000, 2000, 209, 162, 225, 195, 241, 2001, 210, 163, 226, 146, 2002, 211, 196, 131, 242, 227,
    179, 180, 212, 147, 243, 164, 2003, 2004, 228, 244,
]
HELD, B, TILE = "held", "b_", "tile"
BACK_WEIGHTS = [QKV, OUT, UP, DOWN]
BACK_IN = BACK_WEIGHTS + [S + n for n in SAVED + ["y", "z", "vecs"]] + ["out_grad", "lengths"]


def back_order(dims, u):
    return BACK_ORDERS[u] if dims == 4 else axis_order(dims, KINDS.index(BACK[u]))


def box_name(u, k):
    return "box%d_%d" % (u, k)


def backward_kernel(dims, names, *refs):
    R = SimpleNamespace(**dict(zip(names, refs)))
    core, bits, partners, sibling = place(dims)
    own = tuple(bits)
    half = bits[-1]
    mate = partners[-1]
    greet([sibling] + partners)
    total = 2 * NB
    count = 2**dims
    length = R.lengths[core]
    vecs, grads = R.vecs, R.grads
    first_head, second_head = head_masks()

    def load(name, layer):
        if name == N.y:
            source = R.s_y
        elif name == N.og:
            source = R.out_grad.at[core, 0]
        elif name == N.vecs:
            source = R.s_vecs
        elif name in (N.w_down, N.w_up, N.w_qkv, N.w_out):
            source = getattr(R, name[2:] + FLAT).at[layer]
        else:
            source = getattr(R, S + name).at[layer]
        if name == N.vecs:
            target = vecs
        elif name == N.w_up:
            target = R.b_w_wide.at[:, pl.ds(0, FF // 2)]
        elif name == N.w_qkv:
            target = R.b_w_wide
        else:
            target = getattr(R, B + name)
        return pltpu.make_async_copy(source, target, R.load_sem.at[LOADS.index(name)])

    def need(layer, *which):
        for name in which:
            load(name, layer).wait()

    def again(layer, *which):
        if layer == 1:
            for name in which:
                load(name, 0).start()

    def unit_of(v):
        return 1 - v // NB, BACK[v % NB]

    def columns_of(v, column_half):
        kind, block = BACK[v % NB]
        if kind == DOWN:
            return span(block * BACK_WIDE + column_half * (BACK_WIDE // 2), BACK_WIDE // 2)
        return span(block * 1024 + column_half * 512, 512)

    def order_of(v):
        return tuple(reversed(back_order(dims, v % NB)))

    def held(v):
        return getattr(R, HELD + str(v % NB))

    def box(v, k):
        if k == 0:
            kind, block = BACK[v % NB]
            return (R.down_box if kind == DOWN else R.wide_box).at[v % 2]
        return getattr(R, box_name(v % NB, k))

    def stage(v):
        kind, block = BACK[v % NB]
        return (R.down_stage if kind == DOWN else R.wide_stage).at[v % 2]

    def is_up(v):
        return BACK[v % NB][0] == UP

    def steps(v):
        return len(order_of(v)) + (1 if is_up(v) else 0)

    def where(v, k, away):
        order = order_of(v)
        place_of = []
        for i in range(dims - 1 if BACK[v % NB][0] == DOWN else dims):
            if i in order[: max(k - 1, 0)]:
                place_of.append(bits[i])
            elif 0 < k <= len(order) and i == order[k - 1]:
                place_of.append(1 - bits[i] if away else bits[i])
            elif k > len(order) and i == dims - 1:
                place_of.append(1 - half if away else half)
            elif k > len(order):
                place_of.append(bits[i])
            else:
                place_of.append(slice(None))
        return tuple(place_of)

    def device_of(v, k):
        if k == 0:
            return sibling
        return partners[order_of(v)[k - 1]] if k <= len(order_of(v)) else mate

    def move(v, k):
        source = stage(v) if k == 0 else held(v).at[where(v, k, True)]
        return remote(source, box(v, k), R.send.at[v, k], R.recv.at[v, k], device_of(v, k))

    def earlier(v, k):
        if k > 0:
            return v - NB if v >= NB else None
        low = BACK[v % NB][0] == DOWN
        same = [w for w in range(v) if (BACK[w % NB][0] == DOWN) == low and w % 2 == v % 2]
        return same[-1] if same else None

    def later(v, k):
        return any(earlier(w, k) == v for w in range(v + 1, total))

    def begin(v, k):
        if earlier(v, k) is not None:
            pl.semaphore_wait(R.credit.at[v % NB, k], 1)
        move(v, k).start()

    def consumed(v, k):
        for w in range(v + 1, total):
            if earlier(w, k) == v:
                pl.semaphore_signal(
                    R.credit.at[w % NB, k], inc=1, device_id=device_of(v, k), device_id_type=MESH
                )

    def finals(v):
        kind, block = BACK[v % NB]
        cols = columns_of(v, core)
        if kind == UP:
            pairs = []
            for i in range(2):
                block_id = block * 4 + core * 2 + i
                part = (slice(None), pl.ds(i * 256, 256))
                for which, source in ((half, held(v).at[own + part]), (1 - half, box(v, dims).at[part])):
                    pairs.append((source, R.g_up.at[:, span((2 * block_id + which) * 256, 256)]))
            return pairs
        if kind == DOWN:
            return [(held(v).at[own[:-1]], R.g_down.at[:, cols])]
        return [(held(v).at[own], getattr(R, "g_" + kind).at[:, cols])]

    def final_local(v):
        return [
            pltpu.make_async_copy(s, t, R.out_sem.at[v, i]) for i, (s, t) in enumerate(finals(v))
        ]

    def final_remote(v):
        return [
            remote(s, t, R.end_send.at[v, i], R.end_recv.at[v, i], sibling)
            for i, (s, t) in enumerate(finals(v))
        ]

    def finish(v):
        @pl.when(core == unit_of(v)[0])
        def _():
            for copy in final_local(v):
                copy.start()

        @pl.when(core != unit_of(v)[0])
        def _():
            for copy in final_remote(v):
                copy.start()

    def finished(v):
        @pl.when(core == unit_of(v)[0])
        def _():
            for copy in final_local(v):
                copy.wait()

        @pl.when(core != unit_of(v)[0])
        def _():
            for copy in final_remote(v):
                copy.wait_send()
        if is_up(v):
            consumed(v, dims)

    def event(v, k):
        move(v, k).wait()
        if not (is_up(v) and k == steps(v)):
            view = held(v).at[where(v, k, False)]
            view[...] = view[...] + box(v, k)[...]
            consumed(v, k)
        if k < steps(v):
            begin(v, k + 1)
        else:
            finish(v)

    def vec(layer, i):
        return vecs[layer, i : i + 1, :]

    def collect(layer, i, values):
        grads[layer, i : i + 1, :] = grads[layer, i : i + 1, :] + jnp.sum(values, 0, keepdims=True)

    def send_e(layer, block):
        ref = R.e.at[layer]
        at = pl.ds(block * BACK_WIDE, BACK_WIDE)
        send, recv = R.act_send.at[layer, 1 + block], R.act_recv.at[layer, 1 + block]
        return remote(ref.at[0, :, at], ref.at[1, :, at], send, recv, mate)

    def send_dc(layer):
        ref = R.dc_part
        return remote(ref.at[0], ref.at[1], R.act_send.at[layer, 0], R.act_recv.at[layer, 0], mate)

    def top(layer):
        if layer == 1:
            need(1, N.vecs, N.og, N.y)

        def rows(i):
            at = span(i * 32, 32)
            valid = valid_rows(length, i * 32, 32)
            if layer == 1:
                grad_z = R.b_og[at, :].astype(WIDE) * valid
                normed, factor = norm_parts(R.b_y[at, :])
                collect(1, 8, grad_z * normed)
                collect(1, 9, grad_z)
                grad_y = norm_back(grad_z * vec(1, 8), normed, factor)
            else:
                grad_y = R.dx[at, :].astype(WIDE) * valid
            R.dy[at, :] = grad_y
            branch = grad_y.astype(LOW)
            R.e[layer, 0, at, :] = branch
            collect(layer, 7, branch.astype(WIDE))

        for_each(SEQ // 32, rows)

    def produce(v, body, quarter_shape):
        for target, column_half in ((stage(v), 1 - core), (held(v), core)):
            cols = columns_of(v, column_half)

            def quarter(i):
                target[lax.div(i, 2), lax.rem(i, 2)] = body(i, cols).astype(LOW).reshape(quarter_shape)

            for_each(4, quarter)
            if column_half is not core:
                begin(v, 0)

    def pair_rows(ref, cols):
        values = ref[:, :, cols]
        return values.reshape(2 * SEQ, values.shape[-1])

    inner = (2,) * (dims - 2) + (D // count, 512)
    down_inner = (2,) * (dims - 3) + (FF // count, BACK_WIDE // 2)

    def grad_down(layer, v, block):
        if block == 0:
            need(layer, N.g)
        produce(
            v,
            lambda i, cols: dot(pair_rows(R.b_g, span(i * 512, 512)), pair_rows(R.e.at[layer], cols), BY_ROWS),
            down_inner,
        )
        if block == BACK_PARTS - 1:
            again(layer, N.g)

    def feed_hidden(layer, who):
        if who == 0:
            need(layer, N.w_down, N.gp)

        def hidden(n):
            at = span(n * 256, 256)
            grad_act = dot(R.e[layer, who], R.b_w_down[at, :], BY_COLUMNS)
            grad_upper = (grad_act * R.b_gp[who, :, at].astype(WIDE)).astype(LOW)
            R.b_gp[who, :, at] = grad_upper
            sums = jnp.sum(grad_upper.astype(WIDE), 0, keepdims=True)
            R.bias_grads[layer, 0:1, at] = sums if who == 0 else R.bias_grads[layer, 0:1, at] + sums

        for_each(FF // 2 // 256, hidden)
        if who == 1:
            again(layer, N.w_down)

    def feed_theirs(layer):
        need(layer, N.w_up)

        def theirs(n):
            at = span(n * 256, 256)
            R.dc_part[0, :, at] = dot(R.b_gp[1], R.b_w_wide[at, pl.ds(0, FF // 2)], BY_COLUMNS).astype(LOW)

        for_each(D // 256, theirs)

    def feed_mine(layer):
        def mine(n):
            at = span(n * 256, 256)
            R.dc[:, at] = dot(R.b_gp[0], R.b_w_wide[at, pl.ds(0, FF // 2)], BY_COLUMNS)

        for_each(D // 256, mine)
        load(N.w_qkv, layer).start()

    def grad_up(layer, v, block):
        if block == 0:
            need(layer, N.c)

        def body(i, cols):
            return dot(pair_rows(R.b_c, span(i * 256, 256)), pair_rows(R.b_gp, cols), BY_ROWS)

        produce(v, body, inner)
        if block == 1:
            again(layer, N.c, N.gp)

    def middle(layer):
        need(layer, N.h)

        def rows(i):
            at = span(i * 32, 32)
            grad_in = R.dc[at, :] + R.dc_part[1, at, :].astype(WIDE)
            normed, factor = norm_parts(R.b_h[at, :])
            collect(layer, 5, grad_in * normed)
            collect(layer, 6, grad_in)
            grad_hidden = R.dy[at, :] + norm_back(grad_in * vec(layer, 5), normed, factor)
            R.dy[at, :] = grad_hidden
            branch = grad_hidden.astype(LOW)
            R.f[at, :] = branch
            collect(layer, 4, branch.astype(WIDE))

        for_each(SEQ // 32, rows)
        again(layer, N.h)

    def grad_out(layer, v):
        need(layer, N.o)
        produce(v, lambda i, cols: dot(R.b_o[:, span(i * 256, 256)], R.f[:, cols], BY_ROWS), inner)
        again(layer, N.o)

    def grad_mixed(layer):
        need(layer, N.w_out)

        def columns(n):
            at = span(n * 256, 256)
            R.do[:, at] = dot(R.f[...], R.b_w_out[at, :], BY_COLUMNS).astype(LOW)

        for_each(D // 256, columns)
        again(layer, N.w_out)

    def attention_back(layer):
        need(layer, N.q, N.k, N.v, N.p)

        def pair(n):
            at = span(n * 128, 128)
            query, key, value, grad_o = R.b_q[:, at], R.b_k[:, at], R.b_v[:, at], R.do[:, at]
            sums = [0.0, 0.0, 0.0]
            for i, mask in enumerate((first_head.astype(LOW), second_head.astype(LOW))):
                probs = R.b_p[2 * n + i]
                grad_head = grad_o * mask
                wide = probs.astype(WIDE)
                grad_probs = dot(value, grad_head, BY_COLUMNS)
                shift = jnp.sum(grad_probs * wide, 0, keepdims=True)
                grad_scores = (wide * (grad_probs - shift)).astype(LOW)
                sums[0] += dot(grad_scores, key * mask, BY_ROWS)
                sums[1] += dot(grad_scores, query * mask)
                sums[2] += dot(probs, grad_head)
            sums[0] = sums[0] * SCALE
            for j in range(3):
                low = sums[j].astype(LOW)
                R.dp[:, pl.ds(pl.multiple_of(n * 128 + j * D, 128), 128)] = low
                if j != 1:
                    row = 2 if j == 0 else 3
                    grads[layer, row : row + 1, at] = jnp.sum(low.astype(WIDE), 0, keepdims=True)

        for_each(HEADS // 2, pair)
        again(layer, N.q, N.k, N.v, N.p)

    def grad_qkv(layer, v, block):
        if block == 0:
            need(layer, N.a)
        produce(v, lambda i, cols: dot(R.b_a[:, span(i * 256, 256)], R.dp[:, cols], BY_ROWS), inner)
        if block == 2:
            again(layer, N.a)

    def grad_attn_in(layer):
        need(layer, N.w_qkv)

        def columns(n):
            at = span(n * 256, 256)
            R.dc[:, at] = dot(R.dp[...], R.b_w_wide[at, :], BY_COLUMNS)

        for_each(D // 256, columns)
        again(layer, N.w_up)

    def bottom(layer):
        need(layer, N.x)

        def rows(i):
            at = span(i * 32, 32)
            grad_in = R.dc[at, :]
            normed, factor = norm_parts(R.b_x[at, :].astype(WIDE))
            collect(layer, 0, grad_in * normed)
            collect(layer, 1, grad_in)
            grad_x = R.dy[at, :] + norm_back(grad_in * vec(layer, 0), normed, factor)
            if layer == 1:
                R.dx[at, :] = grad_x.astype(LOW)
            else:
                R.b_y[at, :] = grad_x

        for_each(SEQ // 32, rows)
        again(layer, N.x)

    def spread():
        vec_lanes, vec_group, bias_lanes, bias_group, bias_rows = small_layout(count)
        tiles = R.tiles
        tiles[...] = jnp.zeros_like(tiles)
        for layer in range(2):
            for d in range(count):
                lead = tuple((d >> (dims - 1 - i)) & 1 for i in range(dims))
                t = d // vec_group
                tiles[(layer,) + lead + (slice(0, 10),)] = grads[layer, 0:10, t * 128 : (t + 1) * 128]
            for b in range(count // 2):
                lead = tuple((b >> (dims - 2 - i)) & 1 for i in range(dims - 1))
                for i in range(bias_rows):
                    at = (b // bias_group * bias_rows + i) * 128
                    tiles[(layer,) + lead + (half, slice(10 + i, 11 + i))] = R.bias_grads[layer, 0:1, at : at + 128]

    def tile_box(k):
        return getattr(R, TILE + str(k))

    def small_move(k):
        if k == 0:
            return remote(
                R.tiles.at[1 - core], tile_box(0), R.small_send.at[0], R.small_recv.at[0], sibling
            )
        lead = own[: k - 1] + (1 - bits[k - 1],)
        return remote(
            R.tiles.at[(core,) + lead],
            tile_box(k),
            R.small_send.at[k],
            R.small_recv.at[k],
            partners[k - 1],
        )

    def small_event(k):
        small_move(k).wait()
        lead = own[:k]
        view = R.tiles.at[(core,) + lead]
        view[...] = view[...] + tile_box(k)[...]
        if k < dims:
            small_move(k + 1).start()
        else:
            pltpu.make_async_copy(view, R.g_small, R.edge_sem.at[2]).start()

    for name in (N.vecs, N.og, N.y, N.g, N.w_down, N.gp, N.w_up, N.c, N.h, N.o, N.w_out, N.q, N.k, N.v, N.p, N.x, N.a):
        load(name, 1).start()
    grads[...] = jnp.zeros_like(grads)
    edge_local = pltpu.make_async_copy(R.b_y, R.mine, R.edge_sem.at[0])
    edge_remote = [remote(ref, R.theirs, R.edge_send.at[0], R.edge_recv.at[0], sibling) for ref in (R.s_z, R.b_y)]

    @pl.when(core == 0)
    def _():
        edge_remote[0].start()

    def last(layer):
        edge_local.start()

        @pl.when(core == 1)
        def _():
            edge_remote[1].start()

        spread()
        small_move(0).start()

    def unit(layer, u):
        return (1 - layer) * NB + u

    def start_e(block, layer):
        send_e(layer, block).start()

    def wait_e(block, layer):
        send_e(layer, block).wait()

    def down(block, layer):
        grad_down(layer, unit(layer, block), block)

    pieces = [(top, None)]
    pieces += [(functools.partial(start_e, i), None) for i in range(BACK_PARTS)]
    pieces.append((lambda layer: feed_hidden(layer, 0), None))
    for i in range(BACK_PARTS):
        pieces += [(functools.partial(wait_e, i), None), (functools.partial(down, i), i)]
    pieces += [
        (lambda layer: feed_hidden(layer, 1), None),
        (feed_theirs, None),
        (lambda layer: send_dc(layer).start(), None),
        (feed_mine, None),
        (lambda layer: grad_up(layer, unit(layer, BACK_PARTS), 0), BACK_PARTS),
        (lambda layer: grad_up(layer, unit(layer, BACK_PARTS + 1), 1), BACK_PARTS + 1),
        (lambda layer: send_dc(layer).wait(), None),
        (middle, None),
        (lambda layer: grad_out(layer, unit(layer, BACK_PARTS + 2)), BACK_PARTS + 2),
        (grad_mixed, None),
        (attention_back, None),
        (lambda layer: grad_qkv(layer, unit(layer, BACK_PARTS + 3), 0), BACK_PARTS + 3),
        (lambda layer: grad_qkv(layer, unit(layer, BACK_PARTS + 4), 1), BACK_PARTS + 4),
        (lambda layer: grad_qkv(layer, unit(layer, BACK_PARTS + 5), 2), BACK_PARTS + 5),
        (grad_attn_in, None),
        (bottom, None),
    ]

    def plain_schedule():
        timed = []
        for v in range(total):
            for k in range(steps(v) + 1):
                lag = SCATTER_LAGS[k] if k < len(SCATTER_LAGS) else SCATTER_LAGS[-1] + (k - len(SCATTER_LAGS) + 1) / 8
                timed.append((v + lag, 0, -k, v))
            timed.append((v, 1, 0, v))
        result = []
        for turn in range(2):
            at = -1.0
            for w, (unused, u) in enumerate(pieces):
                at = max(at + 0.01, turn * NB + (u or 0))
                timed.append((at, 1, w, (turn, w)))
        codes = []
        for key, is_compute, k, v in sorted(timed, key=lambda item: item[:3]):
            if not is_compute:
                codes.append(16 * v - k)
            elif isinstance(v, tuple):
                codes.append(3000 + 30 * v[0] + v[1])
        codes.append(4000)
        return codes + [2000 + k for k in range(dims + 1)]

    for code in BACK_SCHEDULE if dims == 4 and BACK_SCHEDULE else plain_schedule():
        if code >= 4000:
            last(0)
        elif code >= 3000:
            turn, w = (code - 3000) // 30, (code - 3000) % 30
            u = pieces[w][1]
            if turn == 1 and u is not None:
                finished(u)
            pieces[w][0](1 - turn)
        elif code >= 2000:
            small_event(code - 2000)
        else:
            event(code // 16, code % 16)
    for v in range(NB, total):
        finished(v)

    @pl.when(core == 0)
    def _():
        edge_remote[0].wait_send()

    @pl.when(core == 1)
    def _():
        edge_remote[1].wait_send()

    edge_local.wait()
    edge_remote[0].wait_recv()
    pltpu.make_async_copy(R.tiles.at[(core,) + own], R.g_small, R.edge_sem.at[2]).wait()
    for layer in range(2):

        @pl.when(core == layer)
        def _():
            for v in range((1 - layer) * NB, (2 - layer) * NB):
                for copy in final_remote(v):
                    copy.wait_recv()


def backward(left, out_grad, lengths, dims):
    rows = D // 2**dims
    bits = (2,) * dims
    outs = dict(
        g_qkv=((rows, 3 * D), LOW),
        g_out=((rows, D), LOW),
        g_up=((rows, FF), LOW),
        g_down=((4 * rows, D), LOW),
        g_small=((16, 128), WIDE),
        mine=((SEQ, D), WIDE),
        theirs=((SEQ, D), WIDE),
    )
    dma = pltpu.SemaphoreType.DMA
    total = 2 * NB
    vmem = lambda shape, dtype=LOW: pltpu.VMEM(shape, dtype)
    scratch = dict(
        vecs=vmem((2, 16, D), WIDE),
        grads=vmem((2, 16, D), WIDE),
        bias_grads=vmem((2, 8, FF // 2), WIDE),
        b_og=vmem((SEQ, D)),
        b_y=vmem((SEQ, D), WIDE),
        b_w_down=vmem((FF // 2, D)),
        b_w_wide=vmem((D, 3 * D)),
        b_w_out=vmem((D, D)),
        e=vmem((2, 2, SEQ, D)),
        dc_part=vmem((2, SEQ, D)),
        dc=vmem((SEQ, D), WIDE),
        dy=vmem((SEQ, D), WIDE),
        dx=vmem((SEQ, D)),
        f=vmem((SEQ, D)),
        do=vmem((SEQ, D)),
        dp=vmem((SEQ, 3 * D)),
        tiles=vmem((2,) + bits + (16, 128), WIDE),
        wide_stage=vmem((2,) + bits + (rows, 512)),
        wide_box=vmem((2,) + bits + (rows, 512)),
        down_stage=vmem((2,) + bits[:-1] + (4 * rows, BACK_WIDE // 2)),
        down_box=vmem((2,) + bits[:-1] + (4 * rows, BACK_WIDE // 2)),
        send=dma((total, dims + 1)),
        recv=dma((total, dims + 1)),
        credit=pltpu.SemaphoreType.REGULAR((NB, dims + 1)),
        out_sem=dma((total, 4)),
        end_send=dma((total, 4)),
        end_recv=dma((total, 4)),
        load_sem=dma((len(LOADS),)),
        act_send=dma((2, 1 + BACK_PARTS)),
        act_recv=dma((2, 1 + BACK_PARTS)),
        small_send=dma((dims + 1,)),
        small_recv=dma((dims + 1,)),
        edge_sem=dma((3,)),
        edge_send=dma((1,)),
        edge_recv=dma((1,)),
    )
    for k in range(dims + 1):
        scratch[TILE + str(k)] = vmem(bits[k:] + (16, 128), WIDE)
    for name, (shape, dtype) in saved_shapes().items():
        scratch[B + name] = vmem(shape, dtype)
    for u, (kind, block) in enumerate(BACK):
        piece = (4 * rows, BACK_WIDE // 2) if kind == DOWN else (rows, 512)
        lead = bits[:-1] if kind == DOWN else bits
        scratch[HELD + str(u)] = vmem(lead + piece)
        count = dims if kind in (QKV, OUT) else dims - 1
        for k in range(1, count + 1):
            scratch[box_name(u, k)] = vmem(lead[k:] + piece)
        if kind == UP:
            scratch[box_name(u, dims)] = vmem(piece)
    names = BACK_IN + list(outs) + list(scratch)

    def kernel(*refs):
        by_name = dict(zip(names, refs))
        extra = dict(
            qkv_flat=by_name[QKV].reshape(2, D, 3 * D),
            out_flat=by_name[OUT].reshape(2, D, D),
            up_flat=by_name[UP].reshape(2, D, FF // 2),
            down_flat=by_name[DOWN].reshape(2, FF // 2, D),
        )
        backward_kernel(dims, names + list(extra), *refs, *extra.values())

    anywhere = pl.BlockSpec(memory_space=pl.ANY)
    arguments = [left[n] for n in BACK_IN[:-2]] + [out_grad, lengths]
    results = pl.pallas_call(
        kernel,
        out_shape=[jax.ShapeDtypeStruct(s, t) for s, t in outs.values()],
        in_specs=[anywhere] * (len(arguments) - 1) + [pl.BlockSpec(memory_space=pltpu.SMEM)],
        out_specs=[anywhere] * len(outs),
        scratch_shapes=list(scratch.values()),
        compiler_params=pltpu.CompilerParams(collective_id=2, has_side_effects=True, vmem_limit_bytes=62 << 20),
        name="backward",
    )(*arguments)
    return SimpleNamespace(**dict(zip(outs, results)))


def finish_kernel(dims, *refs):
    sums, outs, low, wide, edges = refs[:8], refs[8:15], refs[15:20], refs[20:26], refs[26]
    sem = refs[27]
    core = lax.axis_index(PIPE)
    copies = [pltpu.make_async_copy(sums[i], low[i], sem.at[0, i]) for i in range(5)]
    theirs = pltpu.make_async_copy(sums[5], edges.at[1 - core], sem.at[0, 5])
    mine = [pltpu.make_async_copy(sums[6 + i], edges.at[core], sem.at[0, 6]) for i in range(2)]
    for copy in copies + [theirs]:
        copy.start()
    for i in range(2):

        @pl.when(core == i)
        def _():
            mine[i].start()

    writes = []
    for i in range(4):
        copies[i].wait()
        wide[i][...] = low[i][...].astype(WIDE)
        writes.append(pltpu.make_async_copy(wide[i], outs[i].at[0], sem.at[1, i]))
        writes[-1].start()
    theirs.wait()
    mine[0].wait()
    writes.append(pltpu.make_async_copy(edges, outs[6].at[0, :, 0], sem.at[1, 6]))
    writes[-1].start()
    copies[4].wait()
    small = low[4]
    vec_lanes, vec_group, bias_lanes, bias_group, bias_rows = small_layout(2**dims)
    here = lax.axis_index(DP)

    def pick(values, lanes, at, group):
        result = values[:, 0:lanes]
        for i in range(1, group):
            result = jnp.where(at == i, values[:, i * lanes : (i + 1) * lanes], result)
        return result

    wide[4][0] = pick(small[0:10, :], vec_lanes, lax.rem(here, vec_group), vec_group)
    if bias_group > 1:
        wide[5][...] = pick(small[10:11, :], bias_lanes, lax.rem(lax.div(here, 2), bias_group), bias_group)
    else:
        for i in range(bias_rows):
            wide[5][:, i * 128 : (i + 1) * 128] = small[10 + i : 11 + i, :]
    for i in range(4, 6):
        writes.append(pltpu.make_async_copy(wide[i], outs[i], sem.at[1, i]))
        writes[-1].start()
    for copy in writes:
        copy.wait()


def finish(sums, result, dims):
    count = 2**dims
    rows = D // count
    anywhere = pl.BlockSpec(memory_space=pl.ANY)
    shapes = [(rows, 3 * D), (rows, D), (rows, FF), (4 * rows, D)]
    small = [(1, 10, D // count), (1, FF // count)]
    outs = [(1,) + shape for shape in shapes] + small + [(1, 2, 1, SEQ, D)]
    return pl.pallas_call(
        functools.partial(finish_kernel, dims),
        out_shape=[jax.ShapeDtypeStruct(shape, WIDE) for shape in outs],
        in_specs=[anywhere] * 8,
        out_specs=[anywhere] * 7,
        scratch_shapes=[pltpu.VMEM(shape, LOW) for shape in shapes]
        + [pltpu.VMEM((16, 128), WIDE)]
        + [pltpu.VMEM(shape, WIDE) for shape in shapes + small]
        + [pltpu.VMEM((2, SEQ, D), WIDE), pltpu.SemaphoreType.DMA((2, 7))],
        compiler_params=pltpu.CompilerParams(vmem_limit_bytes=62 << 20),
        name="finish",
    )(sums.g_qkv, sums.g_out, sums.g_up, sums.g_down, sums.g_small, sums.theirs, sums.mine, result)


def regroup(values, outer, inner):
    lead = values.shape[:-1]
    values = values.reshape(lead + (-1, 2, inner))
    values = jnp.moveaxis(values, -2, -3).reshape(lead + (2, -1, outer))
    return jnp.moveaxis(values, -3, -2).reshape(lead + (-1,))


def per_device(dims, hidden_in, lengths, out_grad, w_qkv, w_out, w_up, w_down, vectors, up_bias):
    lanes = FF // 2**dims
    if lanes != 256:
        w_up = regroup(w_up, 256, lanes)
    lengths = lengths[:, 0]
    left = forward((w_qkv, w_out, w_up, w_down), hidden_in, vectors, up_bias, lengths, dims)
    sums = backward(left, out_grad, lengths, dims)
    qkv, out, up, down, grad_vec, grad_bias, edges = finish(sums, left["s_z"], dims)
    if lanes != 256:
        up = regroup(up, lanes, 256)
    return (edges, qkv, out, up, down, grad_vec, grad_bias)


def solution(mesh):
    dims = (mesh.shape[DP] - 1).bit_length()
    weights = P(PIPE, DP, None)
    placed = (
        P(None, DP, None, None),
        P(None, DP),
        P(None, DP, None, None),
        weights,
        weights,
        weights,
        weights,
        P(PIPE, None, DP),
        P(PIPE, DP),
    )
    return jax.shard_map(
        functools.partial(per_device, dims),
        mesh=mesh,
        in_specs=placed,
        out_specs=(
            P(PIPE, None, DP, None, None),
            weights,
            weights,
            weights,
            weights,
            P(PIPE, None, DP),
            P(PIPE, DP),
        ),
        check_vma=False,
    )
```

```python
import functools
from types import SimpleNamespace

import jax
import jax.numpy as jnp
from jax import lax
from jax.experimental import pallas as pl
from jax.experimental.pallas import tpu as pltpu
from jax.sharding import PartitionSpec as P

D = 1024
HEADS = 16
HEAD_DIM = 64
FF = 4096
SEQ = 256
EPS = 1e-05
SCALE = HEAD_DIM**-0.5
MESH = pl.DeviceIdType.MESH
LOW = jnp.bfloat16
WIDE = jnp.float32
QKV, OUT, UP, DOWN = "qkv", "out", "up", "down"
FLAT = "_flat"
PIPE, DP = "pipe", "dp"
PARTS = 4
DOWN_WIDE = D // PARTS
KINDS = [(QKV, 0), (QKV, 1), (QKV, 2), (OUT, 0), (UP, 0), (UP, 1)] + [(DOWN, i) for i in range(PARTS)]
NU = len(KINDS)
GATHER_ORDERS = [
    (0, 1, 2, 3), (0, 1, 2, 3), (0, 1, 3, 2), (0, 1, 3, 2),
    (0, 1, 2), (0, 1, 2), (0, 1, 2), (2, 0, 1),
    (2, 0, 1), (0, 1, 2), (0, 1, 3, 2), (2, 0, 1, 3),
    (0, 1, 2, 3), (0, 1, 3, 2), (0, 1, 2), (2, 0, 1),
    (0, 1, 2), (2, 0, 1), (2, 0, 1), (0, 1, 2),
]
SCHEDULE = [
    2000, 2001, 16, 112, 2002, 32, 240, 80, 241, 17, 128, 176, 0, 33, 2003, 224, 2004, 48, 18, 64,
    288, 1, 2005, 34, 192, 49, 272, 81, 19, 2, 193, 96, 160, 35, 82, 50, 177, 161, 194, 3,
    65, 36, 51, 178, 208, 256, 66, 195, 144, 3000, 20, 47, 4, 3003, 97, 113, 83, 15, 209, 225,
    31, 179, 52, 162, 67, 145, 3002, 129, 3001, 63, 84, 98, 114, 3004, 3005, 3006, 3007, 68, 146, 210,
    130, 95, 180, 242, 226, 3009, 79, 99, 111, 163, 115, 147, 127, 3008, 257, 159, 3010, 3011, 3012, 3013,
    3016, 3017, 131, 196, 3015, 211, 3022, 3023, 3018, 304, 3014, 143, 3019, 243, 3020, 207, 164, 3024, 289, 3021,
    227, 175, 191, 305, 273, 3025, 3026, 3030, 212, 3031, 3033, 258, 3032, 223, 3034, 3035, 3036, 3037, 244, 228,
    290, 255, 306, 3039, 239, 259, 274, 3038, 291, 271, 3040, 3041, 3042, 3043, 3044, 307, 303, 275, 3049, 3050,
    319, 3051, 287, 3052, 3053, 3045, 3046, 3047, 3054, 3048, 3055, 3056,
]
GATHER_FIRST = -10
GATHER_LAGS = [3, 1, -1, -4]
GATHER_READY = 5


def axis_order(dims, u):
    kind, block = KINDS[u]
    if kind in (UP, DOWN):
        return tuple(range(dims - 1))
    return tuple((i + 2 * u) % dims for i in range(dims))


def gather_order(dims, v):
    return GATHER_ORDERS[v] if dims == 4 else axis_order(dims, v % NU)


def place(dims):
    core, here = lax.axis_index(PIPE), lax.axis_index(DP)
    bits = [lax.rem(lax.div(here, 2 ** (dims - 1 - i)), 2) for i in range(dims)]
    partners = [(core, here + (1 - 2 * bits[i]) * 2 ** (dims - 1 - i)) for i in range(dims)]
    return core, bits, partners, (1 - core, here)


def greet(everyone):
    barrier = pltpu.get_barrier_semaphore()
    for device in everyone:
        pl.semaphore_signal(barrier, inc=1, device_id=device, device_id_type=MESH)
    return lambda: pl.semaphore_wait(barrier, len(everyone))


def remote(source, target, send, recv, device):
    return pltpu.make_async_remote_copy(
        src_ref=source, dst_ref=target, send_sem=send, recv_sem=recv, device_id=device, device_id_type=MESH
    )


def span(start, size):
    if isinstance(start, int):
        return pl.ds(start, size)
    return pl.ds(pl.multiple_of(start, size), size)


def for_each(count, body):
    lax.fori_loop(0, count, lambda i, carry: (body(i), carry)[1], 0, unroll=min(count, 8))


def unit_columns(u, column_half):
    kind, block = KINDS[u]
    if kind == DOWN:
        return span(block * DOWN_WIDE + column_half * (DOWN_WIDE // 2), DOWN_WIDE // 2)
    return span(block * 1024 + column_half * 512, 512)


def norm_parts(values):
    center = values - jnp.mean(values, -1, keepdims=True)
    factor = lax.rsqrt(jnp.mean(center * center, -1, keepdims=True) + EPS)
    return (center * factor, factor)


def norm_back(grad_normed, normed, factor):
    return factor * (
        grad_normed
        - jnp.mean(grad_normed, -1, keepdims=True)
        - normed * jnp.mean(grad_normed * normed, -1, keepdims=True)
    )


def dot(left, right, dims=((1,), (0,))):
    return lax.dot_general(left, right, (dims, ((), ())), preferred_element_type=WIDE)


BY_ROWS = ((0,), (0,))
BY_COLUMNS = ((1,), (1,))


def small_layout(count):
    vec_lanes, bias_lanes = D // count, FF // count
    return vec_lanes, 128 // vec_lanes, bias_lanes, max(1, 128 // bias_lanes), max(1, bias_lanes // 128)


def head_masks():
    lanes = lax.broadcasted_iota(jnp.int32, (1, 128), 1)
    first = (lanes < HEAD_DIM).astype(WIDE)
    return first, 1.0 - first


def valid_rows(length, start, count):
    rows = lax.broadcasted_iota(jnp.int32, (count, 1), 0) + start
    return (rows < length).astype(WIDE)


FORWARD_IN = ["w_qkv", "w_out", "w_up", "w_down", "hidden", "vectors", "up_bias", "lengths"]
S = "s_"
SAVED = ["x", "a", "q", "k", "v", "o", "p", "h", "c", "g", "gp"]
LOADS = ["vecs", "og", "y", "w_down", "w_up", "w_qkv", "w_out"] + SAVED
N = SimpleNamespace(**{n: n for n in LOADS})


def saved_shapes():
    wide = lambda *s: (s, WIDE)
    low = lambda *s: (s, LOW)
    return dict(
        x=low(SEQ, D),
        a=low(SEQ, D),
        q=low(SEQ, D),
        k=low(SEQ, D),
        v=low(SEQ, D),
        o=low(SEQ, D),
        p=low(HEADS, SEQ, SEQ),
        h=wide(SEQ, D),
        c=low(2, SEQ, D),
        g=low(2, SEQ, FF // 2),
        gp=low(2, SEQ, FF // 2),
    )


def forward_kernel(dims, names, *refs):
    R = SimpleNamespace(**dict(zip(names, refs)))
    core, bits, partners, sibling = place(dims)
    own = tuple(bits)
    half = bits[-1]
    mate = partners[-1]
    load_x = pltpu.make_async_copy(R.hidden.at[core, 0], R.x0, R.io.at[0])
    load_x.start()
    own_loads = [
        pltpu.make_async_copy(source.at[0], target, R.io.at[1 + i])
        for i, (source, target) in enumerate(
            [(R.w_qkv, R.own_qkv), (R.w_out, R.own_out), (R.w_up, R.own_up), (R.w_down, R.own_down)]
        )
    ]
    for copy in own_loads:
        copy.start()
    met = greet([sibling] + partners)
    total = 2 * NU
    count = 2**dims
    saved = SimpleNamespace(**{n: [getattr(R, n + str(l)) for l in range(2)] for n in SAVED})

    def first_pairs(u, layer, column_half):
        kind, block = KINDS[u]
        cols = unit_columns(u, column_half)
        if kind == UP:
            pairs = []
            for i in range(2):
                block_id = block * 4 + column_half * 2 + i
                to = span(block_id * 256, 256)
                for which, target in ((half, R.up.at[(layer,) + own]), (1 - half, R.stage.at[layer])):
                    pairs.append((R.own_up.at[:, span((2 * block_id + which) * 256, 256)], target.at[:, to]))
            return pairs
        if kind == DOWN:
            return [(R.own_down.at[:, cols], R.down.at[(layer,) + own[:-1] + (slice(None), cols)])]
        return [(getattr(R, "own_" + kind).at[:, cols], getattr(R, kind).at[(layer,) + own + (slice(None), cols)])]

    def first_local(u, layer):
        return [
            pltpu.make_async_copy(s, t, R.local_sem.at[u, i])
            for i, (s, t) in enumerate(first_pairs(u, layer, core))
        ]

    def first_remote(u, layer):
        return [
            remote(s, t, R.first_send.at[u, i], R.first_recv.at[u, i], sibling)
            for i, (s, t) in enumerate(first_pairs(u, layer, 1 - core))
        ]

    def chain(v):
        layer, u = v // NU, v % NU
        kind, block = KINDS[u]
        cols = unit_columns(u, core)
        moves = []
        if kind == UP:
            moves.append((R.stage.at[layer, :, cols], R.up.at[(layer,) + own + (slice(None), cols)], mate))
        order = gather_order(dims, v)
        known = dims - 1 if kind == DOWN else dims
        free = {dims - 1} if kind == UP else set()
        for k in range(len(order) + 1):
            gathered = set(order[:k]) | free
            where = tuple(slice(None) if i in gathered else bits[i] for i in range(known))
            ref = getattr(R, kind).at[(layer,) + where + (slice(None), cols)]
            moves.append((ref, ref, partners[order[k]] if k < len(order) else sibling))
        return [remote(s, t, R.send.at[v, i], R.recv.at[v, i], d) for i, (s, t, d) in enumerate(moves)]

    def small_step(k):
        where = tuple(slice(None) if i < k else bits[i] for i in range(dims))
        ref = R.small_all.at[(core,) + where]
        return remote(ref, ref, R.small_send.at[k], R.small_recv.at[k], partners[k] if k < dims else sibling)

    def pack_small():
        vec_lanes, vec_group, bias_lanes, bias_group, bias_rows = small_layout(count)
        here = lax.axis_index(DP)

        def put(values, at, group):
            if group == 1:
                return values
            return jnp.concatenate([jnp.where(at == i, values, 0.0) for i in range(group)], axis=1)

        tile = R.tile
        tile[...] = jnp.zeros_like(tile)
        tile[0:10, :] = put(R.vectors[0].astype(WIDE), lax.rem(here, vec_group), vec_group)
        bias = put(R.up_bias[...].astype(WIDE), lax.rem(lax.div(here, 2), bias_group), bias_group)
        for i in range(bias_rows):
            tile[10 + i : 11 + i, :] = bias[:, i * 128 : (i + 1) * 128]
        R.small_all[(core,) + own] = tile[...].astype(LOW)

    pack_small()
    for copy in own_loads:
        copy.wait()
    for layer in range(2):

        @pl.when(core == layer)
        def _():
            for u in range(NU):
                for copy in first_local(u, layer):
                    copy.start()

    met()
    for layer in range(2):

        @pl.when(core == layer)
        def _():
            for u in range(NU):
                for copy in first_remote(u, layer):
                    copy.start()

    def arrive(v):
        layer, u = v // NU, v % NU

        @pl.when(core == layer)
        def _():
            for copy in first_local(u, layer):
                copy.wait()
            for copy in first_remote(u, layer):
                copy.wait_send()

        @pl.when(core != layer)
        def _():
            for copy in first_remote(u, layer):
                copy.wait_recv()

    length = R.lengths[core]
    vecs, biases = R.vecs, R.biases
    first_head, second_head = head_masks()

    def assemble():
        vec_lanes, vec_group, bias_lanes, bias_group, bias_rows = small_layout(count)
        small = R.small_all

        def shard(layer, d):
            return small[(layer,) + tuple((d >> (dims - 1 - i)) & 1 for i in range(dims))].astype(WIDE)

        def half_shard(layer, b):
            lead = tuple((b >> (dims - 2 - i)) & 1 for i in range(dims - 1))
            return small[(layer,) + lead + (half,)].astype(WIDE)

        for layer in range(2):
            for t in range(D // 128):
                vecs[layer, :, t * 128 : (t + 1) * 128] = sum(
                    shard(layer, d) for d in range(t * vec_group, (t + 1) * vec_group)
                )
            for t in range(count // 2 // bias_group):
                tile = sum(half_shard(layer, b) for b in range(t * bias_group, (t + 1) * bias_group))
                for i in range(bias_rows):
                    at = (t * bias_rows + i) * 128
                    biases[layer, 0:1, at : at + 128] = tile[10 + i : 11 + i, :]

    save_queue = []

    def save(name, layer):
        copy = pltpu.make_async_copy(
            getattr(saved, name)[layer], getattr(R, S + name).at[layer], R.save_sem.at[layer, SAVED.index(name)]
        )
        copy.start()
        save_queue.append(copy)

    def vec(layer, i, cols=slice(None)):
        return vecs[layer, i : i + 1, cols]

    def load_weight(v):
        layer, u = v // NU, v % NU
        kind, block = KINDS[u]
        if kind == DOWN:
            flat = R.down_flat.at[layer, :, pl.ds(block * DOWN_WIDE, DOWN_WIDE)]
            target = R.w_low.at[:, pl.ds(block * DOWN_WIDE, DOWN_WIDE)]
        else:
            flat = getattr(R, kind + FLAT).at[layer, :, pl.ds(block * 1024, 1024)]
            target = R.w_slots.at[u]
        return pltpu.make_async_copy(flat, target, R.weight_sem.at[u])

    def first_norm(layer):
        def rows(i):
            at = span(i * 32, 32)
            normed, unused = norm_parts(saved.x[layer][at, :].astype(WIDE))
            saved.a[layer][at, :] = (normed * vec(layer, 0) + vec(layer, 1)).astype(LOW)

        for_each(SEQ // 32, rows)
        save(N.x, layer)
        save(N.a, layer)

    def project(layer, block):
        target = (saved.q, saved.k, saved.v)[block][layer]
        weight = R.w_slots.at[block]

        def columns(n):
            at = span(n * 256, 256)
            values = dot(saved.a[layer][...], weight[:, at])
            if block == 0:
                values = (values + vec(layer, 2, at)).astype(LOW) * SCALE
            elif block == 2:
                values = values + vec(layer, 3, at)
            target[:, at] = values.astype(LOW)

        for_each(D // 256, columns)
        save((N.q, N.k, N.v)[block], layer)

    def attention(layer):
        key_ids = lax.broadcasted_iota(jnp.int32, (SEQ, SEQ), 0)
        query_ids = lax.broadcasted_iota(jnp.int32, (SEQ, SEQ), 1)
        blocked = jnp.where((key_ids <= query_ids) & (key_ids < length), 0.0, -1e30)

        def pair(n):
            at = span(n * 128, 128)
            query, key, value = (part[layer][:, at] for part in (saved.q, saved.k, saved.v))
            parts = []
            for i, mask in enumerate((first_head, second_head)):
                scores = dot(key, query * mask.astype(LOW), BY_COLUMNS) + blocked
                weights = jnp.exp(scores - jnp.max(scores, 0, keepdims=True))
                probs = (weights * (1.0 / jnp.sum(weights, 0, keepdims=True))).astype(LOW)
                saved.p[layer][2 * n + i] = probs
                parts.append(dot(probs, value, BY_ROWS) * mask)
            saved.o[layer][:, at] = (parts[0] + parts[1]).astype(LOW)

        for_each(HEADS // 2, pair)
        save(N.p, layer)
        save(N.o, layer)

    def send_c(layer):
        ref = saved.c[layer]
        return remote(ref.at[0], ref.at[1], R.act_send.at[layer, 0], R.act_recv.at[layer, 0], mate)

    def attend_out(layer):
        weight = R.w_slots.at[3]
        hidden = saved.h[layer]

        def columns(n):
            at = span(n * 256, 256)
            values = dot(saved.o[layer][...], weight[:, at])
            hidden[:, at] = saved.x[layer][:, at].astype(WIDE) + values + vec(layer, 4, at)

        for_each(D // 256, columns)

    def second_norm(layer):
        def rows(i):
            at = span(i * 32, 32)
            normed, unused = norm_parts(saved.h[layer][at, :])
            saved.c[layer][0, at, :] = (normed * vec(layer, 5) + vec(layer, 6)).astype(LOW)

        for_each(SEQ // 32, rows)
        save(N.h, layer)

    def feed_up(layer, block, who):
        weight = R.w_slots.at[4 + block]

        def columns(n):
            at = span(n * 256, 256)
            to = span(block * 1024 + n * 256, 256)
            value = dot(saved.c[layer][who], weight[:, at]) + biases[layer, 0:1, to]
            share = 0.5 + 0.5 * lax.erf(value * 0.7071067811865476)
            slope = share + value * (jnp.exp(value * value * -0.5) * 0.3989422804014327)
            saved.g[layer][who, :, to] = (value * share).astype(LOW)
            saved.gp[layer][who, :, to] = slope.astype(LOW)

        for_each(4, columns)
        if block == 1 and who == 1:
            save(N.g, layer)
            save(N.gp, layer)

    def send_part(layer, block):
        at = pl.ds(block * DOWN_WIDE, DOWN_WIDE)
        return remote(
            R.part.at[layer, 0, :, at],
            R.part.at[layer, 1, :, at],
            R.act_send.at[layer, 1 + block],
            R.act_recv.at[layer, 1 + block],
            mate,
        )

    def down_theirs(layer, block):
        at = pl.ds(block * DOWN_WIDE, DOWN_WIDE)
        R.part[layer, 0, :, at] = dot(saved.g[layer][1], R.w_low[:, at]).astype(LOW)

    def down_mine(layer, block):
        at = pl.ds(block * DOWN_WIDE, DOWN_WIDE)
        values = dot(saved.g[layer][0], R.w_low[:, at])
        R.y[:, at] = saved.h[layer][:, at] + values + vec(layer, 7, at)

    def end(layer):
        def rows(i):
            at = span(i * 32, 32)
            valid = valid_rows(length, i * 32, 32)
            values = R.y[at, :] + R.part[layer, 1, at, :].astype(WIDE)
            if layer == 0:
                saved.x[1][at, :] = (values * valid).astype(LOW)
            else:
                R.y[at, :] = values
                normed, unused = norm_parts(values)
                R.z[at, :] = (normed * vec(1, 8) + vec(1, 9)) * valid

        for_each(SEQ // 32, rows)

    def weight(layer, u):
        load_weight(layer * NU + u).wait()

    def wait_parts(layer):
        for block in range(PARTS):
            send_part(layer, block).wait()

    def wait_c(layer):
        send_c(layer).wait()
        save(N.c, layer)

    pieces = [
        (first_norm, None),
        (lambda layer: project(layer, 0), 0),
        (lambda layer: project(layer, 1), 1),
        (lambda layer: project(layer, 2), 2),
        (attention, None),
        (attend_out, 3),
        (second_norm, None),
        (lambda layer: send_c(layer).start(), None),
        (lambda layer: feed_up(layer, 0, 0), 4),
        (lambda layer: feed_up(layer, 1, 0), 5),
        (wait_c, None),
        (lambda layer: feed_up(layer, 0, 1), None),
        (lambda layer: feed_up(layer, 1, 1), None),
    ]
    for block in range(PARTS):
        pieces.append((functools.partial(lambda block, layer: down_theirs(layer, block), block), 6 + block))
        pieces.append((functools.partial(lambda block, layer: send_part(layer, block).start(), block), None))
        pieces.append((functools.partial(lambda block, layer: down_mine(layer, block), block), None))
    pieces += [(wait_parts, None), (end, None)]

    chains = [chain(v) for v in range(total)]

    def plain_schedule():
        moves = []
        for v in range(total):
            for i in range(len(chains[v])):
                left = len(chains[v]) - 1 - i
                lag = GATHER_LAGS[left] if left < len(GATHER_LAGS) else GATHER_LAGS[-1] - left + len(GATHER_LAGS) - 1
                moves.append((v + (lag if i else min(GATHER_FIRST, lag)), -i, v))
            moves.append((v + GATHER_READY, -99, v))
        codes = [16 * v - i if i > -99 else 16 * v + 15 for unused, i, v in sorted(moves)]
        for k in range(dims + 2):
            codes.insert(6 * k, 2000 + k)
        result, done = [], set()
        jobs = [(layer, w) for layer in range(2) for w in range(len(pieces))]
        for code in codes:
            result.append(code)
            done.add(code)
            while jobs and 2000 + dims + 1 in done:
                layer, w = jobs[0]
                u = pieces[w][1]
                if u is not None and 16 * (layer * NU + u) + 15 not in done:
                    break
                result.append(3000 + 30 * layer + w)
                jobs.pop(0)
        return result

    load_x.wait()
    for code in SCHEDULE if dims == 4 and SCHEDULE else plain_schedule():
        if code >= 3000:
            layer, w = (code - 3000) // 30, (code - 3000) % 30
            if pieces[w][1] is not None:
                weight(layer, pieces[w][1])
            pieces[w][0](layer)
        elif code >= 2000:
            k = code - 2000
            if k > 0:
                small_step(k - 1).wait()
            if k <= dims:
                small_step(k).start()
            else:
                assemble()
        elif code % 16 == 15:
            v = code // 16
            chains[v][-1].wait()
            load_weight(v).start()
        else:
            v, i = code // 16, code % 16
            if i == 0:
                arrive(v)
            else:
                chains[v][i - 1].wait()
            chains[v][i].start()

    last = [(R.y, R.s_y, 0), (R.z, R.s_z, 1), (R.vecs, R.s_vecs, 2)]
    for source, target, i in last:
        pltpu.make_async_copy(source, target, R.last_sem.at[i]).start()
    for copy in save_queue:
        copy.wait()
    for source, target, i in last:
        pltpu.make_async_copy(source, target, R.last_sem.at[i]).wait()


def forward(shards, hidden, vectors, up_bias, lengths, dims):
    rows = D // 2**dims
    bits = (2,) * dims
    outs = dict(
        qkv=((2,) + bits + (rows, 3 * D), LOW),
        out=((2,) + bits + (rows, D), LOW),
        up=((2,) + bits + (rows, FF // 2), LOW),
        down=((2,) + bits[:-1] + (4 * rows, D), LOW),
        stage=((2, rows, FF // 2), LOW),
    )
    for name, (shape, dtype) in saved_shapes().items():
        outs[S + name] = ((2,) + shape, dtype)
    outs[S + N.y] = ((SEQ, D), WIDE)
    outs[S + "z"] = ((SEQ, D), WIDE)
    outs[S + N.vecs] = ((2, 16, D), WIDE)
    dma = pltpu.SemaphoreType.DMA
    total = 2 * NU
    scratch = dict(
        small_all=pltpu.VMEM((2,) + bits + (16, 128), LOW),
        vecs=pltpu.VMEM((2, 16, D), WIDE),
        biases=pltpu.VMEM((2, 8, FF // 2), WIDE),
        w_slots=pltpu.VMEM((6, D, D), LOW),
        w_low=pltpu.VMEM((FF // 2, D), LOW),
        part=pltpu.VMEM((2, 2, SEQ, D), LOW),
        y=pltpu.VMEM((SEQ, D), WIDE),
        z=pltpu.VMEM((SEQ, D), WIDE),
        local_sem=dma((NU, 4)),
        first_send=dma((NU, 4)),
        first_recv=dma((NU, 4)),
        send=dma((total, dims + 2)),
        recv=dma((total, dims + 2)),
        small_send=dma((dims + 1,)),
        small_recv=dma((dims + 1,)),
        io=dma((5,)),
        tile=pltpu.VMEM((16, 128), WIDE),
        own_qkv=pltpu.VMEM((rows, 3 * D), LOW),
        own_out=pltpu.VMEM((rows, D), LOW),
        own_up=pltpu.VMEM((rows, FF), LOW),
        own_down=pltpu.VMEM((4 * rows, D), LOW),
        save_sem=dma((2, len(SAVED))),
        weight_sem=dma((NU,)),
        act_send=dma((2, 1 + PARTS)),
        act_recv=dma((2, 1 + PARTS)),
        last_sem=dma((3,)),
    )
    for name, (shape, dtype) in saved_shapes().items():
        for layer in range(2):
            scratch[name + str(layer)] = pltpu.VMEM(shape, dtype)
    names = FORWARD_IN + list(outs) + list(scratch)

    def kernel(*refs):
        by_name = dict(zip(names, refs))
        extra = dict(
            qkv_flat=by_name[QKV].reshape(2, D, 3 * D),
            out_flat=by_name[OUT].reshape(2, D, D),
            up_flat=by_name[UP].reshape(2, D, FF // 2),
            down_flat=by_name[DOWN].reshape(2, FF // 2, D),
        )
        forward_kernel(dims, names + list(extra), *refs, *extra.values())

    anywhere = pl.BlockSpec(memory_space=pl.ANY)
    whole = pl.BlockSpec(memory_space=pltpu.VMEM)
    results = pl.pallas_call(
        kernel,
        out_shape=[jax.ShapeDtypeStruct(s, t) for s, t in outs.values()],
        in_specs=[anywhere] * 5 + [whole] * 2 + [pl.BlockSpec(memory_space=pltpu.SMEM)],
        out_specs=[anywhere] * len(outs),
        scratch_shapes=list(scratch.values()),
        compiler_params=pltpu.CompilerParams(collective_id=1, has_side_effects=True, vmem_limit_bytes=60 << 20),
        name="forward",
    )(*shards, hidden, vectors, up_bias, lengths)
    return dict(zip(outs, results))


BACK_PARTS = 2
BACK_WIDE = D // BACK_PARTS
BACK = [(DOWN, i) for i in range(BACK_PARTS)] + [(UP, 0), (UP, 1), (OUT, 0), (QKV, 0), (QKV, 1), (QKV, 2)]
NB = len(BACK)
SCATTER_LAGS = [1, 3, 4, 5, 6]
BACK_ORDERS = [
    (0, 1, 2), (2, 0, 1), (0, 1, 2), (0, 1, 2),
    (0, 1, 2, 3), (0, 1, 2, 3), (0, 1, 3, 2), (0, 1, 2, 3),
]
BACK_SCHEDULE = [
    3000, 3001, 3003, 3002, 3004, 3005, 0, 3006, 3008, 3009, 3010, 3007, 3012, 16, 3011, 32, 1, 3013, 3014, 3015,
    3016, 48, 17, 64, 3017, 3018, 33, 3019, 80, 3020, 3022, 3023, 2, 65, 49, 3030, 3033, 3031, 18, 34,
    3021, 3032, 81, 66, 112, 3, 19, 96, 3034, 50, 3035, 35, 82, 67, 3036, 3037, 144, 128, 51, 3038,
    113, 3039, 3040, 68, 97, 52, 36, 83, 3041, 3042, 145, 3043, 176, 160, 3044, 114, 3045, 3046, 98, 84,
    192, 3047, 115, 129, 3048, 3049, 99, 177, 208, 100, 193, 116, 3050, 130, 3051, 161, 224, 178, 240, 3052,
    3053, 194, 4000, 2000, 209, 162, 225, 195, 241, 2001, 210, 163, 226, 146, 2002, 211, 196, 131, 242, 227,
    179, 180, 212, 147, 243, 164, 2003, 2004, 228, 244,
]
HELD, B, TILE = "held", "b_", "tile"
BACK_WEIGHTS = [QKV, OUT, UP, DOWN]
BACK_IN = BACK_WEIGHTS + [S + n for n in SAVED + ["y", "z", "vecs"]] + ["out_grad", "lengths"]


def back_order(dims, u):
    return BACK_ORDERS[u] if dims == 4 else axis_order(dims, KINDS.index(BACK[u]))


def box_name(u, k):
    return "box%d_%d" % (u, k)


def backward_kernel(dims, names, *refs):
    R = SimpleNamespace(**dict(zip(names, refs)))
    core, bits, partners, sibling = place(dims)
    own = tuple(bits)
    half = bits[-1]
    mate = partners[-1]
    met = greet([sibling] + partners)
    total = 2 * NB
    count = 2**dims
    length = R.lengths[core]
    vecs, grads = R.vecs, R.grads
    first_head, second_head = head_masks()

    def load(name, layer):
        if name == N.y:
            source = R.s_y
        elif name == N.og:
            source = R.out_grad.at[core, 0]
        elif name == N.vecs:
            source = R.s_vecs
        elif name in (N.w_down, N.w_up, N.w_qkv, N.w_out):
            source = getattr(R, name[2:] + FLAT).at[layer]
        else:
            source = getattr(R, S + name).at[layer]
        if name == N.vecs:
            target = vecs
        elif name == N.w_up:
            target = R.b_w_wide.at[:, pl.ds(0, FF // 2)]
        elif name == N.w_qkv:
            target = R.b_w_wide
        else:
            target = getattr(R, B + name)
        return pltpu.make_async_copy(source, target, R.load_sem.at[LOADS.index(name)])

    def need(layer, *which):
        for name in which:
            load(name, layer).wait()

    def again(layer, *which):
        if layer == 1:
            for name in which:
                load(name, 0).start()

    def unit_of(v):
        return 1 - v // NB, BACK[v % NB]

    def columns_of(v, column_half):
        kind, block = BACK[v % NB]
        if kind == DOWN:
            return span(block * BACK_WIDE + column_half * (BACK_WIDE // 2), BACK_WIDE // 2)
        return span(block * 1024 + column_half * 512, 512)

    def order_of(v):
        return tuple(reversed(back_order(dims, v % NB)))

    def held(v):
        return getattr(R, HELD + str(v % NB))

    def box(v, k):
        if k == 0:
            kind, block = BACK[v % NB]
            return (R.down_box if kind == DOWN else R.wide_box).at[v % 2]
        return getattr(R, box_name(v % NB, k))

    def stage(v):
        kind, block = BACK[v % NB]
        return (R.down_stage if kind == DOWN else R.wide_stage).at[v % 2]

    def is_up(v):
        return BACK[v % NB][0] == UP

    def steps(v):
        return len(order_of(v)) + (1 if is_up(v) else 0)

    def where(v, k, away):
        order = order_of(v)
        place_of = []
        for i in range(dims - 1 if BACK[v % NB][0] == DOWN else dims):
            if i in order[: max(k - 1, 0)]:
                place_of.append(bits[i])
            elif 0 < k <= len(order) and i == order[k - 1]:
                place_of.append(1 - bits[i] if away else bits[i])
            elif k > len(order) and i == dims - 1:
                place_of.append(1 - half if away else half)
            elif k > len(order):
                place_of.append(bits[i])
            else:
                place_of.append(slice(None))
        return tuple(place_of)

    def device_of(v, k):
        if k == 0:
            return sibling
        return partners[order_of(v)[k - 1]] if k <= len(order_of(v)) else mate

    def move(v, k):
        source = stage(v) if k == 0 else held(v).at[where(v, k, True)]
        return remote(source, box(v, k), R.send.at[v, k], R.recv.at[v, k], device_of(v, k))

    def earlier(v, k):
        if k > 0:
            return v - NB if v >= NB else None
        low = BACK[v % NB][0] == DOWN
        same = [w for w in range(v) if (BACK[w % NB][0] == DOWN) == low and w % 2 == v % 2]
        return same[-1] if same else None

    def later(v, k):
        return any(earlier(w, k) == v for w in range(v + 1, total))

    def begin(v, k):
        if earlier(v, k) is not None:
            pl.semaphore_wait(R.credit.at[v % NB, k], 1)
        move(v, k).start()

    def consumed(v, k):
        for w in range(v + 1, total):
            if earlier(w, k) == v:
                pl.semaphore_signal(
                    R.credit.at[w % NB, k], inc=1, device_id=device_of(v, k), device_id_type=MESH
                )

    def finals(v):
        kind, block = BACK[v % NB]
        cols = columns_of(v, core)
        if kind == UP:
            pairs = []
            for i in range(2):
                block_id = block * 4 + core * 2 + i
                part = (slice(None), pl.ds(i * 256, 256))
                for which, source in ((half, held(v).at[own + part]), (1 - half, box(v, dims).at[part])):
                    pairs.append((source, R.g_up.at[:, span((2 * block_id + which) * 256, 256)]))
            return pairs
        if kind == DOWN:
            return [(held(v).at[own[:-1]], R.g_down.at[:, cols])]
        return [(held(v).at[own], getattr(R, "g_" + kind).at[:, cols])]

    def final_local(v):
        return [
            pltpu.make_async_copy(s, t, R.out_sem.at[v, i]) for i, (s, t) in enumerate(finals(v))
        ]

    def final_remote(v):
        return [
            remote(s, t, R.end_send.at[v, i], R.end_recv.at[v, i], sibling)
            for i, (s, t) in enumerate(finals(v))
        ]

    def finish(v):
        @pl.when(core == unit_of(v)[0])
        def _():
            for copy in final_local(v):
                copy.start()

        @pl.when(core != unit_of(v)[0])
        def _():
            for copy in final_remote(v):
                copy.start()

    def finished(v):
        @pl.when(core == unit_of(v)[0])
        def _():
            for copy in final_local(v):
                copy.wait()

        @pl.when(core != unit_of(v)[0])
        def _():
            for copy in final_remote(v):
                copy.wait_send()
        if is_up(v):
            consumed(v, dims)

    def event(v, k):
        move(v, k).wait()
        if not (is_up(v) and k == steps(v)):
            view = held(v).at[where(v, k, False)]
            view[...] = view[...] + box(v, k)[...]
            consumed(v, k)
        if k < steps(v):
            begin(v, k + 1)
        else:
            finish(v)

    def vec(layer, i):
        return vecs[layer, i : i + 1, :]

    def collect(layer, i, values):
        grads[layer, i : i + 1, :] = grads[layer, i : i + 1, :] + jnp.sum(values, 0, keepdims=True)

    def send_e(layer, block):
        ref = R.e.at[layer]
        at = pl.ds(block * BACK_WIDE, BACK_WIDE)
        send, recv = R.act_send.at[layer, 1 + block], R.act_recv.at[layer, 1 + block]
        return remote(ref.at[0, :, at], ref.at[1, :, at], send, recv, mate)

    def send_dc(layer):
        ref = R.dc_part
        return remote(ref.at[0], ref.at[1], R.act_send.at[layer, 0], R.act_recv.at[layer, 0], mate)

    def top(layer):
        if layer == 1:
            need(1, N.vecs, N.og, N.y)

        def rows(i):
            at = span(i * 32, 32)
            valid = valid_rows(length, i * 32, 32)
            if layer == 1:
                grad_z = R.b_og[at, :].astype(WIDE) * valid
                normed, factor = norm_parts(R.b_y[at, :])
                collect(1, 8, grad_z * normed)
                collect(1, 9, grad_z)
                grad_y = norm_back(grad_z * vec(1, 8), normed, factor)
            else:
                grad_y = R.dx[at, :].astype(WIDE) * valid
            R.dy[at, :] = grad_y
            branch = grad_y.astype(LOW)
            R.e[layer, 0, at, :] = branch
            collect(layer, 7, branch.astype(WIDE))

        for_each(SEQ // 32, rows)

    def produce(v, body, quarter_shape):
        for target, column_half in ((stage(v), 1 - core), (held(v), core)):
            cols = columns_of(v, column_half)

            def quarter(i):
                target[lax.div(i, 2), lax.rem(i, 2)] = body(i, cols).astype(LOW).reshape(quarter_shape)

            for_each(4, quarter)
            if column_half is not core:
                begin(v, 0)

    def pair_rows(ref, cols):
        values = ref[:, :, cols]
        return values.reshape(2 * SEQ, values.shape[-1])

    inner = (2,) * (dims - 2) + (D // count, 512)
    down_inner = (2,) * (dims - 3) + (FF // count, BACK_WIDE // 2)

    def grad_down(layer, v, block):
        if block == 0:
            need(layer, N.g)
        produce(
            v,
            lambda i, cols: dot(pair_rows(R.b_g, span(i * 512, 512)), pair_rows(R.e.at[layer], cols), BY_ROWS),
            down_inner,
        )
        if block == BACK_PARTS - 1:
            again(layer, N.g)

    def feed_hidden(layer, who):
        if who == 0:
            need(layer, N.w_down, N.gp)

        def hidden(n):
            at = span(n * 256, 256)
            grad_act = dot(R.e[layer, who], R.b_w_down[at, :], BY_COLUMNS)
            grad_upper = (grad_act * R.b_gp[who, :, at].astype(WIDE)).astype(LOW)
            R.b_gp[who, :, at] = grad_upper
            sums = jnp.sum(grad_upper.astype(WIDE), 0, keepdims=True)
            R.bias_grads[layer, 0:1, at] = sums if who == 0 else R.bias_grads[layer, 0:1, at] + sums

        for_each(FF // 2 // 256, hidden)
        if who == 1:
            again(layer, N.w_down)

    def feed_theirs(layer):
        need(layer, N.w_up)

        def theirs(n):
            at = span(n * 256, 256)
            R.dc_part[0, :, at] = dot(R.b_gp[1], R.b_w_wide[at, pl.ds(0, FF // 2)], BY_COLUMNS).astype(LOW)

        for_each(D // 256, theirs)

    def feed_mine(layer):
        def mine(n):
            at = span(n * 256, 256)
            R.dc[:, at] = dot(R.b_gp[0], R.b_w_wide[at, pl.ds(0, FF // 2)], BY_COLUMNS)

        for_each(D // 256, mine)
        load(N.w_qkv, layer).start()

    def grad_up(layer, v, block):
        if block == 0:
            need(layer, N.c)

        def body(i, cols):
            return dot(pair_rows(R.b_c, span(i * 256, 256)), pair_rows(R.b_gp, cols), BY_ROWS)

        produce(v, body, inner)
        if block == 1:
            again(layer, N.c, N.gp)

    def middle(layer):
        need(layer, N.h)

        def rows(i):
            at = span(i * 32, 32)
            grad_in = R.dc[at, :] + R.dc_part[1, at, :].astype(WIDE)
            normed, factor = norm_parts(R.b_h[at, :])
            collect(layer, 5, grad_in * normed)
            collect(layer, 6, grad_in)
            grad_hidden = R.dy[at, :] + norm_back(grad_in * vec(layer, 5), normed, factor)
            R.dy[at, :] = grad_hidden
            branch = grad_hidden.astype(LOW)
            R.f[at, :] = branch
            collect(layer, 4, branch.astype(WIDE))

        for_each(SEQ // 32, rows)
        again(layer, N.h)

    def grad_out(layer, v):
        need(layer, N.o)
        produce(v, lambda i, cols: dot(R.b_o[:, span(i * 256, 256)], R.f[:, cols], BY_ROWS), inner)
        again(layer, N.o)

    def grad_mixed(layer):
        need(layer, N.w_out)

        def columns(n):
            at = span(n * 256, 256)
            R.do[:, at] = dot(R.f[...], R.b_w_out[at, :], BY_COLUMNS).astype(LOW)

        for_each(D // 256, columns)
        again(layer, N.w_out)

    def attention_back(layer):
        need(layer, N.q, N.k, N.v, N.p)

        def pair(n):
            at = span(n * 128, 128)
            query, key, value, grad_o = R.b_q[:, at], R.b_k[:, at], R.b_v[:, at], R.do[:, at]
            sums = [0.0, 0.0, 0.0]
            for i, mask in enumerate((first_head.astype(LOW), second_head.astype(LOW))):
                probs = R.b_p[2 * n + i]
                grad_head = grad_o * mask
                wide = probs.astype(WIDE)
                grad_probs = dot(value, grad_head, BY_COLUMNS)
                shift = jnp.sum(grad_probs * wide, 0, keepdims=True)
                grad_scores = (wide * (grad_probs - shift)).astype(LOW)
                sums[0] += dot(grad_scores, key * mask, BY_ROWS)
                sums[1] += dot(grad_scores, query * mask)
                sums[2] += dot(probs, grad_head)
            sums[0] = sums[0] * SCALE
            for j in range(3):
                low = sums[j].astype(LOW)
                R.dp[:, pl.ds(pl.multiple_of(n * 128 + j * D, 128), 128)] = low
                if j != 1:
                    row = 2 if j == 0 else 3
                    grads[layer, row : row + 1, at] = jnp.sum(low.astype(WIDE), 0, keepdims=True)

        for_each(HEADS // 2, pair)
        again(layer, N.q, N.k, N.v, N.p)

    def grad_qkv(layer, v, block):
        if block == 0:
            need(layer, N.a)
        produce(v, lambda i, cols: dot(R.b_a[:, span(i * 256, 256)], R.dp[:, cols], BY_ROWS), inner)
        if block == 2:
            again(layer, N.a)

    def grad_attn_in(layer):
        need(layer, N.w_qkv)

        def columns(n):
            at = span(n * 256, 256)
            R.dc[:, at] = dot(R.dp[...], R.b_w_wide[at, :], BY_COLUMNS)

        for_each(D // 256, columns)
        again(layer, N.w_up)

    def bottom(layer):
        need(layer, N.x)

        def rows(i):
            at = span(i * 32, 32)
            grad_in = R.dc[at, :]
            normed, factor = norm_parts(R.b_x[at, :].astype(WIDE))
            collect(layer, 0, grad_in * normed)
            collect(layer, 1, grad_in)
            grad_x = R.dy[at, :] + norm_back(grad_in * vec(layer, 0), normed, factor)
            if layer == 1:
                R.dx[at, :] = grad_x.astype(LOW)
            else:
                R.b_y[at, :] = grad_x

        for_each(SEQ // 32, rows)
        again(layer, N.x)

    def spread():
        vec_lanes, vec_group, bias_lanes, bias_group, bias_rows = small_layout(count)
        tiles = R.tiles
        tiles[...] = jnp.zeros_like(tiles)
        for layer in range(2):
            for d in range(count):
                lead = tuple((d >> (dims - 1 - i)) & 1 for i in range(dims))
                t = d // vec_group
                tiles[(layer,) + lead + (slice(0, 10),)] = grads[layer, 0:10, t * 128 : (t + 1) * 128]
            for b in range(count // 2):
                lead = tuple((b >> (dims - 2 - i)) & 1 for i in range(dims - 1))
                for i in range(bias_rows):
                    at = (b // bias_group * bias_rows + i) * 128
                    tiles[(layer,) + lead + (half, slice(10 + i, 11 + i))] = R.bias_grads[layer, 0:1, at : at + 128]

    def tile_box(k):
        return getattr(R, TILE + str(k))

    def small_move(k):
        if k == 0:
            return remote(
                R.tiles.at[1 - core], tile_box(0), R.small_send.at[0], R.small_recv.at[0], sibling
            )
        lead = own[: k - 1] + (1 - bits[k - 1],)
        return remote(
            R.tiles.at[(core,) + lead],
            tile_box(k),
            R.small_send.at[k],
            R.small_recv.at[k],
            partners[k - 1],
        )

    def small_event(k):
        small_move(k).wait()
        lead = own[:k]
        view = R.tiles.at[(core,) + lead]
        view[...] = view[...] + tile_box(k)[...]
        if k < dims:
            small_move(k + 1).start()
        else:
            pltpu.make_async_copy(view, R.g_small, R.edge_sem.at[2]).start()

    for name in (N.vecs, N.og, N.y, N.g, N.w_down, N.gp, N.w_up, N.c, N.h, N.o, N.w_out, N.q, N.k, N.v, N.p, N.x, N.a):
        load(name, 1).start()
    grads[...] = jnp.zeros_like(grads)
    top(1)
    met()
    edge_local = pltpu.make_async_copy(R.b_y, R.mine, R.edge_sem.at[0])
    edge_remote = [remote(ref, R.theirs, R.edge_send.at[0], R.edge_recv.at[0], sibling) for ref in (R.s_z, R.b_y)]

    @pl.when(core == 0)
    def _():
        edge_remote[0].start()

    def last(layer):
        edge_local.start()

        @pl.when(core == 1)
        def _():
            edge_remote[1].start()

        spread()
        small_move(0).start()

    def unit(layer, u):
        return (1 - layer) * NB + u

    def start_e(block, layer):
        send_e(layer, block).start()

    def wait_e(block, layer):
        send_e(layer, block).wait()

    def down(block, layer):
        grad_down(layer, unit(layer, block), block)

    pieces = [(top, None)]
    pieces += [(functools.partial(start_e, i), None) for i in range(BACK_PARTS)]
    pieces.append((lambda layer: feed_hidden(layer, 0), None))
    for i in range(BACK_PARTS):
        pieces += [(functools.partial(wait_e, i), None), (functools.partial(down, i), i)]
    pieces += [
        (lambda layer: feed_hidden(layer, 1), None),
        (feed_theirs, None),
        (lambda layer: send_dc(layer).start(), None),
        (feed_mine, None),
        (lambda layer: grad_up(layer, unit(layer, BACK_PARTS), 0), BACK_PARTS),
        (lambda layer: grad_up(layer, unit(layer, BACK_PARTS + 1), 1), BACK_PARTS + 1),
        (lambda layer: send_dc(layer).wait(), None),
        (middle, None),
        (lambda layer: grad_out(layer, unit(layer, BACK_PARTS + 2)), BACK_PARTS + 2),
        (grad_mixed, None),
        (attention_back, None),
        (lambda layer: grad_qkv(layer, unit(layer, BACK_PARTS + 3), 0), BACK_PARTS + 3),
        (lambda layer: grad_qkv(layer, unit(layer, BACK_PARTS + 4), 1), BACK_PARTS + 4),
        (lambda layer: grad_qkv(layer, unit(layer, BACK_PARTS + 5), 2), BACK_PARTS + 5),
        (grad_attn_in, None),
        (bottom, None),
    ]

    def plain_schedule():
        timed = []
        for v in range(total):
            for k in range(steps(v) + 1):
                lag = SCATTER_LAGS[k] if k < len(SCATTER_LAGS) else SCATTER_LAGS[-1] + (k - len(SCATTER_LAGS) + 1) / 8
                timed.append((v + lag, 0, -k, v))
            timed.append((v, 1, 0, v))
        result = []
        for turn in range(2):
            at = -1.0
            for w, (unused, u) in enumerate(pieces):
                at = max(at + 0.01, turn * NB + (u or 0))
                timed.append((at, 1, w, (turn, w)))
        codes = []
        for key, is_compute, k, v in sorted(timed, key=lambda item: item[:3]):
            if not is_compute:
                codes.append(16 * v - k)
            elif isinstance(v, tuple):
                codes.append(3000 + 30 * v[0] + v[1])
        codes.append(4000)
        return codes + [2000 + k for k in range(dims + 1)]

    for code in BACK_SCHEDULE if dims == 4 and BACK_SCHEDULE else plain_schedule():
        if code == 3000:
            continue
        if code >= 4000:
            last(0)
        elif code >= 3000:
            turn, w = (code - 3000) // 30, (code - 3000) % 30
            u = pieces[w][1]
            if turn == 1 and u is not None:
                finished(u)
            pieces[w][0](1 - turn)
        elif code >= 2000:
            small_event(code - 2000)
        else:
            event(code // 16, code % 16)
    for v in range(NB, total):
        finished(v)

    @pl.when(core == 0)
    def _():
        edge_remote[0].wait_send()

    @pl.when(core == 1)
    def _():
        edge_remote[1].wait_send()

    edge_local.wait()
    edge_remote[0].wait_recv()
    pltpu.make_async_copy(R.tiles.at[(core,) + own], R.g_small, R.edge_sem.at[2]).wait()
    for layer in range(2):

        @pl.when(core == layer)
        def _():
            for v in range((1 - layer) * NB, (2 - layer) * NB):
                for copy in final_remote(v):
                    copy.wait_recv()


def backward(left, out_grad, lengths, dims):
    rows = D // 2**dims
    bits = (2,) * dims
    outs = dict(
        g_qkv=((rows, 3 * D), LOW),
        g_out=((rows, D), LOW),
        g_up=((rows, FF), LOW),
        g_down=((4 * rows, D), LOW),
        g_small=((16, 128), WIDE),
        mine=((SEQ, D), WIDE),
        theirs=((SEQ, D), WIDE),
    )
    dma = pltpu.SemaphoreType.DMA
    total = 2 * NB
    vmem = lambda shape, dtype=LOW: pltpu.VMEM(shape, dtype)
    scratch = dict(
        vecs=vmem((2, 16, D), WIDE),
        grads=vmem((2, 16, D), WIDE),
        bias_grads=vmem((2, 8, FF // 2), WIDE),
        b_og=vmem((SEQ, D)),
        b_y=vmem((SEQ, D), WIDE),
        b_w_down=vmem((FF // 2, D)),
        b_w_wide=vmem((D, 3 * D)),
        b_w_out=vmem((D, D)),
        e=vmem((2, 2, SEQ, D)),
        dc_part=vmem((2, SEQ, D)),
        dc=vmem((SEQ, D), WIDE),
        dy=vmem((SEQ, D), WIDE),
        dx=vmem((SEQ, D)),
        f=vmem((SEQ, D)),
        do=vmem((SEQ, D)),
        dp=vmem((SEQ, 3 * D)),
        tiles=vmem((2,) + bits + (16, 128), WIDE),
        wide_stage=vmem((2,) + bits + (rows, 512)),
        wide_box=vmem((2,) + bits + (rows, 512)),
        down_stage=vmem((2,) + bits[:-1] + (4 * rows, BACK_WIDE // 2)),
        down_box=vmem((2,) + bits[:-1] + (4 * rows, BACK_WIDE // 2)),
        send=dma((total, dims + 1)),
        recv=dma((total, dims + 1)),
        credit=pltpu.SemaphoreType.REGULAR((NB, dims + 1)),
        out_sem=dma((total, 4)),
        end_send=dma((total, 4)),
        end_recv=dma((total, 4)),
        load_sem=dma((len(LOADS),)),
        act_send=dma((2, 1 + BACK_PARTS)),
        act_recv=dma((2, 1 + BACK_PARTS)),
        small_send=dma((dims + 1,)),
        small_recv=dma((dims + 1,)),
        edge_sem=dma((3,)),
        edge_send=dma((1,)),
        edge_recv=dma((1,)),
    )
    for k in range(dims + 1):
        scratch[TILE + str(k)] = vmem(bits[k:] + (16, 128), WIDE)
    for name, (shape, dtype) in saved_shapes().items():
        scratch[B + name] = vmem(shape, dtype)
    for u, (kind, block) in enumerate(BACK):
        piece = (4 * rows, BACK_WIDE // 2) if kind == DOWN else (rows, 512)
        lead = bits[:-1] if kind == DOWN else bits
        scratch[HELD + str(u)] = vmem(lead + piece)
        count = dims if kind in (QKV, OUT) else dims - 1
        for k in range(1, count + 1):
            scratch[box_name(u, k)] = vmem(lead[k:] + piece)
        if kind == UP:
            scratch[box_name(u, dims)] = vmem(piece)
    names = BACK_IN + list(outs) + list(scratch)

    def kernel(*refs):
        by_name = dict(zip(names, refs))
        extra = dict(
            qkv_flat=by_name[QKV].reshape(2, D, 3 * D),
            out_flat=by_name[OUT].reshape(2, D, D),
            up_flat=by_name[UP].reshape(2, D, FF // 2),
            down_flat=by_name[DOWN].reshape(2, FF // 2, D),
        )
        backward_kernel(dims, names + list(extra), *refs, *extra.values())

    anywhere = pl.BlockSpec(memory_space=pl.ANY)
    arguments = [left[n] for n in BACK_IN[:-2]] + [out_grad, lengths]
    results = pl.pallas_call(
        kernel,
        out_shape=[jax.ShapeDtypeStruct(s, t) for s, t in outs.values()],
        in_specs=[anywhere] * (len(arguments) - 1) + [pl.BlockSpec(memory_space=pltpu.SMEM)],
        out_specs=[anywhere] * len(outs),
        scratch_shapes=list(scratch.values()),
        compiler_params=pltpu.CompilerParams(collective_id=2, has_side_effects=True, vmem_limit_bytes=62 << 20),
        name="backward",
    )(*arguments)
    return SimpleNamespace(**dict(zip(outs, results)))


def finish_kernel(dims, *refs):
    sums, outs, low, wide, edges = refs[:8], refs[8:15], refs[15:20], refs[20:26], refs[26]
    sem = refs[27]
    core = lax.axis_index(PIPE)
    copies = [pltpu.make_async_copy(sums[i], low[i], sem.at[0, i]) for i in range(5)]
    theirs = pltpu.make_async_copy(sums[5], edges.at[1 - core], sem.at[0, 5])
    mine = [pltpu.make_async_copy(sums[6 + i], edges.at[core], sem.at[0, 6]) for i in range(2)]
    for copy in copies + [theirs]:
        copy.start()
    for i in range(2):

        @pl.when(core == i)
        def _():
            mine[i].start()

    writes = []
    for i in range(4):
        copies[i].wait()
        wide[i][...] = low[i][...].astype(WIDE)
        writes.append(pltpu.make_async_copy(wide[i], outs[i].at[0], sem.at[1, i]))
        writes[-1].start()
    theirs.wait()
    mine[0].wait()
    writes.append(pltpu.make_async_copy(edges, outs[6].at[0, :, 0], sem.at[1, 6]))
    writes[-1].start()
    copies[4].wait()
    small = low[4]
    vec_lanes, vec_group, bias_lanes, bias_group, bias_rows = small_layout(2**dims)
    here = lax.axis_index(DP)

    def pick(values, lanes, at, group):
        result = values[:, 0:lanes]
        for i in range(1, group):
            result = jnp.where(at == i, values[:, i * lanes : (i + 1) * lanes], result)
        return result

    wide[4][:, 0] = pick(small[0:10, :], vec_lanes, lax.rem(here, vec_group), vec_group)
    if bias_group > 1:
        wide[5][...] = pick(small[10:11, :], bias_lanes, lax.rem(lax.div(here, 2), bias_group), bias_group)
    else:
        for i in range(bias_rows):
            wide[5][:, i * 128 : (i + 1) * 128] = small[10 + i : 11 + i, :]
    for i in range(4, 6):
        writes.append(pltpu.make_async_copy(wide[i], outs[i], sem.at[1, i]))
        writes[-1].start()
    for copy in writes:
        copy.wait()


def finish(sums, result, dims):
    count = 2**dims
    rows = D // count
    anywhere = pl.BlockSpec(memory_space=pl.ANY)
    shapes = [(rows, 3 * D), (rows, D), (rows, FF), (4 * rows, D)]
    small = [(10, 1, D // count), (1, FF // count)]
    outs = [(1,) + shape for shape in shapes] + small + [(1, 2, 1, SEQ, D)]
    return pl.pallas_call(
        functools.partial(finish_kernel, dims),
        out_shape=[jax.ShapeDtypeStruct(shape, WIDE) for shape in outs],
        in_specs=[anywhere] * 8,
        out_specs=[anywhere] * 7,
        scratch_shapes=[pltpu.VMEM(shape, LOW) for shape in shapes]
        + [pltpu.VMEM((16, 128), WIDE)]
        + [pltpu.VMEM(shape, WIDE) for shape in shapes + small]
        + [pltpu.VMEM((2, SEQ, D), WIDE), pltpu.SemaphoreType.DMA((2, 7))],
        compiler_params=pltpu.CompilerParams(vmem_limit_bytes=62 << 20),
        name="finish",
    )(sums.g_qkv, sums.g_out, sums.g_up, sums.g_down, sums.g_small, sums.theirs, sums.mine, result)


def regroup(values, outer, inner):
    lead = values.shape[:-1]
    values = values.reshape(lead + (-1, 2, inner))
    values = jnp.moveaxis(values, -2, -3).reshape(lead + (2, -1, outer))
    return jnp.moveaxis(values, -3, -2).reshape(lead + (-1,))


def per_device(dims, hidden_in, lengths, out_grad, w_qkv, w_out, w_up, w_down, vectors, up_bias):
    lanes = FF // 2**dims
    if lanes != 256:
        w_up = regroup(w_up, 256, lanes)
    lengths = lengths[:, 0]
    left = forward((w_qkv, w_out, w_up, w_down), hidden_in, vectors, up_bias, lengths, dims)
    sums = backward(left, out_grad, lengths, dims)
    qkv, out, up, down, grad_vec, grad_bias, edges = finish(sums, left["s_z"], dims)
    if lanes != 256:
        up = regroup(up, lanes, 256)
    return (edges, qkv, out, up, down, jnp.transpose(grad_vec, (1, 0, 2)), grad_bias)


def solution(mesh):
    dims = (mesh.shape[DP] - 1).bit_length()
    weights = P(PIPE, DP, None)
    placed = (
        P(None, DP, None, None),
        P(None, DP),
        P(None, DP, None, None),
        weights,
        weights,
        weights,
        weights,
        P(PIPE, None, DP),
        P(PIPE, DP),
    )
    return jax.shard_map(
        functools.partial(per_device, dims),
        mesh=mesh,
        in_specs=placed,
        out_specs=(
            P(PIPE, None, DP, None, None),
            weights,
            weights,
            weights,
            weights,
            P(PIPE, None, DP),
            P(PIPE, DP),
        ),
        check_vma=False,
    )
```

```python
import functools
from types import SimpleNamespace

import jax
import jax.numpy as jnp
from jax import lax
from jax.experimental import pallas as pl
from jax.experimental.pallas import tpu as pltpu
from jax.sharding import PartitionSpec as P

D = 1024
HEADS = 16
HEAD_DIM = 64
FF = 4096
SEQ = 256
EPS = 1e-05
SCALE = HEAD_DIM**-0.5
MESH = pl.DeviceIdType.MESH
LOW = jnp.bfloat16
WIDE = jnp.float32
QKV, OUT, UP, DOWN = "qkv", "out", "up", "down"
FLAT = "_flat"
PIPE, DP = "pipe", "dp"
PARTS = 4
DOWN_WIDE = D // PARTS
KINDS = [(QKV, 0), (QKV, 1), (QKV, 2), (OUT, 0), (UP, 0), (UP, 1)] + [(DOWN, i) for i in range(PARTS)]
NU = len(KINDS)
GATHER_ORDERS = [
    (0, 1, 2, 3), (0, 1, 2, 3), (0, 1, 3, 2), (0, 1, 3, 2),
    (0, 1, 2), (0, 1, 2), (0, 1, 2), (2, 0, 1),
    (2, 0, 1), (0, 1, 2), (0, 1, 3, 2), (2, 0, 1, 3),
    (0, 1, 2, 3), (0, 1, 3, 2), (0, 1, 2), (2, 0, 1),
    (0, 1, 2), (2, 0, 1), (2, 0, 1), (0, 1, 2),
]
SCHEDULE = [
    2000, 2001, 16, 112, 2002, 32, 240, 80, 241, 17, 128, 176, 0, 33, 2003, 224, 2004, 48, 18, 64,
    288, 1, 2005, 34, 192, 49, 272, 81, 19, 2, 193, 96, 160, 35, 82, 50, 177, 161, 194, 3,
    65, 36, 51, 178, 208, 256, 66, 195, 144, 3000, 20, 47, 4, 3003, 97, 113, 83, 15, 209, 225,
    31, 179, 52, 162, 67, 145, 3002, 129, 3001, 63, 84, 98, 114, 3004, 3005, 3006, 3007, 68, 146, 210,
    130, 95, 180, 242, 226, 3009, 79, 99, 111, 163, 115, 147, 127, 3008, 257, 159, 3010, 3011, 3012, 3013,
    3016, 3017, 131, 196, 3015, 211, 3022, 3023, 3018, 304, 3014, 143, 3019, 243, 3020, 207, 164, 3024, 289, 3021,
    227, 175, 191, 305, 273, 3025, 3026, 3030, 212, 3031, 3033, 258, 3032, 223, 3034, 3035, 3036, 3037, 244, 228,
    290, 255, 306, 3039, 239, 259, 274, 3038, 291, 271, 3040, 3041, 3042, 3043, 3044, 307, 303, 275, 3049, 3050,
    319, 3051, 287, 3052, 3053, 3045, 3046, 3047, 3054, 3048, 3055, 3056,
]
GATHER_FIRST = -10
GATHER_LAGS = [3, 1, -1, -4]
GATHER_READY = 5


def axis_order(dims, u):
    kind, block = KINDS[u]
    if kind in (UP, DOWN):
        return tuple(range(dims - 1))
    return tuple((i + 2 * u) % dims for i in range(dims))


def gather_order(dims, v):
    return GATHER_ORDERS[v] if dims == 4 else axis_order(dims, v % NU)


def place(dims):
    core, here = lax.axis_index(PIPE), lax.axis_index(DP)
    bits = [lax.rem(lax.div(here, 2 ** (dims - 1 - i)), 2) for i in range(dims)]
    partners = [(core, here + (1 - 2 * bits[i]) * 2 ** (dims - 1 - i)) for i in range(dims)]
    return core, bits, partners, (1 - core, here)


def greet(everyone):
    barrier = pltpu.get_barrier_semaphore()
    for device in everyone:
        pl.semaphore_signal(barrier, inc=1, device_id=device, device_id_type=MESH)
    return lambda: pl.semaphore_wait(barrier, len(everyone))


def remote(source, target, send, recv, device):
    return pltpu.make_async_remote_copy(
        src_ref=source, dst_ref=target, send_sem=send, recv_sem=recv, device_id=device, device_id_type=MESH
    )


def span(start, size):
    if isinstance(start, int):
        return pl.ds(start, size)
    return pl.ds(pl.multiple_of(start, size), size)


def for_each(count, body):
    lax.fori_loop(0, count, lambda i, carry: (body(i), carry)[1], 0, unroll=min(count, 8))


def unit_columns(u, column_half):
    kind, block = KINDS[u]
    if kind == DOWN:
        return span(block * DOWN_WIDE + column_half * (DOWN_WIDE // 2), DOWN_WIDE // 2)
    return span(block * 1024 + column_half * 512, 512)


def norm_parts(values):
    center = values - jnp.mean(values, -1, keepdims=True)
    factor = lax.rsqrt(jnp.mean(center * center, -1, keepdims=True) + EPS)
    return (center * factor, factor)


def norm_back(grad_normed, normed, factor):
    return factor * (
        grad_normed
        - jnp.mean(grad_normed, -1, keepdims=True)
        - normed * jnp.mean(grad_normed * normed, -1, keepdims=True)
    )


def dot(left, right, dims=((1,), (0,))):
    return lax.dot_general(left, right, (dims, ((), ())), preferred_element_type=WIDE)


BY_ROWS = ((0,), (0,))
BY_COLUMNS = ((1,), (1,))


def small_layout(count):
    vec_lanes, bias_lanes = D // count, FF // count
    return vec_lanes, 128 // vec_lanes, bias_lanes, max(1, 128 // bias_lanes), max(1, bias_lanes // 128)


def head_masks():
    lanes = lax.broadcasted_iota(jnp.int32, (1, 128), 1)
    first = (lanes < HEAD_DIM).astype(WIDE)
    return first, 1.0 - first


def valid_rows(length, start, count):
    rows = lax.broadcasted_iota(jnp.int32, (count, 1), 0) + start
    return (rows < length).astype(WIDE)


FORWARD_IN = ["w_qkv", "w_out", "w_up", "w_down", "hidden", "vectors", "up_bias", "lengths"]
S = "s_"
SAVED = ["x", "a", "q", "k", "v", "o", "p", "h", "c", "g", "gp"]
LOADS = ["vecs", "og", "y", "w_down", "w_up", "w_qkv", "w_out"] + SAVED
N = SimpleNamespace(**{n: n for n in LOADS})


def saved_shapes():
    wide = lambda *s: (s, WIDE)
    low = lambda *s: (s, LOW)
    return dict(
        x=low(SEQ, D),
        a=low(SEQ, D),
        q=low(SEQ, D),
        k=low(SEQ, D),
        v=low(SEQ, D),
        o=low(SEQ, D),
        p=low(HEADS, SEQ, SEQ),
        h=wide(SEQ, D),
        c=low(2, SEQ, D),
        g=low(2, SEQ, FF // 2),
        gp=low(2, SEQ, FF // 2),
    )


def forward_kernel(dims, names, *refs):
    R = SimpleNamespace(**dict(zip(names, refs)))
    core, bits, partners, sibling = place(dims)
    own = tuple(bits)
    half = bits[-1]
    mate = partners[-1]
    load_x = pltpu.make_async_copy(R.hidden.at[core, 0], R.x0, R.io.at[0])
    load_x.start()
    own_loads = [
        pltpu.make_async_copy(source.at[0], target, R.io.at[1 + i])
        for i, (source, target) in enumerate(
            [(R.w_qkv, R.own_qkv), (R.w_out, R.own_out), (R.w_up, R.own_up), (R.w_down, R.own_down)]
        )
    ]
    for copy in own_loads:
        copy.start()
    met = greet([sibling] + partners)
    total = 2 * NU
    count = 2**dims
    saved = SimpleNamespace(**{n: [getattr(R, n + str(l)) for l in range(2)] for n in SAVED})

    def first_pairs(u, layer, column_half):
        kind, block = KINDS[u]
        cols = unit_columns(u, column_half)
        if kind == UP:
            pairs = []
            for i in range(2):
                block_id = block * 4 + column_half * 2 + i
                to = span(block_id * 256, 256)
                for which, target in ((half, R.up.at[(layer,) + own]), (1 - half, R.stage.at[layer])):
                    pairs.append((R.own_up.at[:, span((2 * block_id + which) * 256, 256)], target.at[:, to]))
            return pairs
        if kind == DOWN:
            return [(R.own_down.at[:, cols], R.down.at[(layer,) + own[:-1] + (slice(None), cols)])]
        return [(getattr(R, "own_" + kind).at[:, cols], getattr(R, kind).at[(layer,) + own + (slice(None), cols)])]

    def first_local(u, layer):
        return [
            pltpu.make_async_copy(s, t, R.local_sem.at[u, i])
            for i, (s, t) in enumerate(first_pairs(u, layer, core))
        ]

    def first_remote(u, layer):
        return [
            remote(s, t, R.first_send.at[u, i], R.first_recv.at[u, i], sibling)
            for i, (s, t) in enumerate(first_pairs(u, layer, 1 - core))
        ]

    def chain(v):
        layer, u = v // NU, v % NU
        kind, block = KINDS[u]
        cols = unit_columns(u, core)
        moves = []
        if kind == UP:
            moves.append((R.stage.at[layer, :, cols], R.up.at[(layer,) + own + (slice(None), cols)], mate))
        order = gather_order(dims, v)
        known = dims - 1 if kind == DOWN else dims
        free = {dims - 1} if kind == UP else set()
        for k in range(len(order) + 1):
            gathered = set(order[:k]) | free
            where = tuple(slice(None) if i in gathered else bits[i] for i in range(known))
            ref = getattr(R, kind).at[(layer,) + where + (slice(None), cols)]
            moves.append((ref, ref, partners[order[k]] if k < len(order) else sibling))
        return [remote(s, t, R.send.at[v, i], R.recv.at[v, i], d) for i, (s, t, d) in enumerate(moves)]

    def small_step(k):
        where = tuple(slice(None) if i < k else bits[i] for i in range(dims))
        ref = R.small_all.at[(core,) + where]
        return remote(ref, ref, R.small_send.at[k], R.small_recv.at[k], partners[k] if k < dims else sibling)

    def pack_small():
        vec_lanes, vec_group, bias_lanes, bias_group, bias_rows = small_layout(count)
        here = lax.axis_index(DP)

        def put(values, at, group):
            if group == 1:
                return values
            return jnp.concatenate([jnp.where(at == i, values, 0.0) for i in range(group)], axis=1)

        tile = R.tile
        tile[...] = jnp.zeros_like(tile)
        tile[0:10, :] = put(R.vectors[0].astype(WIDE), lax.rem(here, vec_group), vec_group)
        bias = put(R.up_bias[...].astype(WIDE), lax.rem(lax.div(here, 2), bias_group), bias_group)
        for i in range(bias_rows):
            tile[10 + i : 11 + i, :] = bias[:, i * 128 : (i + 1) * 128]
        R.small_all[(core,) + own] = tile[...].astype(LOW)

    pack_small()
    for copy in own_loads:
        copy.wait()
    for layer in range(2):

        @pl.when(core == layer)
        def _():
            for u in range(NU):
                for copy in first_local(u, layer):
                    copy.start()

    met()
    for layer in range(2):

        @pl.when(core == layer)
        def _():
            for u in range(NU):
                for copy in first_remote(u, layer):
                    copy.start()

    def arrive(v):
        layer, u = v // NU, v % NU

        @pl.when(core == layer)
        def _():
            for copy in first_local(u, layer):
                copy.wait()
            for copy in first_remote(u, layer):
                copy.wait_send()

        @pl.when(core != layer)
        def _():
            for copy in first_remote(u, layer):
                copy.wait_recv()

    length = R.lengths[core]
    vecs, biases = R.vecs, R.biases
    first_head, second_head = head_masks()

    def assemble():
        vec_lanes, vec_group, bias_lanes, bias_group, bias_rows = small_layout(count)
        small = R.small_all

        def shard(layer, d):
            return small[(layer,) + tuple((d >> (dims - 1 - i)) & 1 for i in range(dims))].astype(WIDE)

        def half_shard(layer, b):
            lead = tuple((b >> (dims - 2 - i)) & 1 for i in range(dims - 1))
            return small[(layer,) + lead + (half,)].astype(WIDE)

        for layer in range(2):
            for t in range(D // 128):
                vecs[layer, :, t * 128 : (t + 1) * 128] = sum(
                    shard(layer, d) for d in range(t * vec_group, (t + 1) * vec_group)
                )
            for t in range(count // 2 // bias_group):
                tile = sum(half_shard(layer, b) for b in range(t * bias_group, (t + 1) * bias_group))
                for i in range(bias_rows):
                    at = (t * bias_rows + i) * 128
                    biases[layer, 0:1, at : at + 128] = tile[10 + i : 11 + i, :]

    save_queue = []

    def save(name, layer):
        copy = pltpu.make_async_copy(
            getattr(saved, name)[layer], getattr(R, S + name).at[layer], R.save_sem.at[layer, SAVED.index(name)]
        )
        copy.start()
        save_queue.append(copy)

    def vec(layer, i, cols=slice(None)):
        return vecs[layer, i : i + 1, cols]

    def load_weight(v):
        layer, u = v // NU, v % NU
        kind, block = KINDS[u]
        if kind == DOWN:
            flat = R.down_flat.at[layer, :, pl.ds(block * DOWN_WIDE, DOWN_WIDE)]
            target = R.w_low.at[:, pl.ds(block * DOWN_WIDE, DOWN_WIDE)]
        else:
            flat = getattr(R, kind + FLAT).at[layer, :, pl.ds(block * 1024, 1024)]
            target = R.w_slots.at[u]
        return pltpu.make_async_copy(flat, target, R.weight_sem.at[u])

    def first_norm(layer):
        def rows(i):
            at = span(i * 32, 32)
            normed, unused = norm_parts(saved.x[layer][at, :].astype(WIDE))
            saved.a[layer][at, :] = (normed * vec(layer, 0) + vec(layer, 1)).astype(LOW)

        for_each(SEQ // 32, rows)
        save(N.x, layer)
        save(N.a, layer)

    def project(layer, block):
        target = (saved.q, saved.k, saved.v)[block][layer]
        weight = R.w_slots.at[block]

        def columns(n):
            at = span(n * 256, 256)
            values = dot(saved.a[layer][...], weight[:, at])
            if block == 0:
                values = (values + vec(layer, 2, at)).astype(LOW) * SCALE
            elif block == 2:
                values = values + vec(layer, 3, at)
            target[:, at] = values.astype(LOW)

        for_each(D // 256, columns)
        save((N.q, N.k, N.v)[block], layer)

    def attention(layer):
        key_ids = lax.broadcasted_iota(jnp.int32, (SEQ, SEQ), 0)
        query_ids = lax.broadcasted_iota(jnp.int32, (SEQ, SEQ), 1)
        blocked = jnp.where((key_ids <= query_ids) & (key_ids < length), 0.0, -1e30)

        def pair(n):
            at = span(n * 128, 128)
            query, key, value = (part[layer][:, at] for part in (saved.q, saved.k, saved.v))
            parts = []
            for i, mask in enumerate((first_head, second_head)):
                scores = dot(key, query * mask.astype(LOW), BY_COLUMNS) + blocked
                weights = jnp.exp(scores - jnp.max(scores, 0, keepdims=True))
                probs = (weights * (1.0 / jnp.sum(weights, 0, keepdims=True))).astype(LOW)
                saved.p[layer][2 * n + i] = probs
                parts.append(dot(probs, value, BY_ROWS) * mask)
            saved.o[layer][:, at] = (parts[0] + parts[1]).astype(LOW)

        for_each(HEADS // 2, pair)
        save(N.p, layer)
        save(N.o, layer)

    def send_c(layer):
        ref = saved.c[layer]
        return remote(ref.at[0], ref.at[1], R.act_send.at[layer, 0], R.act_recv.at[layer, 0], mate)

    def attend_out(layer):
        weight = R.w_slots.at[3]
        hidden = saved.h[layer]

        def columns(n):
            at = span(n * 256, 256)
            values = dot(saved.o[layer][...], weight[:, at])
            hidden[:, at] = saved.x[layer][:, at].astype(WIDE) + values + vec(layer, 4, at)

        for_each(D // 256, columns)

    def second_norm(layer):
        def rows(i):
            at = span(i * 32, 32)
            normed, unused = norm_parts(saved.h[layer][at, :])
            saved.c[layer][0, at, :] = (normed * vec(layer, 5) + vec(layer, 6)).astype(LOW)

        for_each(SEQ // 32, rows)
        save(N.h, layer)

    def feed_up(layer, block, who):
        weight = R.w_slots.at[4 + block]

        def columns(n):
            at = span(n * 256, 256)
            to = span(block * 1024 + n * 256, 256)
            value = dot(saved.c[layer][who], weight[:, at]) + biases[layer, 0:1, to]
            share = 0.5 + 0.5 * lax.erf(value * 0.7071067811865476)
            slope = share + value * (jnp.exp(value * value * -0.5) * 0.3989422804014327)
            saved.g[layer][who, :, to] = (value * share).astype(LOW)
            saved.gp[layer][who, :, to] = slope.astype(LOW)

        for_each(4, columns)
        if block == 1 and who == 1:
            save(N.g, layer)
            save(N.gp, layer)

    def send_part(layer, block):
        at = pl.ds(block * DOWN_WIDE, DOWN_WIDE)
        return remote(
            R.part.at[layer, 0, :, at],
            R.part.at[layer, 1, :, at],
            R.act_send.at[layer, 1 + block],
            R.act_recv.at[layer, 1 + block],
            mate,
        )

    def down_theirs(layer, block):
        at = pl.ds(block * DOWN_WIDE, DOWN_WIDE)
        R.part[layer, 0, :, at] = dot(saved.g[layer][1], R.w_low[:, at]).astype(LOW)

    def down_mine(layer, block):
        at = pl.ds(block * DOWN_WIDE, DOWN_WIDE)
        values = dot(saved.g[layer][0], R.w_low[:, at])
        R.y[:, at] = saved.h[layer][:, at] + values + vec(layer, 7, at)

    def end(layer):
        def rows(i):
            at = span(i * 32, 32)
            valid = valid_rows(length, i * 32, 32)
            values = R.y[at, :] + R.part[layer, 1, at, :].astype(WIDE)
            if layer == 0:
                saved.x[1][at, :] = (values * valid).astype(LOW)
            else:
                R.y[at, :] = values
                normed, unused = norm_parts(values)
                R.z[at, :] = (normed * vec(1, 8) + vec(1, 9)) * valid

        for_each(SEQ // 32, rows)

    def weight(layer, u):
        load_weight(layer * NU + u).wait()

    def wait_parts(layer):
        for block in range(PARTS):
            send_part(layer, block).wait()

    def wait_c(layer):
        send_c(layer).wait()
        save(N.c, layer)

    pieces = [
        (first_norm, None),
        (lambda layer: project(layer, 0), 0),
        (lambda layer: project(layer, 1), 1),
        (lambda layer: project(layer, 2), 2),
        (attention, None),
        (attend_out, 3),
        (second_norm, None),
        (lambda layer: send_c(layer).start(), None),
        (lambda layer: feed_up(layer, 0, 0), 4),
        (lambda layer: feed_up(layer, 1, 0), 5),
        (wait_c, None),
        (lambda layer: feed_up(layer, 0, 1), None),
        (lambda layer: feed_up(layer, 1, 1), None),
    ]
    for block in range(PARTS):
        pieces.append((functools.partial(lambda block, layer: down_theirs(layer, block), block), 6 + block))
        pieces.append((functools.partial(lambda block, layer: send_part(layer, block).start(), block), None))
        pieces.append((functools.partial(lambda block, layer: down_mine(layer, block), block), None))
    pieces += [(wait_parts, None), (end, None)]

    chains = [chain(v) for v in range(total)]

    def plain_schedule():
        moves = []
        for v in range(total):
            for i in range(len(chains[v])):
                left = len(chains[v]) - 1 - i
                lag = GATHER_LAGS[left] if left < len(GATHER_LAGS) else GATHER_LAGS[-1] - left + len(GATHER_LAGS) - 1
                moves.append((v + (lag if i else min(GATHER_FIRST, lag)), -i, v))
            moves.append((v + GATHER_READY, -99, v))
        codes = [16 * v - i if i > -99 else 16 * v + 15 for unused, i, v in sorted(moves)]
        for k in range(dims + 2):
            codes.insert(6 * k, 2000 + k)
        result, done = [], set()
        jobs = [(layer, w) for layer in range(2) for w in range(len(pieces))]
        for code in codes:
            result.append(code)
            done.add(code)
            while jobs and 2000 + dims + 1 in done:
                layer, w = jobs[0]
                u = pieces[w][1]
                if u is not None and 16 * (layer * NU + u) + 15 not in done:
                    break
                result.append(3000 + 30 * layer + w)
                jobs.pop(0)
        return result

    load_x.wait()
    for code in SCHEDULE if dims == 4 and SCHEDULE else plain_schedule():
        if code >= 3000:
            layer, w = (code - 3000) // 30, (code - 3000) % 30
            if pieces[w][1] is not None:
                weight(layer, pieces[w][1])
            pieces[w][0](layer)
        elif code >= 2000:
            k = code - 2000
            if k > 0:
                small_step(k - 1).wait()
            if k <= dims:
                small_step(k).start()
            else:
                assemble()
        elif code % 16 == 15:
            v = code // 16
            chains[v][-1].wait()
            load_weight(v).start(priority=1)
        else:
            v, i = code // 16, code % 16
            if i == 0:
                arrive(v)
            else:
                chains[v][i - 1].wait()
            chains[v][i].start()

    last = [(R.y, R.s_y, 0), (R.z, R.s_z, 1), (R.vecs, R.s_vecs, 2)]
    for source, target, i in last:
        pltpu.make_async_copy(source, target, R.last_sem.at[i]).start()
    for copy in save_queue:
        copy.wait()
    for source, target, i in last:
        pltpu.make_async_copy(source, target, R.last_sem.at[i]).wait()


def forward(shards, hidden, vectors, up_bias, lengths, dims):
    rows = D // 2**dims
    bits = (2,) * dims
    outs = dict(
        qkv=((2,) + bits + (rows, 3 * D), LOW),
        out=((2,) + bits + (rows, D), LOW),
        up=((2,) + bits + (rows, FF // 2), LOW),
        down=((2,) + bits[:-1] + (4 * rows, D), LOW),
        stage=((2, rows, FF // 2), LOW),
    )
    for name, (shape, dtype) in saved_shapes().items():
        outs[S + name] = ((2,) + shape, dtype)
    outs[S + N.y] = ((SEQ, D), WIDE)
    outs[S + "z"] = ((SEQ, D), WIDE)
    outs[S + N.vecs] = ((2, 16, D), WIDE)
    dma = pltpu.SemaphoreType.DMA
    total = 2 * NU
    scratch = dict(
        small_all=pltpu.VMEM((2,) + bits + (16, 128), LOW),
        vecs=pltpu.VMEM((2, 16, D), WIDE),
        biases=pltpu.VMEM((2, 8, FF // 2), WIDE),
        w_slots=pltpu.VMEM((6, D, D), LOW),
        w_low=pltpu.VMEM((FF // 2, D), LOW),
        part=pltpu.VMEM((2, 2, SEQ, D), LOW),
        y=pltpu.VMEM((SEQ, D), WIDE),
        z=pltpu.VMEM((SEQ, D), WIDE),
        local_sem=dma((NU, 4)),
        first_send=dma((NU, 4)),
        first_recv=dma((NU, 4)),
        send=dma((total, dims + 2)),
        recv=dma((total, dims + 2)),
        small_send=dma((dims + 1,)),
        small_recv=dma((dims + 1,)),
        io=dma((5,)),
        tile=pltpu.VMEM((16, 128), WIDE),
        own_qkv=pltpu.VMEM((rows, 3 * D), LOW),
        own_out=pltpu.VMEM((rows, D), LOW),
        own_up=pltpu.VMEM((rows, FF), LOW),
        own_down=pltpu.VMEM((4 * rows, D), LOW),
        save_sem=dma((2, len(SAVED))),
        weight_sem=dma((NU,)),
        act_send=dma((2, 1 + PARTS)),
        act_recv=dma((2, 1 + PARTS)),
        last_sem=dma((3,)),
    )
    for name, (shape, dtype) in saved_shapes().items():
        for layer in range(2):
            scratch[name + str(layer)] = pltpu.VMEM(shape, dtype)
    names = FORWARD_IN + list(outs) + list(scratch)

    def kernel(*refs):
        by_name = dict(zip(names, refs))
        extra = dict(
            qkv_flat=by_name[QKV].reshape(2, D, 3 * D),
            out_flat=by_name[OUT].reshape(2, D, D),
            up_flat=by_name[UP].reshape(2, D, FF // 2),
            down_flat=by_name[DOWN].reshape(2, FF // 2, D),
        )
        forward_kernel(dims, names + list(extra), *refs, *extra.values())

    anywhere = pl.BlockSpec(memory_space=pl.ANY)
    whole = pl.BlockSpec(memory_space=pltpu.VMEM)
    results = pl.pallas_call(
        kernel,
        out_shape=[jax.ShapeDtypeStruct(s, t) for s, t in outs.values()],
        in_specs=[anywhere] * 5 + [whole] * 2 + [pl.BlockSpec(memory_space=pltpu.SMEM)],
        out_specs=[anywhere] * len(outs),
        scratch_shapes=list(scratch.values()),
        compiler_params=pltpu.CompilerParams(collective_id=1, has_side_effects=True, vmem_limit_bytes=60 << 20),
        name="forward",
    )(*shards, hidden, vectors, up_bias, lengths)
    return dict(zip(outs, results))


BACK_PARTS = 2
BACK_WIDE = D // BACK_PARTS
BACK = [(DOWN, i) for i in range(BACK_PARTS)] + [(UP, 0), (UP, 1), (OUT, 0), (QKV, 0), (QKV, 1), (QKV, 2)]
NB = len(BACK)
SCATTER_LAGS = [1, 3, 4, 5, 6]
BACK_ORDERS = [
    (0, 1, 2), (2, 0, 1), (0, 1, 2), (0, 1, 2),
    (0, 1, 2, 3), (0, 1, 2, 3), (0, 1, 3, 2), (0, 1, 2, 3),
]
BACK_SCHEDULE = [
    3000, 3001, 3003, 3002, 3004, 3005, 0, 3006, 3008, 3009, 3010, 3007, 3012, 16, 3011, 32, 1, 3013, 3014, 3015,
    3016, 48, 17, 64, 3017, 3018, 33, 3019, 80, 3020, 3022, 3023, 2, 65, 49, 3030, 3033, 3031, 18, 34,
    3021, 3032, 81, 66, 112, 3, 19, 96, 3034, 50, 3035, 35, 82, 67, 3036, 3037, 144, 128, 51, 3038,
    113, 3039, 3040, 68, 97, 52, 36, 83, 3041, 3042, 145, 3043, 176, 160, 3044, 114, 3045, 3046, 98, 84,
    192, 3047, 115, 129, 3048, 3049, 99, 177, 208, 100, 193, 116, 3050, 130, 3051, 161, 224, 178, 240, 3052,
    3053, 194, 4000, 2000, 209, 162, 225, 195, 241, 2001, 210, 163, 226, 146, 2002, 211, 196, 131, 242, 227,
    179, 180, 212, 147, 243, 164, 2003, 2004, 228, 244,
]
HELD, B, TILE = "held", "b_", "tile"
BACK_WEIGHTS = [QKV, OUT, UP, DOWN]
BACK_IN = BACK_WEIGHTS + [S + n for n in SAVED + ["y", "z", "vecs"]] + ["out_grad", "lengths"]


def back_order(dims, u):
    return BACK_ORDERS[u] if dims == 4 else axis_order(dims, KINDS.index(BACK[u]))


def box_name(u, k):
    return "box%d_%d" % (u, k)


def backward_kernel(dims, names, *refs):
    R = SimpleNamespace(**dict(zip(names, refs)))
    core, bits, partners, sibling = place(dims)
    own = tuple(bits)
    half = bits[-1]
    mate = partners[-1]
    met = greet([sibling] + partners)
    total = 2 * NB
    count = 2**dims
    length = R.lengths[core]
    vecs, grads = R.vecs, R.grads
    first_head, second_head = head_masks()

    def load(name, layer):
        if name == N.y:
            source = R.s_y
        elif name == N.og:
            source = R.out_grad.at[core, 0]
        elif name == N.vecs:
            source = R.s_vecs
        elif name in (N.w_down, N.w_up, N.w_qkv, N.w_out):
            source = getattr(R, name[2:] + FLAT).at[layer]
        else:
            source = getattr(R, S + name).at[layer]
        if name == N.vecs:
            target = vecs
        elif name == N.w_up:
            target = R.b_w_wide.at[:, pl.ds(0, FF // 2)]
        elif name == N.w_qkv:
            target = R.b_w_wide
        else:
            target = getattr(R, B + name)
        return pltpu.make_async_copy(source, target, R.load_sem.at[LOADS.index(name)])

    def need(layer, *which):
        for name in which:
            load(name, layer).wait()

    def again(layer, *which):
        if layer == 1:
            for name in which:
                load(name, 0).start()

    def unit_of(v):
        return 1 - v // NB, BACK[v % NB]

    def columns_of(v, column_half):
        kind, block = BACK[v % NB]
        if kind == DOWN:
            return span(block * BACK_WIDE + column_half * (BACK_WIDE // 2), BACK_WIDE // 2)
        return span(block * 1024 + column_half * 512, 512)

    def order_of(v):
        return tuple(reversed(back_order(dims, v % NB)))

    def held(v):
        return getattr(R, HELD + str(v % NB))

    def box(v, k):
        if k == 0:
            kind, block = BACK[v % NB]
            return (R.down_box if kind == DOWN else R.wide_box).at[v % 2]
        return getattr(R, box_name(v % NB, k))

    def stage(v):
        kind, block = BACK[v % NB]
        return (R.down_stage if kind == DOWN else R.wide_stage).at[v % 2]

    def is_up(v):
        return BACK[v % NB][0] == UP

    def steps(v):
        return len(order_of(v)) + (1 if is_up(v) else 0)

    def where(v, k, away):
        order = order_of(v)
        place_of = []
        for i in range(dims - 1 if BACK[v % NB][0] == DOWN else dims):
            if i in order[: max(k - 1, 0)]:
                place_of.append(bits[i])
            elif 0 < k <= len(order) and i == order[k - 1]:
                place_of.append(1 - bits[i] if away else bits[i])
            elif k > len(order) and i == dims - 1:
                place_of.append(1 - half if away else half)
            elif k > len(order):
                place_of.append(bits[i])
            else:
                place_of.append(slice(None))
        return tuple(place_of)

    def device_of(v, k):
        if k == 0:
            return sibling
        return partners[order_of(v)[k - 1]] if k <= len(order_of(v)) else mate

    def move(v, k):
        source = stage(v) if k == 0 else held(v).at[where(v, k, True)]
        return remote(source, box(v, k), R.send.at[v, k], R.recv.at[v, k], device_of(v, k))

    def earlier(v, k):
        if k > 0:
            return v - NB if v >= NB else None
        low = BACK[v % NB][0] == DOWN
        same = [w for w in range(v) if (BACK[w % NB][0] == DOWN) == low and w % 2 == v % 2]
        return same[-1] if same else None

    def later(v, k):
        return any(earlier(w, k) == v for w in range(v + 1, total))

    def begin(v, k):
        if earlier(v, k) is not None:
            pl.semaphore_wait(R.credit.at[v % NB, k], 1)
        move(v, k).start()

    def consumed(v, k):
        for w in range(v + 1, total):
            if earlier(w, k) == v:
                pl.semaphore_signal(
                    R.credit.at[w % NB, k], inc=1, device_id=device_of(v, k), device_id_type=MESH
                )

    def finals(v):
        kind, block = BACK[v % NB]
        cols = columns_of(v, core)
        if kind == UP:
            pairs = []
            for i in range(2):
                block_id = block * 4 + core * 2 + i
                part = (slice(None), pl.ds(i * 256, 256))
                for which, source in ((half, held(v).at[own + part]), (1 - half, box(v, dims).at[part])):
                    pairs.append((source, R.g_up.at[:, span((2 * block_id + which) * 256, 256)]))
            return pairs
        if kind == DOWN:
            return [(held(v).at[own[:-1]], R.g_down.at[:, cols])]
        return [(held(v).at[own], getattr(R, "g_" + kind).at[:, cols])]

    def final_local(v):
        return [
            pltpu.make_async_copy(s, t, R.out_sem.at[v, i]) for i, (s, t) in enumerate(finals(v))
        ]

    def final_remote(v):
        return [
            remote(s, t, R.end_send.at[v, i], R.end_recv.at[v, i], sibling)
            for i, (s, t) in enumerate(finals(v))
        ]

    def finish(v):
        @pl.when(core == unit_of(v)[0])
        def _():
            for copy in final_local(v):
                copy.start()

        @pl.when(core != unit_of(v)[0])
        def _():
            for copy in final_remote(v):
                copy.start()

    def finished(v):
        @pl.when(core == unit_of(v)[0])
        def _():
            for copy in final_local(v):
                copy.wait()

        @pl.when(core != unit_of(v)[0])
        def _():
            for copy in final_remote(v):
                copy.wait_send()
        if is_up(v):
            consumed(v, dims)

    def event(v, k):
        move(v, k).wait()
        if not (is_up(v) and k == steps(v)):
            view = held(v).at[where(v, k, False)]
            view[...] = view[...] + box(v, k)[...]
            consumed(v, k)
        if k < steps(v):
            begin(v, k + 1)
        else:
            finish(v)

    def vec(layer, i):
        return vecs[layer, i : i + 1, :]

    def collect(layer, i, values):
        grads[layer, i : i + 1, :] = grads[layer, i : i + 1, :] + jnp.sum(values, 0, keepdims=True)

    def send_e(layer, block):
        ref = R.e.at[layer]
        at = pl.ds(block * BACK_WIDE, BACK_WIDE)
        send, recv = R.act_send.at[layer, 1 + block], R.act_recv.at[layer, 1 + block]
        return remote(ref.at[0, :, at], ref.at[1, :, at], send, recv, mate)

    def send_dc(layer):
        ref = R.dc_part
        return remote(ref.at[0], ref.at[1], R.act_send.at[layer, 0], R.act_recv.at[layer, 0], mate)

    def top(layer):
        if layer == 1:
            need(1, N.vecs, N.og, N.y)

        def rows(i):
            at = span(i * 32, 32)
            valid = valid_rows(length, i * 32, 32)
            if layer == 1:
                grad_z = R.b_og[at, :].astype(WIDE) * valid
                normed, factor = norm_parts(R.b_y[at, :])
                collect(1, 8, grad_z * normed)
                collect(1, 9, grad_z)
                grad_y = norm_back(grad_z * vec(1, 8), normed, factor)
            else:
                grad_y = R.dx[at, :].astype(WIDE) * valid
            R.dy[at, :] = grad_y
            branch = grad_y.astype(LOW)
            R.e[layer, 0, at, :] = branch
            collect(layer, 7, branch.astype(WIDE))

        for_each(SEQ // 32, rows)

    def produce(v, body, quarter_shape):
        for target, column_half in ((stage(v), 1 - core), (held(v), core)):
            cols = columns_of(v, column_half)

            def quarter(i):
                target[lax.div(i, 2), lax.rem(i, 2)] = body(i, cols).astype(LOW).reshape(quarter_shape)

            for_each(4, quarter)
            if column_half is not core:
                begin(v, 0)

    def pair_rows(ref, cols):
        values = ref[:, :, cols]
        return values.reshape(2 * SEQ, values.shape[-1])

    inner = (2,) * (dims - 2) + (D // count, 512)
    down_inner = (2,) * (dims - 3) + (FF // count, BACK_WIDE // 2)

    def grad_down(layer, v, block):
        if block == 0:
            need(layer, N.g)
        produce(
            v,
            lambda i, cols: dot(pair_rows(R.b_g, span(i * 512, 512)), pair_rows(R.e.at[layer], cols), BY_ROWS),
            down_inner,
        )
        if block == BACK_PARTS - 1:
            again(layer, N.g)

    def feed_hidden(layer, who):
        if who == 0:
            need(layer, N.w_down, N.gp)

        def hidden(n):
            at = span(n * 256, 256)
            grad_act = dot(R.e[layer, who], R.b_w_down[at, :], BY_COLUMNS)
            grad_upper = (grad_act * R.b_gp[who, :, at].astype(WIDE)).astype(LOW)
            R.b_gp[who, :, at] = grad_upper
            sums = jnp.sum(grad_upper.astype(WIDE), 0, keepdims=True)
            R.bias_grads[layer, 0:1, at] = sums if who == 0 else R.bias_grads[layer, 0:1, at] + sums

        for_each(FF // 2 // 256, hidden)
        if who == 1:
            again(layer, N.w_down)

    def feed_theirs(layer):
        need(layer, N.w_up)

        def theirs(n):
            at = span(n * 256, 256)
            R.dc_part[0, :, at] = dot(R.b_gp[1], R.b_w_wide[at, pl.ds(0, FF // 2)], BY_COLUMNS).astype(LOW)

        for_each(D // 256, theirs)

    def feed_mine(layer):
        def mine(n):
            at = span(n * 256, 256)
            R.dc[:, at] = dot(R.b_gp[0], R.b_w_wide[at, pl.ds(0, FF // 2)], BY_COLUMNS)

        for_each(D // 256, mine)
        load(N.w_qkv, layer).start()

    def grad_up(layer, v, block):
        if block == 0:
            need(layer, N.c)

        def body(i, cols):
            return dot(pair_rows(R.b_c, span(i * 256, 256)), pair_rows(R.b_gp, cols), BY_ROWS)

        produce(v, body, inner)
        if block == 1:
            again(layer, N.c, N.gp)

    def middle(layer):
        need(layer, N.h)

        def rows(i):
            at = span(i * 32, 32)
            grad_in = R.dc[at, :] + R.dc_part[1, at, :].astype(WIDE)
            normed, factor = norm_parts(R.b_h[at, :])
            collect(layer, 5, grad_in * normed)
            collect(layer, 6, grad_in)
            grad_hidden = R.dy[at, :] + norm_back(grad_in * vec(layer, 5), normed, factor)
            R.dy[at, :] = grad_hidden
            branch = grad_hidden.astype(LOW)
            R.f[at, :] = branch
            collect(layer, 4, branch.astype(WIDE))

        for_each(SEQ // 32, rows)
        again(layer, N.h)

    def grad_out(layer, v):
        need(layer, N.o)
        produce(v, lambda i, cols: dot(R.b_o[:, span(i * 256, 256)], R.f[:, cols], BY_ROWS), inner)
        again(layer, N.o)

    def grad_mixed(layer):
        need(layer, N.w_out)

        def columns(n):
            at = span(n * 256, 256)
            R.do[:, at] = dot(R.f[...], R.b_w_out[at, :], BY_COLUMNS).astype(LOW)

        for_each(D // 256, columns)
        again(layer, N.w_out)

    def attention_back(layer):
        need(layer, N.q, N.k, N.v, N.p)

        def pair(n):
            at = span(n * 128, 128)
            query, key, value, grad_o = R.b_q[:, at], R.b_k[:, at], R.b_v[:, at], R.do[:, at]
            sums = [0.0, 0.0, 0.0]
            for i, mask in enumerate((first_head.astype(LOW), second_head.astype(LOW))):
                probs = R.b_p[2 * n + i]
                grad_head = grad_o * mask
                wide = probs.astype(WIDE)
                grad_probs = dot(value, grad_head, BY_COLUMNS)
                shift = jnp.sum(grad_probs * wide, 0, keepdims=True)
                grad_scores = (wide * (grad_probs - shift)).astype(LOW)
                sums[0] += dot(grad_scores, key * mask, BY_ROWS)
                sums[1] += dot(grad_scores, query * mask)
                sums[2] += dot(probs, grad_head)
            sums[0] = sums[0] * SCALE
            for j in range(3):
                low = sums[j].astype(LOW)
                R.dp[:, pl.ds(pl.multiple_of(n * 128 + j * D, 128), 128)] = low
                if j != 1:
                    row = 2 if j == 0 else 3
                    grads[layer, row : row + 1, at] = jnp.sum(low.astype(WIDE), 0, keepdims=True)

        for_each(HEADS // 2, pair)
        again(layer, N.q, N.k, N.v, N.p)

    def grad_qkv(layer, v, block):
        if block == 0:
            need(layer, N.a)
        produce(v, lambda i, cols: dot(R.b_a[:, span(i * 256, 256)], R.dp[:, cols], BY_ROWS), inner)
        if block == 2:
            again(layer, N.a)

    def grad_attn_in(layer):
        need(layer, N.w_qkv)

        def columns(n):
            at = span(n * 256, 256)
            R.dc[:, at] = dot(R.dp[...], R.b_w_wide[at, :], BY_COLUMNS)

        for_each(D // 256, columns)
        again(layer, N.w_up)

    def bottom(layer):
        need(layer, N.x)

        def rows(i):
            at = span(i * 32, 32)
            grad_in = R.dc[at, :]
            normed, factor = norm_parts(R.b_x[at, :].astype(WIDE))
            collect(layer, 0, grad_in * normed)
            collect(layer, 1, grad_in)
            grad_x = R.dy[at, :] + norm_back(grad_in * vec(layer, 0), normed, factor)
            if layer == 1:
                R.dx[at, :] = grad_x.astype(LOW)
            else:
                R.b_y[at, :] = grad_x

        for_each(SEQ // 32, rows)
        again(layer, N.x)

    def spread():
        vec_lanes, vec_group, bias_lanes, bias_group, bias_rows = small_layout(count)
        tiles = R.tiles
        tiles[...] = jnp.zeros_like(tiles)
        for layer in range(2):
            for d in range(count):
                lead = tuple((d >> (dims - 1 - i)) & 1 for i in range(dims))
                t = d // vec_group
                tiles[(layer,) + lead + (slice(0, 10),)] = grads[layer, 0:10, t * 128 : (t + 1) * 128]
            for b in range(count // 2):
                lead = tuple((b >> (dims - 2 - i)) & 1 for i in range(dims - 1))
                for i in range(bias_rows):
                    at = (b // bias_group * bias_rows + i) * 128
                    tiles[(layer,) + lead + (half, slice(10 + i, 11 + i))] = R.bias_grads[layer, 0:1, at : at + 128]

    def tile_box(k):
        return getattr(R, TILE + str(k))

    def small_move(k):
        if k == 0:
            return remote(
                R.tiles.at[1 - core], tile_box(0), R.small_send.at[0], R.small_recv.at[0], sibling
            )
        lead = own[: k - 1] + (1 - bits[k - 1],)
        return remote(
            R.tiles.at[(core,) + lead],
            tile_box(k),
            R.small_send.at[k],
            R.small_recv.at[k],
            partners[k - 1],
        )

    def small_event(k):
        small_move(k).wait()
        lead = own[:k]
        view = R.tiles.at[(core,) + lead]
        view[...] = view[...] + tile_box(k)[...]
        if k < dims:
            small_move(k + 1).start()
        else:
            pltpu.make_async_copy(view, R.g_small, R.edge_sem.at[2]).start()

    for name in (N.vecs, N.og, N.y, N.g, N.w_down, N.gp, N.w_up, N.c, N.h, N.o, N.w_out, N.q, N.k, N.v, N.p, N.x, N.a):
        load(name, 1).start(priority=1 if name in (N.vecs, N.og, N.y) else 0)
    grads[...] = jnp.zeros_like(grads)
    top(1)
    met()
    edge_local = pltpu.make_async_copy(R.b_y, R.mine, R.edge_sem.at[0])
    edge_remote = [remote(ref, R.theirs, R.edge_send.at[0], R.edge_recv.at[0], sibling) for ref in (R.s_z, R.b_y)]

    @pl.when(core == 0)
    def _():
        edge_remote[0].start()

    def last(layer):
        edge_local.start()

        @pl.when(core == 1)
        def _():
            edge_remote[1].start()

        spread()
        small_move(0).start()

    def unit(layer, u):
        return (1 - layer) * NB + u

    def start_e(block, layer):
        send_e(layer, block).start()

    def wait_e(block, layer):
        send_e(layer, block).wait()

    def down(block, layer):
        grad_down(layer, unit(layer, block), block)

    pieces = [(top, None)]
    pieces += [(functools.partial(start_e, i), None) for i in range(BACK_PARTS)]
    pieces.append((lambda layer: feed_hidden(layer, 0), None))
    for i in range(BACK_PARTS):
        pieces += [(functools.partial(wait_e, i), None), (functools.partial(down, i), i)]
    pieces += [
        (lambda layer: feed_hidden(layer, 1), None),
        (feed_theirs, None),
        (lambda layer: send_dc(layer).start(), None),
        (feed_mine, None),
        (lambda layer: grad_up(layer, unit(layer, BACK_PARTS), 0), BACK_PARTS),
        (lambda layer: grad_up(layer, unit(layer, BACK_PARTS + 1), 1), BACK_PARTS + 1),
        (lambda layer: send_dc(layer).wait(), None),
        (middle, None),
        (lambda layer: grad_out(layer, unit(layer, BACK_PARTS + 2)), BACK_PARTS + 2),
        (grad_mixed, None),
        (attention_back, None),
        (lambda layer: grad_qkv(layer, unit(layer, BACK_PARTS + 3), 0), BACK_PARTS + 3),
        (lambda layer: grad_qkv(layer, unit(layer, BACK_PARTS + 4), 1), BACK_PARTS + 4),
        (lambda layer: grad_qkv(layer, unit(layer, BACK_PARTS + 5), 2), BACK_PARTS + 5),
        (grad_attn_in, None),
        (bottom, None),
    ]

    def plain_schedule():
        timed = []
        for v in range(total):
            for k in range(steps(v) + 1):
                lag = SCATTER_LAGS[k] if k < len(SCATTER_LAGS) else SCATTER_LAGS[-1] + (k - len(SCATTER_LAGS) + 1) / 8
                timed.append((v + lag, 0, -k, v))
            timed.append((v, 1, 0, v))
        result = []
        for turn in range(2):
            at = -1.0
            for w, (unused, u) in enumerate(pieces):
                at = max(at + 0.01, turn * NB + (u or 0))
                timed.append((at, 1, w, (turn, w)))
        codes = []
        for key, is_compute, k, v in sorted(timed, key=lambda item: item[:3]):
            if not is_compute:
                codes.append(16 * v - k)
            elif isinstance(v, tuple):
                codes.append(3000 + 30 * v[0] + v[1])
        codes.append(4000)
        return codes + [2000 + k for k in range(dims + 1)]

    for code in BACK_SCHEDULE if dims == 4 and BACK_SCHEDULE else plain_schedule():
        if code == 3000:
            continue
        if code >= 4000:
            last(0)
        elif code >= 3000:
            turn, w = (code - 3000) // 30, (code - 3000) % 30
            u = pieces[w][1]
            if turn == 1 and u is not None:
                finished(u)
            pieces[w][0](1 - turn)
        elif code >= 2000:
            small_event(code - 2000)
        else:
            event(code // 16, code % 16)
    for v in range(NB, total):
        finished(v)

    @pl.when(core == 0)
    def _():
        edge_remote[0].wait_send()

    @pl.when(core == 1)
    def _():
        edge_remote[1].wait_send()

    edge_local.wait()
    edge_remote[0].wait_recv()
    pltpu.make_async_copy(R.tiles.at[(core,) + own], R.g_small, R.edge_sem.at[2]).wait()
    for layer in range(2):

        @pl.when(core == layer)
        def _():
            for v in range((1 - layer) * NB, (2 - layer) * NB):
                for copy in final_remote(v):
                    copy.wait_recv()


def backward(left, out_grad, lengths, dims):
    rows = D // 2**dims
    bits = (2,) * dims
    outs = dict(
        g_qkv=((rows, 3 * D), LOW),
        g_out=((rows, D), LOW),
        g_up=((rows, FF), LOW),
        g_down=((4 * rows, D), LOW),
        g_small=((16, 128), WIDE),
        mine=((SEQ, D), WIDE),
        theirs=((SEQ, D), WIDE),
    )
    dma = pltpu.SemaphoreType.DMA
    total = 2 * NB
    vmem = lambda shape, dtype=LOW: pltpu.VMEM(shape, dtype)
    scratch = dict(
        vecs=vmem((2, 16, D), WIDE),
        grads=vmem((2, 16, D), WIDE),
        bias_grads=vmem((2, 8, FF // 2), WIDE),
        b_og=vmem((SEQ, D)),
        b_y=vmem((SEQ, D), WIDE),
        b_w_down=vmem((FF // 2, D)),
        b_w_wide=vmem((D, 3 * D)),
        b_w_out=vmem((D, D)),
        e=vmem((2, 2, SEQ, D)),
        dc_part=vmem((2, SEQ, D)),
        dc=vmem((SEQ, D), WIDE),
        dy=vmem((SEQ, D), WIDE),
        dx=vmem((SEQ, D)),
        f=vmem((SEQ, D)),
        do=vmem((SEQ, D)),
        dp=vmem((SEQ, 3 * D)),
        tiles=vmem((2,) + bits + (16, 128), WIDE),
        wide_stage=vmem((2,) + bits + (rows, 512)),
        wide_box=vmem((2,) + bits + (rows, 512)),
        down_stage=vmem((2,) + bits[:-1] + (4 * rows, BACK_WIDE // 2)),
        down_box=vmem((2,) + bits[:-1] + (4 * rows, BACK_WIDE // 2)),
        send=dma((total, dims + 1)),
        recv=dma((total, dims + 1)),
        credit=pltpu.SemaphoreType.REGULAR((NB, dims + 1)),
        out_sem=dma((total, 4)),
        end_send=dma((total, 4)),
        end_recv=dma((total, 4)),
        load_sem=dma((len(LOADS),)),
        act_send=dma((2, 1 + BACK_PARTS)),
        act_recv=dma((2, 1 + BACK_PARTS)),
        small_send=dma((dims + 1,)),
        small_recv=dma((dims + 1,)),
        edge_sem=dma((3,)),
        edge_send=dma((1,)),
        edge_recv=dma((1,)),
    )
    for k in range(dims + 1):
        scratch[TILE + str(k)] = vmem(bits[k:] + (16, 128), WIDE)
    for name, (shape, dtype) in saved_shapes().items():
        scratch[B + name] = vmem(shape, dtype)
    for u, (kind, block) in enumerate(BACK):
        piece = (4 * rows, BACK_WIDE // 2) if kind == DOWN else (rows, 512)
        lead = bits[:-1] if kind == DOWN else bits
        scratch[HELD + str(u)] = vmem(lead + piece)
        count = dims if kind in (QKV, OUT) else dims - 1
        for k in range(1, count + 1):
            scratch[box_name(u, k)] = vmem(lead[k:] + piece)
        if kind == UP:
            scratch[box_name(u, dims)] = vmem(piece)
    names = BACK_IN + list(outs) + list(scratch)

    def kernel(*refs):
        by_name = dict(zip(names, refs))
        extra = dict(
            qkv_flat=by_name[QKV].reshape(2, D, 3 * D),
            out_flat=by_name[OUT].reshape(2, D, D),
            up_flat=by_name[UP].reshape(2, D, FF // 2),
            down_flat=by_name[DOWN].reshape(2, FF // 2, D),
        )
        backward_kernel(dims, names + list(extra), *refs, *extra.values())

    anywhere = pl.BlockSpec(memory_space=pl.ANY)
    arguments = [left[n] for n in BACK_IN[:-2]] + [out_grad, lengths]
    results = pl.pallas_call(
        kernel,
        out_shape=[jax.ShapeDtypeStruct(s, t) for s, t in outs.values()],
        in_specs=[anywhere] * (len(arguments) - 1) + [pl.BlockSpec(memory_space=pltpu.SMEM)],
        out_specs=[anywhere] * len(outs),
        scratch_shapes=list(scratch.values()),
        compiler_params=pltpu.CompilerParams(collective_id=2, has_side_effects=True, vmem_limit_bytes=62 << 20),
        name="backward",
    )(*arguments)
    return SimpleNamespace(**dict(zip(outs, results)))


def finish_kernel(dims, *refs):
    sums, outs, low, wide, edges = refs[:8], refs[8:15], refs[15:20], refs[20:26], refs[26]
    sem = refs[27]
    core = lax.axis_index(PIPE)
    copies = [pltpu.make_async_copy(sums[i], low[i], sem.at[0, i]) for i in range(5)]
    theirs = pltpu.make_async_copy(sums[5], edges.at[1 - core], sem.at[0, 5])
    mine = [pltpu.make_async_copy(sums[6 + i], edges.at[core], sem.at[0, 6]) for i in range(2)]
    for copy in copies + [theirs]:
        copy.start()
    for i in range(2):

        @pl.when(core == i)
        def _():
            mine[i].start()

    writes = []
    for i in range(4):
        copies[i].wait()
        wide[i][...] = low[i][...].astype(WIDE)
        writes.append(pltpu.make_async_copy(wide[i], outs[i].at[0], sem.at[1, i]))
        writes[-1].start()
    theirs.wait()
    mine[0].wait()
    writes.append(pltpu.make_async_copy(edges, outs[6].at[0, :, 0], sem.at[1, 6]))
    writes[-1].start()
    copies[4].wait()
    small = low[4]
    vec_lanes, vec_group, bias_lanes, bias_group, bias_rows = small_layout(2**dims)
    here = lax.axis_index(DP)

    def pick(values, lanes, at, group):
        result = values[:, 0:lanes]
        for i in range(1, group):
            result = jnp.where(at == i, values[:, i * lanes : (i + 1) * lanes], result)
        return result

    wide[4][:, 0] = pick(small[0:10, :], vec_lanes, lax.rem(here, vec_group), vec_group)
    if bias_group > 1:
        wide[5][...] = pick(small[10:11, :], bias_lanes, lax.rem(lax.div(here, 2), bias_group), bias_group)
    else:
        for i in range(bias_rows):
            wide[5][:, i * 128 : (i + 1) * 128] = small[10 + i : 11 + i, :]
    for i in range(4, 6):
        writes.append(pltpu.make_async_copy(wide[i], outs[i], sem.at[1, i]))
        writes[-1].start()
    for copy in writes:
        copy.wait()


def finish(sums, result, dims):
    count = 2**dims
    rows = D // count
    anywhere = pl.BlockSpec(memory_space=pl.ANY)
    shapes = [(rows, 3 * D), (rows, D), (rows, FF), (4 * rows, D)]
    small = [(10, 1, D // count), (1, FF // count)]
    outs = [(1,) + shape for shape in shapes] + small + [(1, 2, 1, SEQ, D)]
    return pl.pallas_call(
        functools.partial(finish_kernel, dims),
        out_shape=[jax.ShapeDtypeStruct(shape, WIDE) for shape in outs],
        in_specs=[anywhere] * 8,
        out_specs=[anywhere] * 7,
        scratch_shapes=[pltpu.VMEM(shape, LOW) for shape in shapes]
        + [pltpu.VMEM((16, 128), WIDE)]
        + [pltpu.VMEM(shape, WIDE) for shape in shapes + small]
        + [pltpu.VMEM((2, SEQ, D), WIDE), pltpu.SemaphoreType.DMA((2, 7))],
        compiler_params=pltpu.CompilerParams(vmem_limit_bytes=62 << 20),
        name="finish",
    )(sums.g_qkv, sums.g_out, sums.g_up, sums.g_down, sums.g_small, sums.theirs, sums.mine, result)


def regroup(values, outer, inner):
    lead = values.shape[:-1]
    values = values.reshape(lead + (-1, 2, inner))
    values = jnp.moveaxis(values, -2, -3).reshape(lead + (2, -1, outer))
    return jnp.moveaxis(values, -3, -2).reshape(lead + (-1,))


def per_device(dims, hidden_in, lengths, out_grad, w_qkv, w_out, w_up, w_down, vectors, up_bias):
    lanes = FF // 2**dims
    if lanes != 256:
        w_up = regroup(w_up, 256, lanes)
    lengths = lengths[:, 0]
    left = forward((w_qkv, w_out, w_up, w_down), hidden_in, vectors, up_bias, lengths, dims)
    sums = backward(left, out_grad, lengths, dims)
    qkv, out, up, down, grad_vec, grad_bias, edges = finish(sums, left["s_z"], dims)
    if lanes != 256:
        up = regroup(up, lanes, 256)
    return (edges, qkv, out, up, down, jnp.transpose(grad_vec, (1, 0, 2)), grad_bias)


def solution(mesh):
    dims = (mesh.shape[DP] - 1).bit_length()
    weights = P(PIPE, DP, None)
    placed = (
        P(None, DP, None, None),
        P(None, DP),
        P(None, DP, None, None),
        weights,
        weights,
        weights,
        weights,
        P(PIPE, None, DP),
        P(PIPE, DP),
    )
    return jax.shard_map(
        functools.partial(per_device, dims),
        mesh=mesh,
        in_specs=placed,
        out_specs=(
            P(PIPE, None, DP, None, None),
            weights,
            weights,
            weights,
            weights,
            P(PIPE, None, DP),
            P(PIPE, DP),
        ),
        check_vma=False,
    )
```
